128 devices in a mesh: lat: 8 (over z_lo, x), lon: 16 (over y, z_hi, core).
Axes of the slice: x: 4, y: 4, z: 4 (z_hi: 2, z_lo: 2; z = z_hi * 2 + z_lo), core: 2. Of those that a mesh axis runs over, the one named last changes fastest.
Arguments:
- background: float32 [2, 25, 512, 2048], P(None, None, 'lat', 'lon'), may hold values from -6 to 6
- error_scale: float32 [2, 25, 512, 2048], P(None, None, 'lat', 'lon'), may hold values from 0.5 to 2
- east_rate: float32 [512, 2048], P('lat', 'lon'), may hold values from 0.05 to 0.24
- north_rate: float32 [512, 2048], P('lat', 'lon'), may hold values from 0.05 to 0.24
- sea_mask: int32 [512, 2048], P('lat', 'lon'), may hold values 0 or 1
- partner: int32 [2048], replicated, may hold values from 0 to 2047, as said below
- obs_weight: float32 [128, 128, 50, 128], P(('lat', 'lon')), may hold values from -0.875 to 0.875
- obs_value: float32 [128, 128, 128], P(('lat', 'lon')), may hold values from -8 to 8
- obs_error: float32 [128, 128, 128], P(('lat', 'lon')), may hold values from 0.5 to 2
- obs_column: int32 [128, 128, 128], P(('lat', 'lon')), may hold values from 0 to 8191
- obs_count: int32 [128, 128], P(('lat', 'lon')), may hold values from 0 to 128, as said below
Outputs:
- increment: float32 [2, 25, 512, 2048], P(None, None, 'lat', 'lon')
- cost_share: float32 [], replicated
The draws below stay inside these ranges and needn't reach their ends.
Inputs may be any that keep to these rules, and one draw needn't show every extreme that they name: `obs_count`: every source device fills all 128 slots to at least one owner, and one owner gets all 128 slots from every source. partner[g] = (s - g) modulo 2048 for one s, so partner[partner[g]] = g.
All inputs are finite; a program needn't handle non-finite values. No bound on the sum of `sea_mask` on one device may be relied on, other than what follows from the above.
Results may differ from the reference program's by a relative error of at most 0.0003.
Values sent between devices are 32-bit elements; how exact they have to be, the bound alone decides.
No kernel may reach another device: no remote copies, remote signals or barrier semaphores. Data moves between devices by JAX's collectives and lax.ppermute only.
A program may use at most 128 MiB of HBM per device.

```python
import math
import jax
import jax.numpy as jnp

CY = 64
CX = 128
LEV = 25
STEPS = 4
CAP = 128
BLOCKS = 128
NLAT = 512
NLON = 2048
N_LON = 16


def draw_partner(key, part):
    shift_value = jax.random.randint(jax.random.fold_in(key, 3), (), 0, NLON)
    return ((shift_value - jnp.arange(NLON)) % NLON).astype(jnp.int32)


def draw_obs_count(key, part):
    keys = jax.random.split(jax.random.fold_in(key, 7), 4)
    level_of = jax.random.randint(keys[0], (BLOCKS,), 1, 5)
    base_count = jax.random.randint(keys[1], (BLOCKS, BLOCKS), 0, CAP + 1)
    counts = jnp.minimum(CAP, base_count * level_of[None, :] // 2)
    hot_owner = jax.random.randint(keys[2], (BLOCKS,), 0, BLOCKS)
    owner_index = jnp.arange(BLOCKS)
    counts = jnp.where(owner_index[None, :] == hot_owner[:, None], CAP, counts)
    full_owner = jax.random.randint(keys[3], (), 0, BLOCKS)
    counts = jnp.where(owner_index[None, :] == full_owner, CAP, counts)
    return counts.astype(jnp.int32)


def plant(array, key, low, high):
    index_at = [jax.random.randint(jax.random.fold_in(key, axis), (), 0, length) for axis, length in enumerate(array.shape)]
    main_axis = array.shape.index(max(array.shape))
    neighbour = index_at[:main_axis] + [(index_at[main_axis] + 1) % array.shape[main_axis]] + index_at[main_axis + 1:]
    return array.at[tuple(index_at)].set(low).at[tuple(neighbour)].set(high)


def block_scale(rng, shape, shards, smallest, high):
    def one(dim, parts):
        steps = jax.random.uniform(jax.random.fold_in(jax.random.fold_in(rng, 6), dim), (parts,), jnp.float32, smallest / len(shards), high / len(shards))
        return jnp.repeat(jnp.exp(steps), shape[dim] // parts).reshape((-1,) + (1,) * (len(shape) - dim - 1))

    factor_of = one(*shards[0])
    for cut in shards[1:]:
        factor_of = factor_of * one(*cut)
    return factor_of


def noise(own_key, dims, width, reach, pieces=(), kind=jnp.bfloat16):
    result = jax.random.normal(own_key, dims, jnp.float32) * width
    if len(pieces) > 0:
        result = block_scale(own_key, dims, pieces, -0.22, 0.18) * result
    return jnp.clip(result, min=-reach, max=reach).astype(kind)


def setup_inputs(seed: int = 0) -> dict:
    key_of = jax.random.split(jax.random.key(seed), 12)
    background = noise(key_of[0], (2, LEV, NLAT, NLON), 1.0, 6.0, ((2, 8), (3, 16)), jnp.float32)
    error_scale = jnp.clip(jnp.exp(math.log(2.0) - 1.3862944 * jax.random.uniform(key_of[1], (2, LEV, NLAT, NLON), jnp.float32) ** block_scale(key_of[1], (2, LEV, NLAT, NLON), ((2, 8), (3, 16)), -0.2, 0.2)), 0.5, 2.0)
    east_rate = jnp.clip(jnp.exp(math.log(0.24) - 1.5686159 * jax.random.uniform(key_of[2], (NLAT, NLON), jnp.float32) ** block_scale(key_of[2], (NLAT, NLON), ((0, 8), (1, 16)), -0.2, 0.2)), 0.05, 0.24)
    north_rate = jnp.clip(jnp.exp(math.log(0.24) - 1.5686159 * jax.random.uniform(key_of[3], (NLAT, NLON), jnp.float32) ** block_scale(key_of[3], (NLAT, NLON), ((0, 8), (1, 16)), -0.2, 0.2)), 0.05, 0.24)
    sea_mask = plant((jax.random.randint(key_of[4], (NLAT, NLON), 0, 4) < 3).astype(jnp.int32), jax.random.fold_in(key_of[4], 1), 0, 1)
    partner = draw_partner(jax.random.fold_in(key_of[11], 71), 0)
    obs_weight = noise(key_of[6], (BLOCKS, BLOCKS, 2 * LEV, CAP), (2 * LEV) ** -0.5, 0.875, ((0, 128),), jnp.float32)
    obs_value = noise(key_of[7], (BLOCKS, BLOCKS, CAP), 2.0, 8.0, ((0, 128),), jnp.float32)
    obs_error = jnp.clip(jnp.exp(math.log(2.0) - 1.3862944 * jax.random.uniform(key_of[8], (BLOCKS, BLOCKS, CAP), jnp.float32) ** block_scale(key_of[8], (BLOCKS, BLOCKS, CAP), ((0, 128),), -0.2, 0.2)), 0.5, 2.0)
    obs_column = plant(jax.random.randint(key_of[9], (BLOCKS, BLOCKS, CAP), 0, CY * CX), jax.random.fold_in(key_of[9], 1), 0, (CY * CX) - 1).astype(jnp.int32)
    obs_count = draw_obs_count(jax.random.fold_in(key_of[11], 71), 0)
    return {"background": background, "error_scale": error_scale, "east_rate": east_rate, "north_rate": north_rate, "sea_mask": sea_mask, "partner": partner, "obs_weight": obs_weight, "obs_value": obs_value, "obs_error": obs_error, "obs_column": obs_column, "obs_count": obs_count}


huber_edge = 1.5


def relax(ext_field, ext_coef):
    center = ext_field[:, 1:-1, 1:-1]
    sea_here = ext_coef[2, 1:-1, 1:-1]
    east_here = ext_coef[0, 1:-1, 1:-1]
    north_here = ext_coef[1, 1:-1, 1:-1]
    along_term = ext_coef[2, 1:-1, 2:] * (ext_field[:, 1:-1, 2:] - center) + ext_coef[2, 1:-1, :-2] * (ext_field[:, 1:-1, :-2] - center)
    across = ext_coef[2, 2:, 1:-1] * (ext_field[:, 2:, 1:-1] - center) + ext_coef[2, :-2, 1:-1] * (ext_field[:, :-2, 1:-1] - center)
    return center + sea_here * (east_here * along_term + north_here * across)


def extend_global(array_in, partner):
    lon_total = array_in.shape[2]
    wrapped = jnp.concatenate([array_in[:, :, -1:], array_in, array_in[:, :, :1]], axis=2)
    columns = ((jnp.arange(lon_total + 2, dtype=jnp.int32) - 1) % lon_total).astype(jnp.int32)
    north_rows = array_in[:, -1:, :][:, :, partner[columns]]
    south_rows = jnp.zeros_like(north_rows)
    return jnp.concatenate([south_rows, wrapped, north_rows], axis=1)


def reference(background, error_scale, east_rate, north_rate, sea_mask, partner, obs_weight, obs_value, obs_error, obs_column, obs_count):
    levels = 2 * LEV
    flat_bg = background.reshape(levels, NLAT * NLON)
    owner_index = jnp.arange(BLOCKS, dtype=jnp.int32)
    owner_row = (owner_index // N_LON)[None, :, None] * CY + obs_column // CX
    owner_col = (owner_index % N_LON)[None, :, None] * CX + obs_column % CX
    flat_index = (owner_row * NLON + owner_col).astype(jnp.int32)
    weights = jnp.moveaxis(obs_weight, 2, 0)
    sampled = flat_bg[:, flat_index]
    equiv = jnp.sum(weights * sampled, axis=0)
    slot_index = jnp.arange(CAP, dtype=jnp.int32)
    valid_slot = slot_index[None, None, :] < obs_count[:, :, None]
    inverse = jnp.where(valid_slot, 1.0 / obs_error, 0.0)
    scaled = (obs_value - equiv) * inverse
    magnitude = jnp.abs(scaled)
    huber_terms = jnp.where(magnitude <= huber_edge, 0.5 * scaled * scaled, huber_edge * magnitude - 0.5 * huber_edge * huber_edge)
    response = huber_edge / jnp.maximum(magnitude, huber_edge) * scaled * inverse
    cost_share = jnp.sum(huber_terms) / (BLOCKS * BLOCKS * CAP)
    forcing = jnp.zeros((levels, NLAT * NLON), jnp.float32).at[:, flat_index.reshape(-1)].add((weights * response[None]).reshape(levels, -1))
    sea_float = sea_mask.astype(jnp.float32)
    spread = error_scale.reshape(levels, NLAT, NLON)
    state = sea_float[None] * spread * forcing.reshape(levels, NLAT, NLON)
    coefficients = jnp.stack([east_rate, north_rate, sea_float])
    coef_ext = extend_global(coefficients, partner)
    for sweep_index in range(STEPS):
        state = relax(extend_global(state, partner), coef_ext)
    increment = (spread * state).reshape(2, LEV, NLAT, NLON)
    return increment, cost_share
```

```python
import jax
import jax.numpy as jnp
from jax import lax
from jax.experimental import pallas as pl
from jax.experimental.pallas import tpu as pltpu
from jax.sharding import PartitionSpec as P

STEPS = 4
HALO = 4
HUBER_EDGE = 1.5
F32 = jnp.float32
BF16 = jnp.bfloat16
VMEM_LIMIT = 56 * 1024 * 1024


def split_background(bg_ref, out_ref):
    levels = bg_ref.shape[0]
    for h in range(4):
        for p in range(2):
            base = (2 * h + p) * levels * 8
            row = 32 * p + 8 * h

            def body(i, _):
                a = bg_ref[2 * i, row : row + 8, :]
                b = bg_ref[2 * i + 1, row : row + 8, :]
                x = jnp.concatenate([a, b], axis=0)
                hi = x.astype(BF16)
                lo = (x - hi.astype(F32)).astype(BF16)
                at = pl.ds(pl.multiple_of(base + i * 16, 16), 16)
                out_ref[at, 0:128] = hi
                out_ref[at, 128:256] = lo
                return 0

            lax.fori_loop(0, levels // 2, body, 0, unroll=5)


def observe(rec_ref, bgm_ref, sea_ref, es_ref, state_ref, cost_ref, tiles, force, whi, wlo, amat):
    step = pl.program_id(0)
    steps = pl.num_programs(0)
    levels = es_ref.shape[0]
    rows_in = 8 * levels

    @pl.when(step == 0)
    def _():
        force[...] = jnp.zeros_like(force)
        cost_ref[...] = jnp.zeros_like(cost_ref)

    lane = lax.broadcasted_iota(jnp.int32, (levels + 3, 128), 1)

    for half in range(2):
        xs = [rec_ref[half * 8 + i] for i in range(8)]
        for d in (1, 2, 4):
            keep = (lane // (16 * d)) % 2 == 0
            new = list(xs)
            for i in range(8):
                if i & d == 0:
                    lo, hi = xs[i], xs[i + d]
                    new[i] = jnp.where(keep, lo, pltpu.roll(hi, 16 * d, axis=1))
                    new[i + d] = jnp.where(keep, pltpu.roll(lo, 128 - 16 * d, axis=1), hi)
            xs = new
        for i in range(8):
            tiles[i, 0 : levels + 3, half * 128 : half * 128 + 128] = xs[i]

    iota8 = lax.broadcasted_iota(jnp.int32, (8, 256), 0)

    def tile(q, _):
        value = tiles[q, levels : levels + 1, :]
        inverse = tiles[q, levels + 1 : levels + 2, :]
        cell = tiles[q, levels + 2 : levels + 3, :].astype(jnp.int32)
        row = cell >> 7
        col = cell & 127
        part = row >> 5
        block = (row >> 3) & 3
        group = 2 * block + part
        valid = inverse > 0.0
        gmin = jnp.min(jnp.where(valid, group, 8))
        gmax = jnp.max(jnp.where(valid, group, -1))
        rmask = iota8 == (row & 7)
        iota128 = lax.broadcasted_iota(jnp.int32, (128, 256), 0)
        pick = jnp.where(iota128 == col, 1.0, 0.0).astype(BF16)
        pick2 = jnp.concatenate([pick, pick], axis=0)

        def sample(g, acc):
            s = jnp.dot(
                bgm_ref[pl.ds(pl.multiple_of(g * rows_in, 16), rows_in), :],
                pick2,
                preferred_element_type=F32,
            )
            parts = [jnp.zeros((8, 256), F32) for _ in range(4)]
            for k in range(levels):
                parts[k % 4] = parts[k % 4] + tiles[q, k : k + 1, :] * s[8 * k : 8 * k + 8, :]
            total = (parts[0] + parts[1]) + (parts[2] + parts[3])
            return acc + jnp.where(group == g, total, 0.0)

        acc = lax.fori_loop(gmin, gmax + 1, sample, jnp.zeros((8, 256), F32))
        equiv = jnp.sum(jnp.where(rmask, acc, 0.0), axis=0, keepdims=True)
        scaled = (value - equiv) * inverse
        magnitude = jnp.abs(scaled)
        cost_ref[...] += jnp.where(
            magnitude <= HUBER_EDGE,
            0.5 * scaled * scaled,
            HUBER_EDGE * magnitude - 0.5 * HUBER_EDGE * HUBER_EDGE,
        )
        response = HUBER_EDGE / jnp.maximum(magnitude, HUBER_EDGE) * scaled * inverse
        wr = tiles[q, 0:levels, :] * response
        hi = wr.astype(BF16).astype(F32)
        whi[0:levels, :] = hi
        wlo[0:levels, :] = wr - hi
        iota256 = lax.broadcasted_iota(jnp.int32, (256, 256), 0)
        place = jnp.where(iota256 == col + 128 * part, 1.0, 0.0).astype(BF16)
        place2 = jnp.concatenate([place, place], axis=1)

        def spread(b, _):
            m = jnp.where(rmask & (block == b), 1.0, 0.0)
            for k in range(0, levels, 2):
                for half, src in ((0, whi), (256, wlo)):
                    x = jnp.concatenate([m * src[k : k + 1, :], m * src[k + 1 : k + 2, :]], axis=0)
                    amat[8 * k : 8 * k + 16, half : half + 256] = x.astype(BF16)
            at = pl.ds(pl.multiple_of(b * rows_in, 8), rows_in)
            force[at, :] += lax.dot_general(
                amat[...], place2, (((1,), (1,)), ((), ())), preferred_element_type=F32
            )
            return 0

        lax.fori_loop(gmin >> 1, (gmax >> 1) + 1, spread, 0)
        return 0

    lax.fori_loop(0, 8, tile, 0)

    @pl.when(step == steps - 1)
    def _():
        for b in range(4):
            for part in range(2):
                r0 = 32 * part + 8 * b
                sea = sea_ref[r0 : r0 + 8, :].astype(F32)

                def body(k, _):
                    f = force[pl.ds(pl.multiple_of(b * rows_in + 8 * k, 8), 8), 128 * part : 128 * part + 128]
                    state_ref[k, r0 : r0 + 8, :] = sea * es_ref[k, r0 : r0 + 8, :] * f
                    return 0

                lax.fori_loop(0, levels, body, 0, unroll=5)


def edges(x_ref, east_ref, west_ref):
    ny = x_ref.shape[1]
    nx = x_ref.shape[2]

    def body(k, _):
        x = x_ref[k]
        t = jnp.transpose(x)
        pad = jnp.zeros((8, nx - ny), F32)
        last = jnp.concatenate([t[nx - 8 : nx, :], pad], axis=1)
        sub = lax.broadcasted_iota(jnp.int32, (8, nx), 0)
        top = pltpu.roll(x[ny - 8 : ny, :], 4, axis=0)
        east_ref[k] = jnp.where(sub < 4, top, last)
        west_ref[k] = jnp.concatenate([t[0:8, :], pad], axis=1)
        return 0

    lax.fori_loop(0, x_ref.shape[0], body, 0)


def assemble(info_ref, x_ref, fw_ref, fe_ref, side_ref, one_ref, two_ref):
    levels, ny, nx = x_ref.shape
    shift = info_ref[0]
    even = info_ref[1]
    fold = info_ref[2]
    lane = lax.broadcasted_iota(jnp.int32, (8, 128), 1)
    rel_a = shift + 3 - lane
    rel_b = jnp.where(lane < 64, shift + 3 - 128 - lane, shift + 3 + 128 - lane)

    def mirror(west, own, east, rel):
        idx = rel & 127
        w = jnp.take_along_axis(west, idx, axis=1)
        o = jnp.take_along_axis(own, idx, axis=1)
        e = jnp.take_along_axis(east, idx, axis=1)
        return jnp.where(rel < 0, w, jnp.where(rel < 128, o, e))

    def body(k, _):
        fw = fw_ref[k]
        fe = fe_ref[k]
        wt = jnp.concatenate([fw, jnp.zeros((nx - 8, nx), F32)], axis=0)
        et = jnp.concatenate([fe, jnp.zeros((nx - 8, nx), F32)], axis=0)
        full = jnp.concatenate([fe, jnp.zeros((nx - 16, nx), F32), fw], axis=0)
        side = jnp.transpose(full)[0:ny, :]
        side_ref[k] = side
        top_a = pltpu.roll(x_ref[k, ny - 8 : ny, :], 4, axis=0)[0:4, :]
        top_b = pltpu.roll(side[ny - 8 : ny, :], 4, axis=0)[0:4, :]
        bot_a = x_ref[k, 0:8, :][0:4, :]
        bot_b = side[0:8, :][0:4, :]
        own8 = x_ref[k, ny - 8 : ny, :]
        east8 = side[ny - 8 : ny, :]
        west8 = pltpu.roll(fw, 4, axis=0)
        fold_a = mirror(west8, own8, east8, rel_a)
        fold_b = mirror(west8, own8, east8, rel_b)

        @pl.when(even == 1)
        def _():
            one_ref[k, :, 0:nx] = top_a
            one_ref[k, :, nx : 2 * nx] = top_b
            two_ref[k, :, 0:nx] = bot_a
            two_ref[k, :, nx : 2 * nx] = bot_b

        @pl.when(even == 0)
        def _():
            one_ref[k, :, 0:nx] = bot_a
            one_ref[k, :, nx : 2 * nx] = bot_b

            @pl.when(fold == 0)
            def _():
                two_ref[k, :, 0:nx] = top_a
                two_ref[k, :, nx : 2 * nx] = top_b

            @pl.when(fold == 1)
            def _():
                for d in range(4):
                    two_ref[k, d : d + 1, 0:nx] = fold_a[7 - d : 8 - d, :]
                    two_ref[k, d : d + 1, nx : 2 * nx] = fold_b[7 - d : 8 - d, :]

        return 0

    lax.fori_loop(0, levels, body, 0)


def diffuse(info_ref, x_ref, side_ref, one_ref, two_ref, cx_ref, cside_ref, cone_ref, ctwo_ref, es_ref, out_ref, coef):
    ny, nx = x_ref.shape[1], x_ref.shape[2]
    even = info_ref[1]

    def halo_rows(one, two):
        return jnp.where(
            even == 1,
            jnp.concatenate([one, two], axis=0),
            jnp.concatenate([two, one], axis=0),
        )

    def whole(k, x, side, one, two):
        left = jnp.concatenate([x[k], side[k]], axis=1)
        return jnp.concatenate([left, halo_rows(one[k], two[k])], axis=0)

    rows = ny + 8
    cols = 2 * nx

    @pl.when(pl.program_id(0) == 0)
    def _():
        col = lax.broadcasted_iota(jnp.int32, (rows, cols), 1)
        live = (col < nx + 4) | (col >= cols - 4)
        east = whole(0, cx_ref, cside_ref, cone_ref, ctwo_ref)
        north = whole(1, cx_ref, cside_ref, cone_ref, ctwo_ref)
        sea = whole(2, cx_ref, cside_ref, cone_ref, ctwo_ref)
        sea = jnp.where(live, sea, 0.0)
        east = jnp.where(live, east, 0.0) * sea
        north = jnp.where(live, north, 0.0) * sea
        a_e = east * pltpu.roll(sea, cols - 1, axis=1)
        a_w = east * pltpu.roll(sea, 1, axis=1)
        a_n = north * pltpu.roll(sea, rows - 1, axis=0)
        a_s = north * pltpu.roll(sea, 1, axis=0)
        coef[0] = 1.0 - ((a_e + a_w) + (a_n + a_s))
        coef[1] = a_e
        coef[2] = a_w
        coef[3] = a_n
        coef[4] = a_s

    def body(k, _):
        s = whole(k, x_ref, side_ref, one_ref, two_ref)
        for _ in range(STEPS):
            s = (
                coef[0] * s
                + (coef[1] * pltpu.roll(s, cols - 1, axis=1) + coef[2] * pltpu.roll(s, 1, axis=1))
                + (coef[3] * pltpu.roll(s, rows - 1, axis=0) + coef[4] * pltpu.roll(s, 1, axis=0))
            )
        out_ref[k] = es_ref[k] * s[0:ny, 0:nx]
        return 0

    lax.fori_loop(0, x_ref.shape[0], body, 0)


def vmem():
    return pl.BlockSpec(memory_space=pltpu.VMEM)


def smem():
    return pl.BlockSpec(memory_space=pltpu.SMEM)


def params():
    return pltpu.CompilerParams(vmem_limit_bytes=VMEM_LIMIT)


def perm_of(n_lat, n_lon, rule):
    pairs = []
    for a in range(n_lat):
        for b in range(n_lon):
            to = rule(a, b)
            if to is not None:
                pairs.append((a * n_lon + b, to[0] * n_lon + to[1] % n_lon))
    return pairs


def exchange(x, info, turn):
    levels, ny, nx = x.shape
    n_lat = lax.axis_size("lat")
    n_lon = lax.axis_size("lon")
    msg = jax.ShapeDtypeStruct((levels, 8, nx), F32)
    to_east, to_west = pl.pallas_call(
        edges,
        out_shape=(msg, msg),
        in_specs=[vmem()],
        out_specs=(vmem(), vmem()),
        compiler_params=params(),
        cost_estimate=pl.CostEstimate(flops=levels * 1000, bytes_accessed=levels * 40000, transcendentals=0),
        name="edges",
    )(x)
    from_west = lax.ppermute(to_east, "lon", [(i, (i + 1) % n_lon) for i in range(n_lon)])
    from_east = lax.ppermute(to_west, "lon", [((i + 1) % n_lon, i) for i in range(n_lon)])
    rows = jax.ShapeDtypeStruct((levels, 4, 2 * nx), F32)
    side, one, two = pl.pallas_call(
        assemble,
        out_shape=(jax.ShapeDtypeStruct(x.shape, F32), rows, rows),
        in_specs=[smem(), vmem(), vmem(), vmem()],
        out_specs=(vmem(), vmem(), vmem()),
        compiler_params=params(),
        cost_estimate=pl.CostEstimate(flops=levels * 1000, bytes_accessed=levels * 80000, transcendentals=0),
        name="assemble",
    )(info, x, from_west, from_east)
    got_one = lax.ppermute(one, ("lat", "lon"), perm_of(n_lat, n_lon, lambda a, b: (a ^ 1, b)))

    def branch(q):
        def rule(a, b):
            if a == n_lat - 1:
                return (a, q - b)
            if a == 0:
                return None
            return (((a + 1) ^ 1) - 1, b)

        return lambda v: lax.ppermute(v, ("lat", "lon"), perm_of(n_lat, n_lon, rule))

    got_two = lax.switch(turn, [branch(q) for q in range(n_lon)], two)
    return side, got_one, got_two


def shards(
    background,
    error_scale,
    east_rate,
    north_rate,
    sea_mask,
    partner,
    obs_weight,
    obs_value,
    obs_error,
    obs_column,
    obs_count,
):
    levels = background.shape[0] * background.shape[1]
    ny = background.shape[2]
    nx = background.shape[3]
    capacity = obs_weight.shape[3]
    owners = obs_weight.shape[1]
    n_lat = lax.axis_size("lat")
    n_lon = lax.axis_size("lon")
    lat_at = lax.axis_index("lat").astype(jnp.int32)

    slot_index = lax.broadcasted_iota(jnp.int32, (owners, capacity), 1)
    valid_slot = slot_index < obs_count[0][:, None]
    inverse = jnp.where(valid_slot, 1.0 / obs_error[0], 0.0)
    packed = jnp.concatenate(
        [
            obs_weight[0],
            obs_value[0][:, None, :],
            inverse[:, None, :],
            obs_column[0].astype(F32)[:, None, :],
        ],
        axis=1,
    )
    received = lax.all_to_all(packed, ("lat", "lon"), split_axis=0, concat_axis=0, tiled=True)

    moved = (partner[0] - 3) % (nx * n_lon)
    turn = moved // nx
    info = jnp.stack([moved % nx, 1 - lat_at % 2, (lat_at == n_lat - 1).astype(jnp.int32), turn]).astype(jnp.int32)
    coefs = jnp.stack([east_rate, north_rate, sea_mask.astype(F32)])
    cside, cone, ctwo = exchange(coefs, info, turn)

    bg = background.reshape(levels, ny, nx)
    es = error_scale.reshape(levels, ny, nx)
    bgm = pl.pallas_call(
        split_background,
        out_shape=jax.ShapeDtypeStruct((8 * levels * 8, 256), BF16),
        in_specs=[vmem()],
        out_specs=vmem(),
        compiler_params=params(),
        cost_estimate=pl.CostEstimate(flops=3000000, bytes_accessed=3300000, transcendentals=0),
        name="split_background",
    )(bg)

    per = 16
    state, cost = pl.pallas_call(
        observe,
        grid=(owners // per,),
        out_shape=(
            jax.ShapeDtypeStruct((levels, ny, nx), F32),
            jax.ShapeDtypeStruct((1, 256), F32),
        ),
        in_specs=[
            pl.BlockSpec((per, levels + 3, capacity), lambda i: (i, 0, 0)),
            pl.BlockSpec((64 * levels, 256), lambda i: (0, 0)),
            pl.BlockSpec((ny, nx), lambda i: (0, 0)),
            pl.BlockSpec((levels, ny, nx), lambda i: (0, 0, 0)),
        ],
        out_specs=(
            pl.BlockSpec((levels, ny, nx), lambda i: (0, 0, 0)),
            pl.BlockSpec((1, 256), lambda i: (0, 0)),
        ),
        scratch_shapes=[
            pltpu.VMEM((8, 56, 256), F32),
            pltpu.VMEM((32 * levels, 256), F32),
            pltpu.VMEM((56, 256), F32),
            pltpu.VMEM((56, 256), F32),
            pltpu.VMEM((8 * levels, 512), BF16),
        ],
        compiler_params=params(),
        name="observe",
    )(received, bgm, sea_mask, es)

    share = jnp.sum(cost)
    shares = lax.all_to_all(
        jnp.broadcast_to(share, (owners, 1, 128)), ("lat", "lon"), split_axis=0, concat_axis=0, tiled=True
    )
    cost_share = jnp.sum(shares[:, 0, 0]) / (owners * owners * capacity)

    side, one, two = exchange(state, info, turn)

    blk = 5
    lev = lambda i: (i, 0, 0)
    fix = lambda i: (0, 0, 0)
    increment = pl.pallas_call(
        diffuse,
        grid=(levels // blk,),
        out_shape=jax.ShapeDtypeStruct((levels, ny, nx), F32),
        in_specs=[
            smem(),
            pl.BlockSpec((blk, ny, nx), lev),
            pl.BlockSpec((blk, ny, nx), lev),
            pl.BlockSpec((blk, 4, 2 * nx), lev),
            pl.BlockSpec((blk, 4, 2 * nx), lev),
            pl.BlockSpec((3, ny, nx), fix),
            pl.BlockSpec((3, ny, nx), fix),
            pl.BlockSpec((3, 4, 2 * nx), fix),
            pl.BlockSpec((3, 4, 2 * nx), fix),
            pl.BlockSpec((blk, ny, nx), lev),
        ],
        out_specs=pl.BlockSpec((blk, ny, nx), lev),
        scratch_shapes=[pltpu.VMEM((5, ny + 8, 2 * nx), F32)],
        compiler_params=params(),
        name="diffuse",
    )(info, state, side, one, two, coefs, cside, cone, ctwo, es)
    return (increment.reshape(background.shape), cost_share)


def solution(mesh):
    in_specs = (
        P(None, None, "lat", "lon"),
        P(None, None, "lat", "lon"),
        P("lat", "lon"),
        P("lat", "lon"),
        P("lat", "lon"),
        P(),
        P(("lat", "lon"), None, None, None),
        P(("lat", "lon"), None, None),
        P(("lat", "lon"), None, None),
        P(("lat", "lon"), None, None),
        P(("lat", "lon"), None),
    )
    out_specs = (P(None, None, "lat", "lon"), P())
    return jax.shard_map(shards, mesh=mesh, in_specs=in_specs, out_specs=out_specs, check_vma=False)
```

```python
import jax
import jax.numpy as jnp
from jax import lax
from jax.experimental import pallas as pl
from jax.experimental.pallas import tpu as pltpu
from jax.sharding import PartitionSpec as P

STEPS = 4
HALO = 4
HUBER_EDGE = 1.5
F32 = jnp.float32
BF16 = jnp.bfloat16
WIDE = 2048
VMEM_LIMIT = 56 * 1024 * 1024


def split_background(bg_ref, out_ref):
    levels = bg_ref.shape[0]
    for h in range(4):
        for p in range(2):
            base = (2 * h + p) * levels * 8
            row = 32 * p + 8 * h

            def body(i, _):
                a = bg_ref[2 * i, row : row + 8, :]
                b = bg_ref[2 * i + 1, row : row + 8, :]
                x = jnp.concatenate([a, b], axis=0)
                hi = x.astype(BF16)
                lo = (x - hi.astype(F32)).astype(BF16)
                at = pl.ds(pl.multiple_of(base + i * 16, 16), 16)
                out_ref[at, 0:128] = hi
                out_ref[at, 128:256] = lo
                return 0

            lax.fori_loop(0, levels // 2, body, 0, unroll=5)


def pack(count_ref, w_ref, value_ref, error_ref, cell_ref, out_ref, order_ref):
    levels, some, n = w_ref.shape
    owners = order_ref.shape[0]
    lane8 = lax.broadcasted_iota(jnp.int32, (8, n), 1)

    @pl.when(pl.program_id(0) == 0)
    def _():
        counts = jnp.transpose(jnp.broadcast_to(count_ref[...], (owners, n)))
        lane = lax.broadcasted_iota(jnp.int32, (owners, n), 1)
        cell = cell_ref[...]
        row = cell >> 7
        key = (((row >> 3) & 3) << 11) | ((row >> 5) << 10) | ((row & 7) << 7) | (cell & 127)
        key = jnp.where(lane < counts, key, 8192)
        x = (key * n + lane).astype(F32)
        size = 2
        while size <= n:
            step = size // 2
            while step >= 1:
                first = (lane & step) == 0
                other = jnp.where(first, pltpu.roll(x, n - step, axis=1), pltpu.roll(x, step, axis=1))
                least = first == ((lane & size) == 0)
                x = jnp.where(least, jnp.minimum(x, other), jnp.maximum(x, other))
                step //= 2
            size *= 2
        order_ref[...] = x.astype(jnp.int32)

    for o in range(0, some, 8):
        at = pl.ds(pl.multiple_of(pl.program_id(0) * some + o, 8), 8)
        packed = order_ref[at, :]
        order = packed & (n - 1)
        valid = packed < 8192 * n

        def put(k, v):
            out_ref[pl.ds(o * 56 + k, 8, stride=56), :] = v

        for k in range(levels):
            put(k, jnp.take_along_axis(w_ref[k, o : o + 8, :], order, axis=1))
        put(levels, jnp.take_along_axis(value_ref[at, :], order, axis=1))
        error = jnp.take_along_axis(error_ref[at, :], order, axis=1)
        put(levels + 1, jnp.where(valid, 1.0 / error, 0.0))
        put(levels + 2, jnp.take_along_axis(cell_ref[at, :], order, axis=1).astype(F32))
        for k in range(levels + 3, 56):
            put(k, jnp.zeros((8, n), F32))


def pack_call(count, weight, value, error, column):
    levels, owners, n = weight.shape
    some = 16
    return pl.pallas_call(
        pack,
        grid=(owners // some,),
        out_shape=jax.ShapeDtypeStruct((owners * 56, n), F32),
        in_specs=[
            pl.BlockSpec((1, owners), lambda i: (0, 0)),
            pl.BlockSpec((levels, some, n), lambda i: (0, i, 0)),
            pl.BlockSpec((owners, n), lambda i: (0, 0)),
            pl.BlockSpec((owners, n), lambda i: (0, 0)),
            pl.BlockSpec((owners, n), lambda i: (0, 0)),
        ],
        out_specs=pl.BlockSpec((some * 56, n), lambda i: (i, 0)),
        scratch_shapes=[pltpu.VMEM((owners, n), jnp.int32)],
        compiler_params=params(),
        name="pack",
    )(count, weight, value, error, column)


def observe(rec_ref, bgm_ref, sea_ref, es_ref, state_ref, cost_ref, tiles, force, whi, wlo, amat):
    levels = es_ref.shape[0]
    sources = rec_ref.shape[0] // 56
    rows_in = 8 * levels
    wide = whi.shape[1]
    total = tiles.shape[2]

    force[...] = jnp.zeros_like(force)
    cost_ref[...] = jnp.zeros_like(cost_ref)

    def regroup(eight, _):
        lane = lax.broadcasted_iota(jnp.int32, (8, 128), 1)
        for r in range(0, 56, 8):
            xs = [rec_ref[pl.ds(pl.multiple_of((eight * 8 + i) * 56 + r, 8), 8), :] for i in range(8)]
            for d in (1, 2, 4):
                keep = (lane // (16 * d)) % 2 == 0
                new = list(xs)
                for i in range(8):
                    if i & d == 0:
                        lo, hi = xs[i], xs[i + d]
                        new[i] = jnp.where(keep, lo, pltpu.roll(hi, 16 * d, axis=1))
                        new[i + d] = jnp.where(keep, pltpu.roll(lo, 128 - 16 * d, axis=1), hi)
                xs = new
            for i in range(8):
                tiles[i, r : r + 8, pl.ds(pl.multiple_of(eight * 128, 128), 128)] = xs[i]
        return 0

    lax.fori_loop(0, sources // 8, regroup, 0)

    iota8 = lax.broadcasted_iota(jnp.int32, (8, wide), 0)

    def tile(t, _):
        q = t // (total // wide)
        at_r = pl.ds(pl.multiple_of((t % (total // wide)) * wide, wide), wide)
        value = tiles[q, levels : levels + 1, at_r]
        inverse = tiles[q, levels + 1 : levels + 2, at_r]
        cell = tiles[q, levels + 2 : levels + 3, at_r].astype(jnp.int32)
        row = cell >> 7
        col = cell & 127
        part = row >> 5
        block = (row >> 3) & 3
        group = 2 * block + part
        valid = inverse > 0.0
        gmin = jnp.min(jnp.where(valid, group, 8))
        gmax = jnp.max(jnp.where(valid, group, -1))
        rmask = iota8 == (row & 7)
        iota128 = lax.broadcasted_iota(jnp.int32, (128, wide), 0)
        pick = jnp.where(iota128 == col, 1.0, 0.0)
        partf = part.astype(F32)
        pickb = pick.astype(BF16)
        pick2 = jnp.concatenate([pickb, pickb], axis=0)

        def sample(g, acc):
            s = jnp.dot(
                bgm_ref[pl.ds(pl.multiple_of(g * rows_in, 16), rows_in), :],
                pick2,
                preferred_element_type=F32,
            )
            parts = [None] * 4
            for k in range(levels):
                x = tiles[q, k : k + 1, at_r] * s[8 * k : 8 * k + 8, :]
                parts[k % 4] = x if parts[k % 4] is None else parts[k % 4] + x
            total_g = (parts[0] + parts[1]) + (parts[2] + parts[3])
            return acc + jnp.where(group == g, total_g, 0.0)

        acc = lax.fori_loop(gmin, gmax + 1, sample, jnp.zeros((8, wide), F32))
        equiv = jnp.sum(jnp.where(rmask, acc, 0.0), axis=0, keepdims=True)
        scaled = (value - equiv) * inverse
        magnitude = jnp.abs(scaled)
        cost_ref[...] += jnp.where(
            magnitude <= HUBER_EDGE,
            0.5 * scaled * scaled,
            HUBER_EDGE * magnitude - 0.5 * HUBER_EDGE * HUBER_EDGE,
        )
        response = HUBER_EDGE / jnp.maximum(magnitude, HUBER_EDGE) * scaled * inverse
        wr = tiles[q, 0:levels, at_r] * response
        hi = wr.astype(BF16).astype(F32)
        whi[0:levels, :] = hi
        wlo[0:levels, :] = wr - hi
        low = pick * partf
        place = jnp.concatenate([(pick - low).astype(BF16), low.astype(BF16)], axis=0)
        place2 = jnp.concatenate([place, place], axis=1)

        def spread(b, _):
            m = jnp.where(rmask & (block == b), 1.0, 0.0)
            for k in range(0, levels, 2):
                for half, src in ((0, whi), (wide, wlo)):
                    x = jnp.concatenate([m * src[k : k + 1, :], m * src[k + 1 : k + 2, :]], axis=0)
                    amat[8 * k : 8 * k + 16, half : half + wide] = x.astype(BF16)
            at = pl.ds(pl.multiple_of(b * rows_in, 8), rows_in)
            force[at, :] += lax.dot_general(
                amat[...], place2, (((1,), (1,)), ((), ())), preferred_element_type=F32
            )
            return 0

        lax.fori_loop(gmin >> 1, (gmax >> 1) + 1, spread, 0)
        return 0

    lax.fori_loop(0, 8 * (total // wide), tile, 0)

    for b in range(4):
        for part in range(2):
            r0 = 32 * part + 8 * b
            sea = sea_ref[r0 : r0 + 8, :].astype(F32)

            def body(k, _):
                f = force[pl.ds(pl.multiple_of(b * rows_in + 8 * k, 8), 8), 128 * part : 128 * part + 128]
                state_ref[k, r0 : r0 + 8, :] = sea * es_ref[k, r0 : r0 + 8, :] * f
                return 0

            lax.fori_loop(0, levels, body, 0, unroll=5)


def observe_call(received, bgm, sea_mask, es, wide=WIDE):
    levels, ny, nx = es.shape
    owners = received.shape[0] // 56
    return pl.pallas_call(
        observe,
        out_shape=(
            jax.ShapeDtypeStruct((levels, ny, nx), F32),
            jax.ShapeDtypeStruct((1, wide), F32),
        ),
        in_specs=[vmem(), vmem(), vmem(), vmem()],
        out_specs=(vmem(), vmem()),
        scratch_shapes=[
            pltpu.VMEM((8, 56, 16 * owners), F32),
            pltpu.VMEM((32 * levels, 256), F32),
            pltpu.VMEM((56, wide), F32),
            pltpu.VMEM((56, wide), F32),
            pltpu.VMEM((8 * levels, 2 * wide), BF16),
        ],
        compiler_params=params(),
        name="observe",
    )(received, bgm, sea_mask, es)


def edges(x_ref, east_ref, west_ref):
    ny = x_ref.shape[1]
    nx = x_ref.shape[2]

    def body(k, _):
        x = x_ref[k]
        t = jnp.transpose(x)
        pad = jnp.zeros((8, nx - ny), F32)
        last = jnp.concatenate([t[nx - 8 : nx, :], pad], axis=1)
        sub = lax.broadcasted_iota(jnp.int32, (8, nx), 0)
        top = pltpu.roll(x[ny - 8 : ny, :], 4, axis=0)
        east_ref[k] = jnp.where(sub < 4, top, last)
        west_ref[k] = jnp.concatenate([t[0:8, :], pad], axis=1)
        return 0

    lax.fori_loop(0, x_ref.shape[0], body, 0)


def assemble(info_ref, x_ref, fw_ref, fe_ref, side_ref, one_ref, two_ref):
    levels, ny, nx = x_ref.shape
    shift = info_ref[0]
    even = info_ref[1]
    fold = info_ref[2]
    lane = lax.broadcasted_iota(jnp.int32, (8, 128), 1)
    rel_a = shift + 3 - lane
    rel_b = jnp.where(lane < 64, shift + 3 - 128 - lane, shift + 3 + 128 - lane)

    def mirror(west, own, east, rel):
        idx = rel & 127
        w = jnp.take_along_axis(west, idx, axis=1)
        o = jnp.take_along_axis(own, idx, axis=1)
        e = jnp.take_along_axis(east, idx, axis=1)
        return jnp.where(rel < 0, w, jnp.where(rel < 128, o, e))

    def body(k, _):
        fw = fw_ref[k]
        fe = fe_ref[k]
        wt = jnp.concatenate([fw, jnp.zeros((nx - 8, nx), F32)], axis=0)
        et = jnp.concatenate([fe, jnp.zeros((nx - 8, nx), F32)], axis=0)
        full = jnp.concatenate([fe, jnp.zeros((nx - 16, nx), F32), fw], axis=0)
        side = jnp.transpose(full)[0:ny, :]
        side_ref[k] = side
        top_a = pltpu.roll(x_ref[k, ny - 8 : ny, :], 4, axis=0)[0:4, :]
        top_b = pltpu.roll(side[ny - 8 : ny, :], 4, axis=0)[0:4, :]
        bot_a = x_ref[k, 0:8, :][0:4, :]
        bot_b = side[0:8, :][0:4, :]
        own8 = x_ref[k, ny - 8 : ny, :]
        east8 = side[ny - 8 : ny, :]
        west8 = pltpu.roll(fw, 4, axis=0)
        fold_a = mirror(west8, own8, east8, rel_a)
        fold_b = mirror(west8, own8, east8, rel_b)

        @pl.when(even == 1)
        def _():
            one_ref[k, :, 0:nx] = top_a
            one_ref[k, :, nx : 2 * nx] = top_b
            two_ref[k, :, 0:nx] = bot_a
            two_ref[k, :, nx : 2 * nx] = bot_b

        @pl.when(even == 0)
        def _():
            one_ref[k, :, 0:nx] = bot_a
            one_ref[k, :, nx : 2 * nx] = bot_b

            @pl.when(fold == 0)
            def _():
                two_ref[k, :, 0:nx] = top_a
                two_ref[k, :, nx : 2 * nx] = top_b

            @pl.when(fold == 1)
            def _():
                for d in range(4):
                    two_ref[k, d : d + 1, 0:nx] = fold_a[7 - d : 8 - d, :]
                    two_ref[k, d : d + 1, nx : 2 * nx] = fold_b[7 - d : 8 - d, :]

        return 0

    lax.fori_loop(0, levels, body, 0)


def diffuse(info_ref, x_ref, side_ref, one_ref, two_ref, cx_ref, cside_ref, cone_ref, ctwo_ref, es_ref, out_ref, coef):
    ny, nx = x_ref.shape[1], x_ref.shape[2]
    even = info_ref[1]

    def halo_rows(one, two):
        return jnp.where(
            even == 1,
            jnp.concatenate([one, two], axis=0),
            jnp.concatenate([two, one], axis=0),
        )

    def whole(k, x, side, one, two):
        left = jnp.concatenate([x[k], side[k]], axis=1)
        return jnp.concatenate([left, halo_rows(one[k], two[k])], axis=0)

    rows = ny + 8
    cols = 2 * nx

    @pl.when(pl.program_id(0) == 0)
    def _():
        col = lax.broadcasted_iota(jnp.int32, (rows, cols), 1)
        live = (col < nx + 4) | (col >= cols - 4)
        east = whole(0, cx_ref, cside_ref, cone_ref, ctwo_ref)
        north = whole(1, cx_ref, cside_ref, cone_ref, ctwo_ref)
        sea = whole(2, cx_ref, cside_ref, cone_ref, ctwo_ref)
        sea = jnp.where(live, sea, 0.0)
        east = jnp.where(live, east, 0.0) * sea
        north = jnp.where(live, north, 0.0) * sea
        a_e = east * pltpu.roll(sea, cols - 1, axis=1)
        a_w = east * pltpu.roll(sea, 1, axis=1)
        a_n = north * pltpu.roll(sea, rows - 1, axis=0)
        a_s = north * pltpu.roll(sea, 1, axis=0)
        coef[0] = 1.0 - ((a_e + a_w) + (a_n + a_s))
        coef[1] = a_e
        coef[2] = a_w
        coef[3] = a_n
        coef[4] = a_s

    def body(k, _):
        s = whole(k, x_ref, side_ref, one_ref, two_ref)
        for _ in range(STEPS):
            s = (
                coef[0] * s
                + (coef[1] * pltpu.roll(s, cols - 1, axis=1) + coef[2] * pltpu.roll(s, 1, axis=1))
                + (coef[3] * pltpu.roll(s, rows - 1, axis=0) + coef[4] * pltpu.roll(s, 1, axis=0))
            )
        out_ref[k] = es_ref[k] * s[0:ny, 0:nx]
        return 0

    lax.fori_loop(0, x_ref.shape[0], body, 0)


def vmem():
    return pl.BlockSpec(memory_space=pltpu.VMEM)


def smem():
    return pl.BlockSpec(memory_space=pltpu.SMEM)


def params():
    return pltpu.CompilerParams(vmem_limit_bytes=VMEM_LIMIT)


def perm_of(n_lat, n_lon, rule):
    pairs = []
    for a in range(n_lat):
        for b in range(n_lon):
            to = rule(a, b)
            if to is not None:
                pairs.append((a * n_lon + b, to[0] * n_lon + to[1] % n_lon))
    return pairs


def exchange(x, info, turn):
    levels, ny, nx = x.shape
    n_lat = lax.axis_size("lat")
    n_lon = lax.axis_size("lon")
    msg = jax.ShapeDtypeStruct((levels, 8, nx), F32)
    to_east, to_west = pl.pallas_call(
        edges,
        out_shape=(msg, msg),
        in_specs=[vmem()],
        out_specs=(vmem(), vmem()),
        compiler_params=params(),
        cost_estimate=pl.CostEstimate(flops=levels * 1000, bytes_accessed=levels * 40000, transcendentals=0),
        name="edges",
    )(x)
    from_west = lax.ppermute(to_east, "lon", [(i, (i + 1) % n_lon) for i in range(n_lon)])
    from_east = lax.ppermute(to_west, "lon", [((i + 1) % n_lon, i) for i in range(n_lon)])
    rows = jax.ShapeDtypeStruct((levels, 4, 2 * nx), F32)
    side, one, two = pl.pallas_call(
        assemble,
        out_shape=(jax.ShapeDtypeStruct(x.shape, F32), rows, rows),
        in_specs=[smem(), vmem(), vmem(), vmem()],
        out_specs=(vmem(), vmem(), vmem()),
        compiler_params=params(),
        cost_estimate=pl.CostEstimate(flops=levels * 1000, bytes_accessed=levels * 80000, transcendentals=0),
        name="assemble",
    )(info, x, from_west, from_east)
    got_one = lax.ppermute(one, ("lat", "lon"), perm_of(n_lat, n_lon, lambda a, b: (a ^ 1, b)))

    def branch(q):
        def rule(a, b):
            if a == n_lat - 1:
                return (a, q - b)
            if a == 0:
                return None
            return (((a + 1) ^ 1) - 1, b)

        return lambda v: lax.ppermute(v, ("lat", "lon"), perm_of(n_lat, n_lon, rule))

    got_two = lax.switch(turn, [branch(q) for q in range(n_lon)], two)
    return side, got_one, got_two


def shards(
    background,
    error_scale,
    east_rate,
    north_rate,
    sea_mask,
    partner,
    obs_weight,
    obs_value,
    obs_error,
    obs_column,
    obs_count,
):
    levels = background.shape[0] * background.shape[1]
    ny = background.shape[2]
    nx = background.shape[3]
    capacity = obs_weight.shape[3]
    owners = obs_weight.shape[1]
    n_lat = lax.axis_size("lat")
    n_lon = lax.axis_size("lon")
    lat_at = lax.axis_index("lat").astype(jnp.int32)

    packed = pack_call(
        obs_count, jnp.swapaxes(obs_weight[0], 0, 1), obs_value[0], obs_error[0], obs_column[0]
    )
    received = lax.all_to_all(packed, ("lat", "lon"), split_axis=0, concat_axis=0, tiled=True)

    moved = (partner[0] - 3) % (nx * n_lon)
    turn = moved // nx
    info = jnp.stack([moved % nx, 1 - lat_at % 2, (lat_at == n_lat - 1).astype(jnp.int32), turn]).astype(jnp.int32)
    coefs = jnp.stack([east_rate, north_rate, sea_mask.astype(F32)])
    cside, cone, ctwo = exchange(coefs, info, turn)

    bg = background.reshape(levels, ny, nx)
    es = error_scale.reshape(levels, ny, nx)
    bgm = pl.pallas_call(
        split_background,
        out_shape=jax.ShapeDtypeStruct((64 * levels, 256), BF16),
        in_specs=[vmem()],
        out_specs=vmem(),
        compiler_params=params(),
        cost_estimate=pl.CostEstimate(flops=3000000, bytes_accessed=3300000, transcendentals=0),
        name="split_background",
    )(bg)

    bgm, cside, cone, ctwo, received = lax.optimization_barrier((bgm, cside, cone, ctwo, received))
    state, cost = observe_call(received, bgm, sea_mask, es)

    share = jnp.sum(cost)
    shares = lax.all_to_all(
        jnp.broadcast_to(share, (owners, 1, 128)), ("lat", "lon"), split_axis=0, concat_axis=0, tiled=True
    )
    cost_share = jnp.sum(shares[:, 0, 0]) / (owners * owners * capacity)

    side, one, two = exchange(state, info, turn)

    blk = 5
    lev = lambda i: (i, 0, 0)
    fix = lambda i: (0, 0, 0)
    increment = pl.pallas_call(
        diffuse,
        grid=(levels // blk,),
        out_shape=jax.ShapeDtypeStruct((levels, ny, nx), F32),
        in_specs=[
            smem(),
            pl.BlockSpec((blk, ny, nx), lev),
            pl.BlockSpec((blk, ny, nx), lev),
            pl.BlockSpec((blk, 4, 2 * nx), lev),
            pl.BlockSpec((blk, 4, 2 * nx), lev),
            pl.BlockSpec((3, ny, nx), fix),
            pl.BlockSpec((3, ny, nx), fix),
            pl.BlockSpec((3, 4, 2 * nx), fix),
            pl.BlockSpec((3, 4, 2 * nx), fix),
            pl.BlockSpec((blk, ny, nx), lev),
        ],
        out_specs=pl.BlockSpec((blk, ny, nx), lev),
        scratch_shapes=[pltpu.VMEM((5, ny + 8, 2 * nx), F32)],
        compiler_params=params(),
        name="diffuse",
    )(info, state, side, one, two, coefs, cside, cone, ctwo, es)
    return (increment.reshape(background.shape), cost_share)


def solution(mesh):
    in_specs = (
        P(None, None, "lat", "lon"),
        P(None, None, "lat", "lon"),
        P("lat", "lon"),
        P("lat", "lon"),
        P("lat", "lon"),
        P(),
        P(("lat", "lon"), None, None, None),
        P(("lat", "lon"), None, None),
        P(("lat", "lon"), None, None),
        P(("lat", "lon"), None, None),
        P(("lat", "lon"), None),
    )
    out_specs = (P(None, None, "lat", "lon"), P())
    return jax.shard_map(shards, mesh=mesh, in_specs=in_specs, out_specs=out_specs, check_vma=False)
```

```python
import jax
import jax.numpy as jnp
from jax import lax
from jax.experimental import pallas as pl
from jax.experimental.pallas import tpu as pltpu
from jax.sharding import PartitionSpec as P

STEPS = 4
HALO = 4
HUBER_EDGE = 1.5
F32 = jnp.float32
BF16 = jnp.bfloat16
WIDE = 2048
DEEP = 56
UNROLL_DIFFUSE = 4
VMEM_LIMIT = 56 * 1024 * 1024


def split_background(bg_ref, out_ref):
    levels = bg_ref.shape[0]
    for h in range(4):
        for p in range(2):
            base = (2 * h + p) * levels * 8
            row = 32 * p + 8 * h

            def body(i, _):
                a = bg_ref[2 * i, row : row + 8, :]
                b = bg_ref[2 * i + 1, row : row + 8, :]
                x = jnp.concatenate([a, b], axis=0)
                hi = x.astype(BF16)
                lo = (x - hi.astype(F32)).astype(BF16)
                at = pl.ds(pl.multiple_of(base + i * 16, 16), 16)
                out_ref[at, 0:128] = hi
                out_ref[at, 128:256] = lo
                return 0

            lax.fori_loop(0, levels // 2, body, 0, unroll=5)


def pack(count_ref, w_ref, value_ref, error_ref, cell_ref, out_ref, order_ref, counts_ref):
    levels, some, n = w_ref.shape
    owners = order_ref.shape[0]
    lane8 = lax.broadcasted_iota(jnp.int32, (8, n), 1)

    @pl.when(pl.program_id(0) == 0)
    def _():
        counts = jnp.transpose(jnp.broadcast_to(count_ref[...].astype(F32), (owners, n)))
        lane = lax.broadcasted_iota(jnp.int32, (owners, n), 1)
        cell = cell_ref[...]
        row = cell >> 7
        key = (((row >> 3) & 3) << 11) | ((row >> 5) << 10) | ((row & 7) << 7) | (cell & 127)
        counts_ref[...] = counts.astype(jnp.int32)
        filled = lane.astype(F32) < counts
        spread = (lane.astype(F32) - counts + 0.5) * (8192.0 / jnp.maximum(n - counts, 1.0))
        key = jnp.where(filled, key, jnp.clip(spread, 0.0, 8191.0).astype(jnp.int32))
        x = (key * n + lane).astype(F32)
        size = 2
        while size <= n:
            step = size // 2
            while step >= 1:
                first = (lane & step) == 0
                other = jnp.where(first, pltpu.roll(x, n - step, axis=1), pltpu.roll(x, step, axis=1))
                least = first == ((lane & size) == 0)
                x = jnp.where(least, jnp.minimum(x, other), jnp.maximum(x, other))
                step //= 2
            size *= 2
        order_ref[...] = x.astype(jnp.int32) & (n - 1)

    for o in range(0, some, 8):
        at = pl.ds(pl.multiple_of(pl.program_id(0) * some + o, 8), 8)
        order = order_ref[at, :]
        valid = order < counts_ref[at, :]

        def put(k, v):
            out_ref[pl.ds(o * 56 + k, 8, stride=56), :] = v

        for k in range(levels):
            put(k, jnp.take_along_axis(w_ref[k, o : o + 8, :], order, axis=1))
        put(levels, jnp.take_along_axis(value_ref[at, :], order, axis=1))
        error = jnp.take_along_axis(error_ref[at, :], order, axis=1)
        put(levels + 1, jnp.where(valid, 1.0 / error, 0.0))
        put(levels + 2, jnp.take_along_axis(cell_ref[at, :], order, axis=1).astype(F32))
        for k in range(levels + 3, 56):
            put(k, jnp.zeros((8, n), F32))


def pack_call(count, weight, value, error, column):
    levels, owners, n = weight.shape
    some = 16
    return pl.pallas_call(
        pack,
        grid=(owners // some,),
        out_shape=jax.ShapeDtypeStruct((owners * 56, n), F32),
        in_specs=[
            pl.BlockSpec((1, owners), lambda i: (0, 0)),
            pl.BlockSpec((levels, some, n), lambda i: (0, i, 0)),
            pl.BlockSpec((owners, n), lambda i: (0, 0)),
            pl.BlockSpec((owners, n), lambda i: (0, 0)),
            pl.BlockSpec((owners, n), lambda i: (0, 0)),
        ],
        out_specs=pl.BlockSpec((some * 56, n), lambda i: (i, 0)),
        scratch_shapes=[pltpu.VMEM((owners, n), jnp.int32), pltpu.VMEM((owners, n), jnp.int32)],
        compiler_params=params(),
        name="pack",
    )(count, weight, value, error, column)


def observe(rec_ref, bgm_ref, east_ref, north_ref, sea_ref, es_ref, state_ref, to_east_ref, to_west_ref, cost_ref, tiles, force, whi, wlo, amat):
    levels = es_ref.shape[0]
    sources = rec_ref.shape[0] // 56
    rows_in = 8 * levels
    wide = whi.shape[1]
    total = tiles.shape[2]

    force[...] = jnp.zeros_like(force)
    cost_ref[...] = jnp.zeros_like(cost_ref)

    def regroup(eight, _):
        lane = lax.broadcasted_iota(jnp.int32, (8, 128), 1)
        for r in range(0, 56, 8):
            xs = [rec_ref[pl.ds(pl.multiple_of((eight * 8 + i) * 56 + r, 8), 8), :] for i in range(8)]
            for d in (1, 2, 4):
                keep = (lane // (16 * d)) % 2 == 0
                new = list(xs)
                for i in range(8):
                    if i & d == 0:
                        lo, hi = xs[i], xs[i + d]
                        new[i] = jnp.where(keep, lo, pltpu.roll(hi, 16 * d, axis=1))
                        new[i + d] = jnp.where(keep, pltpu.roll(lo, 128 - 16 * d, axis=1), hi)
                xs = new
            for i in range(8):
                tiles[i, r : r + 8, pl.ds(pl.multiple_of(eight * 128, 128), 128)] = xs[i]
        return 0

    lax.fori_loop(0, sources // 8, regroup, 0)

    iota8 = lax.broadcasted_iota(jnp.int32, (8, wide), 0)

    def tile(t, _):
        q = t // (total // wide)
        at_r = pl.ds(pl.multiple_of((t % (total // wide)) * wide, wide), wide)
        value = tiles[q, levels : levels + 1, at_r]
        inverse = tiles[q, levels + 1 : levels + 2, at_r]
        cell = tiles[q, levels + 2 : levels + 3, at_r].astype(jnp.int32)
        row = cell >> 7
        col = cell & 127
        part = row >> 5
        block = (row >> 3) & 3
        group = 2 * block + part
        valid = inverse > 0.0
        gmin = jnp.min(jnp.where(valid, group, 8))
        gmax = jnp.max(jnp.where(valid, group, -1))
        rmask = iota8 == (row & 7)
        iota128 = lax.broadcasted_iota(jnp.int32, (128, wide), 0)
        pick = jnp.where(iota128 == col, 1.0, 0.0)
        partf = part.astype(F32)
        pickb = pick.astype(BF16)
        pick2 = jnp.concatenate([pickb, pickb], axis=0)

        def sample(g, acc):
            s = jnp.dot(
                bgm_ref[pl.ds(pl.multiple_of(g * rows_in, 16), rows_in), :],
                pick2,
                preferred_element_type=F32,
            )
            parts = [None] * 4
            for k in range(levels):
                x = tiles[q, k : k + 1, at_r] * s[8 * k : 8 * k + 8, :]
                parts[k % 4] = x if parts[k % 4] is None else parts[k % 4] + x
            total_g = (parts[0] + parts[1]) + (parts[2] + parts[3])
            return acc + jnp.where(group == g, total_g, 0.0)

        acc = lax.fori_loop(gmin, gmax + 1, sample, jnp.zeros((8, wide), F32))
        equiv = jnp.sum(jnp.where(rmask, acc, 0.0), axis=0, keepdims=True)
        scaled = (value - equiv) * inverse
        magnitude = jnp.abs(scaled)
        cost_ref[...] += jnp.where(
            magnitude <= HUBER_EDGE,
            0.5 * scaled * scaled,
            HUBER_EDGE * magnitude - 0.5 * HUBER_EDGE * HUBER_EDGE,
        )
        response = HUBER_EDGE / jnp.maximum(magnitude, HUBER_EDGE) * scaled * inverse
        wr = tiles[q, 0:levels, at_r] * response
        hi = wr.astype(BF16).astype(F32)
        whi[0:levels, :] = hi
        wlo[0:levels, :] = wr - hi
        low = pick * partf
        place = jnp.concatenate([(pick - low).astype(BF16), low.astype(BF16)], axis=0)
        place2 = jnp.concatenate([place, place], axis=1)

        def spread(b, _):
            m = jnp.where(rmask & (block == b), 1.0, 0.0)
            for k in range(0, levels, 2):
                for half, src in ((0, whi), (wide, wlo)):
                    x = jnp.concatenate([m * src[k : k + 1, :], m * src[k + 1 : k + 2, :]], axis=0)
                    amat[8 * k : 8 * k + 16, half : half + wide] = x.astype(BF16)
            at = pl.ds(pl.multiple_of(b * rows_in, 8), rows_in)
            force[at, :] += lax.dot_general(
                amat[...], place2, (((1,), (1,)), ((), ())), preferred_element_type=F32
            )
            return 0

        lax.fori_loop(gmin >> 1, (gmax >> 1) + 1, spread, 0)
        return 0

    lax.fori_loop(0, 8 * (total // wide), tile, 0)

    for r0 in range(0, 64, 8):
        b, part = (r0 // 8) % 4, r0 // 32
        sea = sea_ref[r0 : r0 + 8, :].astype(F32)

        def level_rows(k):
            return pl.ds(r0 * DEEP + k, 8, stride=DEEP)

        state_ref[level_rows(levels), :] = east_ref[r0 : r0 + 8, :]
        state_ref[level_rows(levels + 1), :] = north_ref[r0 : r0 + 8, :]
        state_ref[level_rows(levels + 2), :] = sea
        for k in range(levels + 3, DEEP):
            state_ref[level_rows(k), :] = jnp.zeros((8, 128), F32)
        for k in range(levels):
            f = force[b * rows_in + 8 * k : b * rows_in + 8 * k + 8, 128 * part : 128 * part + 128]
            state_ref[level_rows(k), :] = sea * es_ref[k, r0 : r0 + 8, :] * f

    lane = lax.broadcasted_iota(jnp.int32, (8, 128), 1)

    def messages(g, _):
        def row(r):
            return state_ref[pl.ds(pl.multiple_of(r * DEEP + 8 * g, 8), 8), :]

        here = pl.ds(pl.multiple_of(8 * g, 8), 8)
        for half in range(2):
            last = jnp.zeros((8, 128), F32)
            first = jnp.zeros((8, 128), F32)
            for i in range(32):
                x = row(32 * half + i)
                mine = (lane >> 2) == i
                last = jnp.where(mine, pltpu.roll(x, (4 * i + 4) % 128, axis=1), last)
                first = jnp.where(mine, pltpu.roll(x, 4 * i, axis=1), first)
            to_east_ref[here, 128 * half : 128 * half + 128] = last
            to_west_ref[here, 128 * half : 128 * half + 128] = first
        more = jnp.zeros((8, 128), F32)
        for d in range(4):
            x = row(60 + d)
            to_east_ref[here, 256 + 128 * d : 384 + 128 * d] = x
            more = jnp.where((lane >> 2) == d, pltpu.roll(x, (4 * d - 4) % 128, axis=1), more)
        to_west_ref[here, 256:384] = more
        return 0

    lax.fori_loop(0, DEEP // 8, messages, 0)


def observe_call(received, bgm, east_rate, north_rate, sea_mask, es, wide=WIDE):
    levels, ny, nx = es.shape
    owners = received.shape[0] // 56
    return pl.pallas_call(
        observe,
        out_shape=(
            jax.ShapeDtypeStruct((ny * DEEP, nx), F32),
            jax.ShapeDtypeStruct((DEEP, 768), F32),
            jax.ShapeDtypeStruct((DEEP, 384), F32),
            jax.ShapeDtypeStruct((1, wide), F32),
        ),
        in_specs=[vmem()] * 6,
        out_specs=(vmem(),) * 4,
        scratch_shapes=[
            pltpu.VMEM((8, 56, 16 * owners), F32),
            pltpu.VMEM((32 * levels, 256), F32),
            pltpu.VMEM((56, wide), F32),
            pltpu.VMEM((56, wide), F32),
            pltpu.VMEM((8 * levels, 2 * wide), BF16),
        ],
        compiler_params=params(),
        name="observe",
    )(received, bgm, east_rate, north_rate, sea_mask, es)


def side_tile(fe, fw, r, lane):
    half, i = r // 32, r % 32
    e = pltpu.roll(fe[128 * half], (128 - 4 * i) % 128, axis=1)
    w = pltpu.roll(fw[128 * half], (124 - 4 * i) % 128, axis=1)
    return jnp.where(lane < 64, e, w)


def assemble(info_ref, bot_ref, top_ref, fw_ref, fe_ref, one_ref, two_ref):
    shift = info_ref[0]
    even = info_ref[1] == 1
    fold = info_ref[2] == 1
    lane = lax.broadcasted_iota(jnp.int32, (8, 128), 1)
    rel_a = shift + 3 - lane
    rel_b = jnp.where(lane < 64, shift + 3 - 128 - lane, shift + 3 + 128 - lane)

    def mirror(west, own, east, rel):
        idx = rel & 127
        w = jnp.take_along_axis(west, idx, axis=1)
        o = jnp.take_along_axis(own, idx, axis=1)
        e = jnp.take_along_axis(east, idx, axis=1)
        return jnp.where(rel < 0, w, jnp.where(rel < 128, o, e))

    def body(g, _):
        here = pl.ds(pl.multiple_of(8 * g, 8), 8)
        fe = {c: fe_ref[here, c : c + 128] for c in (0, 128, 256)}
        fw = {c: fw_ref[here, c : c + 128] for c in range(0, 768, 128)}
        top = [top_ref[d, here, :] for d in range(4)]
        top_side = [side_tile(fe, fw, 60 + d, lane) for d in range(4)]
        for d in range(4):
            u = 3 - d
            east = jnp.where(lane < 4, top_side[u], pltpu.roll(fe[256], (4 - 4 * u) % 128, axis=1))
            fold_a = mirror(fw[256 + 128 * u], top[u], east, rel_a)
            fold_b = mirror(fw[256 + 128 * u], top[u], east, rel_b)
            bot = bot_ref[d, here, :]
            bot_side = side_tile(fe, fw, d, lane)
            one_ref[d, here, 0:128] = jnp.where(even, top[d], bot)
            one_ref[d, here, 128:256] = jnp.where(even, top_side[d], bot_side)
            two_ref[d, here, 0:128] = jnp.where(even, bot, jnp.where(fold, fold_a, top[d]))
            two_ref[d, here, 128:256] = jnp.where(even, bot_side, jnp.where(fold, fold_b, top_side[d]))
        return 0

    lax.fori_loop(0, DEEP // 8, body, 0)


def diffuse(info_ref, x_ref, fw_ref, fe_ref, one_ref, two_ref, es_ref, out_ref, sa, sb, coef):
    levels = es_ref.shape[0] // 64
    even = info_ref[1] == 1
    lane = lax.broadcasted_iota(jnp.int32, (8, 128), 1)

    def fill(g, _):
        here = pl.ds(pl.multiple_of(8 * g, 8), 8)
        fe = {c: fe_ref[here, c : c + 128] for c in (0, 128)}
        fw = {c: fw_ref[here, c : c + 128] for c in (0, 128)}
        for r in range(64):
            sa[r + 4, here, 0:128] = x_ref[r, here, :]
            sa[r + 4, here, 128:256] = side_tile(fe, fw, r, lane)
        for d in range(4):
            one = one_ref[d, here, :]
            two = two_ref[d, here, :]
            sa[d, here, :] = jnp.where(even, two, one)
            sa[68 + d, here, :] = jnp.where(even, one, two)
        return 0

    lax.fori_loop(0, DEEP // 8, fill, 0)

    rows, cols = sa.shape[0], sa.shape[2]
    col = lax.broadcasted_iota(jnp.int32, (rows, cols), 1)
    live = (col < 132) | (col >= 252)
    sea = jnp.where(live, sa[:, levels + 2, :], 0.0)
    east = jnp.where(live, sa[:, levels, :], 0.0) * sea
    north = jnp.where(live, sa[:, levels + 1, :], 0.0) * sea
    a_e = east * pltpu.roll(sea, cols - 1, axis=1)
    a_w = east * pltpu.roll(sea, 1, axis=1)
    a_n = north * pltpu.roll(sea, rows - 1, axis=0)
    a_s = north * pltpu.roll(sea, 1, axis=0)
    coef[0] = 1.0 - ((a_e + a_w) + (a_n + a_s))
    coef[1] = a_e
    coef[2] = a_w
    coef[3] = a_n
    coef[4] = a_s

    def step(src, lo, hi, put):
        def body(r, _):
            c = [coef[i, pl.ds(r, 1), :] for i in range(5)]
            for g in range(DEEP // 8):
                here = slice(8 * g, 8 * g + 8)
                s = src[r, here, :]
                put(
                    r,
                    g,
                    c[0] * s
                    + (c[1] * pltpu.roll(s, cols - 1, axis=1) + c[2] * pltpu.roll(s, 1, axis=1))
                    + (c[3] * src[r + 1, here, :] + c[4] * src[r - 1, here, :]),
                )
            return 0

        lax.fori_loop(lo, hi, body, 0, unroll=UNROLL_DIFFUSE)

    def keep(dst):
        def put(r, g, v):
            dst[r, 8 * g : 8 * g + 8, :] = v

        return put

    def finish(r, g, v):
        n = min(8, levels - 8 * g)
        at = pl.ds(8 * g * 64 + r - 4, n, stride=64)
        out_ref[at, :] = es_ref[at, :] * v[0:n, 0:128]

    step(sa, 1, 71, keep(sb))
    step(sb, 2, 70, keep(sa))
    step(sa, 3, 69, keep(sb))
    step(sb, 4, 68, finish)


def vmem():
    return pl.BlockSpec(memory_space=pltpu.VMEM)


def smem():
    return pl.BlockSpec(memory_space=pltpu.SMEM)


def params():
    return pltpu.CompilerParams(vmem_limit_bytes=VMEM_LIMIT)


def perm_of(n_lat, n_lon, rule):
    pairs = []
    for a in range(n_lat):
        for b in range(n_lon):
            to = rule(a, b)
            if to is not None:
                pairs.append((a * n_lon + b, to[0] * n_lon + to[1] % n_lon))
    return pairs


def assemble_call(info, state, from_west, from_east):
    rows = jax.ShapeDtypeStruct((4, DEEP, 256), F32)
    return pl.pallas_call(
        assemble,
        grid=(1,),
        out_shape=(rows, rows),
        in_specs=[
            smem(),
            pl.BlockSpec((4, DEEP, 128), lambda i: (0, 0, 0)),
            pl.BlockSpec((4, DEEP, 128), lambda i: (15, 0, 0)),
            vmem(),
            vmem(),
        ],
        out_specs=(vmem(), vmem()),
        compiler_params=params(),
        name="assemble",
    )(info, state, state, from_west, from_east)


def exchange(state, to_east, to_west, info, turn):
    n_lat = lax.axis_size("lat")
    n_lon = lax.axis_size("lon")
    from_west = lax.ppermute(to_east, "lon", [(i, (i + 1) % n_lon) for i in range(n_lon)])
    from_east = lax.ppermute(to_west, "lon", [((i + 1) % n_lon, i) for i in range(n_lon)])
    one, two = assemble_call(info, state, from_west, from_east)
    got_one = lax.ppermute(one, ("lat", "lon"), perm_of(n_lat, n_lon, lambda a, b: (a ^ 1, b)))

    def branch(q):
        def rule(a, b):
            if a == n_lat - 1:
                return (a, q - b)
            if a == 0:
                return None
            return (((a + 1) ^ 1) - 1, b)

        return lambda v: lax.ppermute(v, ("lat", "lon"), perm_of(n_lat, n_lon, rule))

    got_two = lax.switch(turn, [branch(q) for q in range(n_lon)], two)
    return from_west, from_east, got_one, got_two


def diffuse_call(info, state, from_west, from_east, one, two, es):
    levels, ny, nx = es.shape
    out = pl.pallas_call(
        diffuse,
        out_shape=jax.ShapeDtypeStruct((levels * ny, nx), F32),
        in_specs=[smem()] + [vmem()] * 6,
        out_specs=vmem(),
        scratch_shapes=[
            pltpu.VMEM((ny + 8, DEEP, 2 * nx), F32),
            pltpu.VMEM((ny + 8, DEEP, 2 * nx), F32),
            pltpu.VMEM((5, ny + 8, 2 * nx), F32),
        ],
        compiler_params=params(),
        name="diffuse",
    )(info, state, from_west, from_east, one, two, es.reshape(levels * ny, nx))
    return out.reshape(levels, ny, nx)


def shards(
    background,
    error_scale,
    east_rate,
    north_rate,
    sea_mask,
    partner,
    obs_weight,
    obs_value,
    obs_error,
    obs_column,
    obs_count,
):
    levels = background.shape[0] * background.shape[1]
    ny = background.shape[2]
    nx = background.shape[3]
    capacity = obs_weight.shape[3]
    owners = obs_weight.shape[1]
    n_lat = lax.axis_size("lat")
    n_lon = lax.axis_size("lon")
    lat_at = lax.axis_index("lat").astype(jnp.int32)

    packed = pack_call(
        obs_count, jnp.swapaxes(obs_weight[0], 0, 1), obs_value[0], obs_error[0], obs_column[0]
    )
    received = lax.all_to_all(packed, ("lat", "lon"), split_axis=0, concat_axis=0, tiled=True)

    moved = (partner[0] - 3) % (nx * n_lon)
    turn = moved // nx
    info = jnp.stack([moved % nx, 1 - lat_at % 2, (lat_at == n_lat - 1).astype(jnp.int32), turn]).astype(jnp.int32)
    bg = background.reshape(levels, ny, nx)
    es = error_scale.reshape(levels, ny, nx)
    bgm = pl.pallas_call(
        split_background,
        out_shape=jax.ShapeDtypeStruct((64 * levels, 256), BF16),
        in_specs=[vmem()],
        out_specs=vmem(),
        compiler_params=params(),
        cost_estimate=pl.CostEstimate(flops=3000000, bytes_accessed=3300000, transcendentals=0),
        name="split_background",
    )(bg)

    state, to_east, to_west, cost = observe_call(received, bgm, east_rate, north_rate, sea_mask, es)
    state = state.reshape(ny, DEEP, nx)

    share = jnp.sum(cost)
    for axis, n in (("lon", n_lon), ("lat", n_lat)):
        shares = lax.all_to_all(jnp.broadcast_to(share, (n, 1, 128)), axis, split_axis=0, concat_axis=0, tiled=True)
        share = jnp.sum(shares[:, 0, 0])
    cost_share = share / (owners * owners * capacity)

    from_west, from_east, one, two = exchange(state, to_east, to_west, info, turn)
    increment = diffuse_call(info, state, from_west, from_east, one, two, es)
    return (increment.reshape(background.shape), cost_share)


def solution(mesh):
    in_specs = (
        P(None, None, "lat", "lon"),
        P(None, None, "lat", "lon"),
        P("lat", "lon"),
        P("lat", "lon"),
        P("lat", "lon"),
        P(),
        P(("lat", "lon"), None, None, None),
        P(("lat", "lon"), None, None),
        P(("lat", "lon"), None, None),
        P(("lat", "lon"), None, None),
        P(("lat", "lon"), None),
    )
    out_specs = (P(None, None, "lat", "lon"), P())
    return jax.shard_map(shards, mesh=mesh, in_specs=in_specs, out_specs=out_specs, check_vma=False)
```

```python
import jax
import jax.numpy as jnp
from jax import lax
from jax.experimental import pallas as pl
from jax.experimental.pallas import tpu as pltpu
from jax.sharding import PartitionSpec as P

STEPS = 4
HALO = 4
HUBER_EDGE = 1.5
F32 = jnp.float32
BF16 = jnp.bfloat16
WIDE = 2048
DEEP = 56
UNROLL_DIFFUSE = 7
VMEM_LIMIT = 56 * 1024 * 1024


def pack(
    partner_ref,
    count_ref,
    w_ref,
    value_ref,
    error_ref,
    cell_ref,
    bg_ref,
    out_ref,
    bgm_ref,
    info_ref,
    order_ref,
    counts_ref,
):
    levels, some, n = w_ref.shape
    owners = order_ref.shape[0]
    lane8 = lax.broadcasted_iota(jnp.int32, (8, n), 1)

    @pl.when(pl.program_id(0) == 0)
    def _():
        counts = jnp.transpose(jnp.broadcast_to(count_ref[...].astype(F32), (owners, n)))
        lane = lax.broadcasted_iota(jnp.int32, (owners, n), 1)
        cell = cell_ref[...]
        row = cell >> 7
        key = (((row >> 3) & 3) << 11) | ((row >> 5) << 10) | ((row & 7) << 7) | (cell & 127)
        counts_ref[...] = counts.astype(jnp.int32)
        filled = lane.astype(F32) < counts
        spread = (lane.astype(F32) - counts + 0.5) * (8192.0 / jnp.maximum(n - counts, 1.0))
        key = jnp.where(filled, key, jnp.clip(spread, 0.0, 8191.0).astype(jnp.int32))
        x = (key * n + lane).astype(F32)
        size = 2
        while size <= n:
            step = size // 2
            while step >= 1:
                first = (lane & step) == 0
                other = jnp.where(first, pltpu.roll(x, n - step, axis=1), pltpu.roll(x, step, axis=1))
                least = first == ((lane & size) == 0)
                x = jnp.where(least, jnp.minimum(x, other), jnp.maximum(x, other))
                step //= 2
            size *= 2
        order_ref[...] = x.astype(jnp.int32) & (n - 1)

    span = n * lax.axis_size("lon")
    moved = (partner_ref[0] + (span - 3)) % span
    lat_at = lax.axis_index("lat")
    info_ref[0] = moved % n
    info_ref[1] = 1 - lat_at % 2
    info_ref[2] = (lat_at == lax.axis_size("lat") - 1).astype(jnp.int32)
    info_ref[3] = moved // n

    for p in range(2):
        for k in range(0, levels, 2):
            x = jnp.concatenate([bg_ref[k, p, 0], bg_ref[k + 1, p, 0]], axis=0)
            hi = x.astype(BF16)
            at = p * 8 * levels + 8 * k
            bgm_ref[at : at + 16, 0:128] = hi
            bgm_ref[at : at + 16, 128:256] = (x - hi.astype(F32)).astype(BF16)

    for o in range(0, some, 8):
        at = pl.ds(pl.multiple_of(pl.program_id(0) * some + o, 8), 8)
        order = order_ref[at, :]
        valid = order < counts_ref[at, :]

        def put(k, v):
            out_ref[pl.ds(o * 56 + k, 8, stride=56), :] = v

        for k in range(levels):
            put(k, jnp.take_along_axis(w_ref[k, o : o + 8, :], order, axis=1))
        put(levels, jnp.take_along_axis(value_ref[at, :], order, axis=1))
        error = jnp.take_along_axis(error_ref[at, :], order, axis=1)
        put(levels + 1, jnp.where(valid, 1.0 / error, 0.0))
        put(levels + 2, jnp.take_along_axis(cell_ref[at, :], order, axis=1).astype(F32))
        for k in range(levels + 3, 56):
            put(k, jnp.zeros((8, n), F32))


def pack_call(partner, count, weight, value, error, column, bg):
    levels, owners, n = weight.shape
    ny, nx = bg.shape[1], bg.shape[2]
    steps = 4
    some = owners // steps
    whole = lambda i: (0, 0)
    return pl.pallas_call(
        pack,
        grid=(steps,),
        out_shape=(
            jax.ShapeDtypeStruct((owners * DEEP, n), F32),
            jax.ShapeDtypeStruct((levels * ny, 2 * nx), BF16),
            jax.ShapeDtypeStruct((4,), jnp.int32),
        ),
        in_specs=[
            smem(),
            pl.BlockSpec((1, owners), whole),
            pl.BlockSpec((levels, some, n), lambda i: (0, i, 0)),
            pl.BlockSpec((owners, n), whole),
            pl.BlockSpec((owners, n), whole),
            pl.BlockSpec((owners, n), whole),
            pl.BlockSpec((levels, 2, 1, 8, nx), lambda i: (0, 0, i, 0, 0)),
        ],
        out_specs=(
            pl.BlockSpec((some * DEEP, n), lambda i: (i, 0)),
            pl.BlockSpec((levels * ny // steps, 2 * nx), lambda i: (i, 0)),
            smem(),
        ),
        scratch_shapes=[pltpu.VMEM((owners, n), jnp.int32), pltpu.VMEM((owners, n), jnp.int32)],
        compiler_params=params(),
        name="pack",
    )(partner, count, weight, value, error, column, bg.reshape(levels, 2, 4, 8, nx))


def observe(rec_ref, bgm_ref, east_ref, north_ref, sea_ref, es_ref, state_ref, to_east_ref, to_west_ref, total_ref, tiles, force, whi, wlo, amat, cost_ref):
    levels = es_ref.shape[0]
    sources = rec_ref.shape[0] // 56
    rows_in = 8 * levels
    wide = whi.shape[1]
    total = tiles.shape[2]

    force[...] = jnp.zeros_like(force)
    cost_ref[...] = jnp.zeros_like(cost_ref)

    def regroup(eight, _):
        lane = lax.broadcasted_iota(jnp.int32, (8, 128), 1)
        for r in range(0, 56, 8):
            xs = [rec_ref[pl.ds(pl.multiple_of((eight * 8 + i) * 56 + r, 8), 8), :] for i in range(8)]
            for d in (1, 2, 4):
                keep = (lane // (16 * d)) % 2 == 0
                new = list(xs)
                for i in range(8):
                    if i & d == 0:
                        lo, hi = xs[i], xs[i + d]
                        new[i] = jnp.where(keep, lo, pltpu.roll(hi, 16 * d, axis=1))
                        new[i + d] = jnp.where(keep, pltpu.roll(lo, 128 - 16 * d, axis=1), hi)
                xs = new
            for i in range(8):
                tiles[i, r : r + 8, pl.ds(pl.multiple_of(eight * 128, 128), 128)] = xs[i]
        return 0

    lax.fori_loop(0, sources // 8, regroup, 0)

    iota8 = lax.broadcasted_iota(jnp.int32, (8, wide), 0)

    def tile(t, _):
        q = t // (total // wide)
        at_r = pl.ds(pl.multiple_of((t % (total // wide)) * wide, wide), wide)
        value = tiles[q, levels : levels + 1, at_r]
        inverse = tiles[q, levels + 1 : levels + 2, at_r]
        cell = tiles[q, levels + 2 : levels + 3, at_r].astype(jnp.int32)
        row = cell >> 7
        col = cell & 127
        part = row >> 5
        block = (row >> 3) & 3
        group = 2 * block + part
        valid = inverse > 0.0
        gmin = jnp.min(jnp.where(valid, group, 8))
        gmax = jnp.max(jnp.where(valid, group, -1))
        rmask = iota8 == (row & 7)
        iota128 = lax.broadcasted_iota(jnp.int32, (128, wide), 0)
        pick = jnp.where(iota128 == col, 1.0, 0.0)
        partf = part.astype(F32)
        pickb = pick.astype(BF16)
        pick2 = jnp.concatenate([pickb, pickb], axis=0)

        def sample(g, acc):
            s = jnp.dot(
                bgm_ref[pl.ds(pl.multiple_of(g * rows_in, 16), rows_in), :],
                pick2,
                preferred_element_type=F32,
            )
            parts = [None] * 4
            for k in range(levels):
                x = tiles[q, k : k + 1, at_r] * s[8 * k : 8 * k + 8, :]
                parts[k % 4] = x if parts[k % 4] is None else parts[k % 4] + x
            total_g = (parts[0] + parts[1]) + (parts[2] + parts[3])
            return acc + jnp.where(group == g, total_g, 0.0)

        acc = lax.fori_loop(gmin, gmax + 1, sample, jnp.zeros((8, wide), F32))
        equiv = jnp.sum(jnp.where(rmask, acc, 0.0), axis=0, keepdims=True)
        scaled = (value - equiv) * inverse
        magnitude = jnp.abs(scaled)
        cost_ref[...] += jnp.where(
            magnitude <= HUBER_EDGE,
            0.5 * scaled * scaled,
            HUBER_EDGE * magnitude - 0.5 * HUBER_EDGE * HUBER_EDGE,
        )
        response = HUBER_EDGE / jnp.maximum(magnitude, HUBER_EDGE) * scaled * inverse
        wr = tiles[q, 0:levels, at_r] * response
        hi = wr.astype(BF16).astype(F32)
        whi[0:levels, :] = hi
        wlo[0:levels, :] = wr - hi
        low = pick * partf
        place = jnp.concatenate([(pick - low).astype(BF16), low.astype(BF16)], axis=0)
        place2 = jnp.concatenate([place, place], axis=1)

        def spread(b, _):
            m = jnp.where(rmask & (block == b), 1.0, 0.0)
            for k in range(0, levels, 2):
                for half, src in ((0, whi), (wide, wlo)):
                    x = jnp.concatenate([m * src[k : k + 1, :], m * src[k + 1 : k + 2, :]], axis=0)
                    amat[8 * k : 8 * k + 16, half : half + wide] = x.astype(BF16)
            at = pl.ds(pl.multiple_of(b * rows_in, 8), rows_in)
            force[at, :] += lax.dot_general(
                amat[...], place2, (((1,), (1,)), ((), ())), preferred_element_type=F32
            )
            return 0

        lax.fori_loop(gmin >> 1, (gmax >> 1) + 1, spread, 0)
        return 0

    lax.fori_loop(0, 8 * (total // wide), tile, 0)

    total_ref[...] = jnp.broadcast_to(jnp.sum(cost_ref[...], axis=1, keepdims=True)[None], total_ref.shape)

    for r0 in range(0, 64, 8):
        b, part = (r0 // 8) % 4, r0 // 32
        sea = sea_ref[r0 : r0 + 8, :].astype(F32)

        def level_rows(k):
            return pl.ds(r0 * DEEP + k, 8, stride=DEEP)

        state_ref[level_rows(levels), :] = east_ref[r0 : r0 + 8, :]
        state_ref[level_rows(levels + 1), :] = north_ref[r0 : r0 + 8, :]
        state_ref[level_rows(levels + 2), :] = sea
        for k in range(levels + 3, DEEP):
            state_ref[level_rows(k), :] = jnp.zeros((8, 128), F32)
        for k in range(levels):
            f = force[b * rows_in + 8 * k : b * rows_in + 8 * k + 8, 128 * part : 128 * part + 128]
            state_ref[level_rows(k), :] = sea * es_ref[k, r0 : r0 + 8, :] * f

    lane = lax.broadcasted_iota(jnp.int32, (8, 128), 1)

    def messages(g, _):
        def row(r):
            return state_ref[pl.ds(pl.multiple_of(r * DEEP + 8 * g, 8), 8), :]

        here = pl.ds(pl.multiple_of(8 * g, 8), 8)
        for half in range(2):
            last = jnp.zeros((8, 128), F32)
            first = jnp.zeros((8, 128), F32)
            for i in range(32):
                x = row(32 * half + i)
                mine = (lane >> 2) == i
                last = jnp.where(mine, pltpu.roll(x, (4 * i + 4) % 128, axis=1), last)
                first = jnp.where(mine, pltpu.roll(x, 4 * i, axis=1), first)
            to_east_ref[here, 128 * half : 128 * half + 128] = last
            to_west_ref[here, 128 * half : 128 * half + 128] = first
        more = jnp.zeros((8, 128), F32)
        for d in range(4):
            x = row(60 + d)
            to_east_ref[here, 256 + 128 * d : 384 + 128 * d] = x
            more = jnp.where((lane >> 2) == d, pltpu.roll(x, (4 * d - 4) % 128, axis=1), more)
        to_west_ref[here, 256:384] = more
        return 0

    lax.fori_loop(0, DEEP // 8, messages, 0)


def observe_call(received, bgm, east_rate, north_rate, sea_mask, es, wide=WIDE):
    levels, ny, nx = es.shape
    owners = received.shape[0] // 56
    return pl.pallas_call(
        observe,
        out_shape=(
            jax.ShapeDtypeStruct((ny * DEEP, nx), F32),
            jax.ShapeDtypeStruct((DEEP, 768), F32),
            jax.ShapeDtypeStruct((DEEP, 384), F32),
            jax.ShapeDtypeStruct((owners, 1, 128), F32),
        ),
        in_specs=[vmem()] * 6,
        out_specs=(vmem(),) * 4,
        scratch_shapes=[
            pltpu.VMEM((8, 56, 16 * owners), F32),
            pltpu.VMEM((32 * levels, 256), F32),
            pltpu.VMEM((56, wide), F32),
            pltpu.VMEM((56, wide), F32),
            pltpu.VMEM((8 * levels, 2 * wide), BF16),
            pltpu.VMEM((1, wide), F32),
        ],
        compiler_params=params(),
        name="observe",
    )(received, bgm, east_rate, north_rate, sea_mask, es)


def side_tile(fe, fw, r, lane):
    half, i = r // 32, r % 32
    e = pltpu.roll(fe[128 * half], (128 - 4 * i) % 128, axis=1)
    w = pltpu.roll(fw[128 * half], (124 - 4 * i) % 128, axis=1)
    return jnp.where(lane < 64, e, w)


def assemble(info_ref, bot_ref, top_ref, fw_ref, fe_ref, one_ref, two_ref):
    shift = info_ref[0]
    even = info_ref[1] == 1
    fold = info_ref[2] == 1
    lane = lax.broadcasted_iota(jnp.int32, (8, 128), 1)
    rel_a = shift + 3 - lane
    rel_b = jnp.where(lane < 64, shift + 3 - 128 - lane, shift + 3 + 128 - lane)

    def mirror(west, own, east, rel):
        idx = rel & 127
        w = jnp.take_along_axis(west, idx, axis=1)
        o = jnp.take_along_axis(own, idx, axis=1)
        e = jnp.take_along_axis(east, idx, axis=1)
        return jnp.where(rel < 0, w, jnp.where(rel < 128, o, e))

    def body(g, _):
        here = pl.ds(pl.multiple_of(8 * g, 8), 8)
        fe = {c: fe_ref[here, c : c + 128] for c in (0, 128, 256)}
        fw = {c: fw_ref[here, c : c + 128] for c in range(0, 768, 128)}
        top = [top_ref[d, here, :] for d in range(4)]
        top_side = [side_tile(fe, fw, 60 + d, lane) for d in range(4)]
        for d in range(4):
            u = 3 - d
            east = jnp.where(lane < 4, top_side[u], pltpu.roll(fe[256], (4 - 4 * u) % 128, axis=1))
            fold_a = mirror(fw[256 + 128 * u], top[u], east, rel_a)
            fold_b = mirror(fw[256 + 128 * u], top[u], east, rel_b)
            bot = bot_ref[d, here, :]
            bot_side = side_tile(fe, fw, d, lane)
            one_ref[d, here, 0:128] = jnp.where(even, top[d], bot)
            one_ref[d, here, 128:256] = jnp.where(even, top_side[d], bot_side)
            two_ref[d, here, 0:128] = jnp.where(even, bot, jnp.where(fold, fold_a, top[d]))
            two_ref[d, here, 128:256] = jnp.where(even, bot_side, jnp.where(fold, fold_b, top_side[d]))
        return 0

    lax.fori_loop(0, DEEP // 8, body, 0)


def diffuse(info_ref, x_ref, fw_ref, fe_ref, one_ref, two_ref, es_ref, out_ref, sa, sb, coef):
    levels = es_ref.shape[0] // 64
    even = info_ref[1] == 1
    lane = lax.broadcasted_iota(jnp.int32, (8, 128), 1)

    def fill(g, _):
        here = pl.ds(pl.multiple_of(8 * g, 8), 8)
        fe = {c: fe_ref[here, c : c + 128] for c in (0, 128)}
        fw = {c: fw_ref[here, c : c + 128] for c in (0, 128)}
        for r in range(64):
            sa[r + 4, here, 0:128] = x_ref[r, here, :]
            sa[r + 4, here, 128:256] = side_tile(fe, fw, r, lane)
        for d in range(4):
            one = one_ref[d, here, :]
            two = two_ref[d, here, :]
            sa[d, here, :] = jnp.where(even, two, one)
            sa[68 + d, here, :] = jnp.where(even, one, two)
        return 0

    lax.fori_loop(0, DEEP // 8, fill, 0)

    rows, cols = sa.shape[0], sa.shape[2]
    col = lax.broadcasted_iota(jnp.int32, (rows, cols), 1)
    live = (col < 132) | (col >= 252)
    sea = jnp.where(live, sa[:, levels + 2, :], 0.0)
    east = jnp.where(live, sa[:, levels, :], 0.0) * sea
    north = jnp.where(live, sa[:, levels + 1, :], 0.0) * sea
    a_e = east * pltpu.roll(sea, cols - 1, axis=1)
    a_w = east * pltpu.roll(sea, 1, axis=1)
    a_n = north * pltpu.roll(sea, rows - 1, axis=0)
    a_s = north * pltpu.roll(sea, 1, axis=0)
    coef[0] = 1.0 - ((a_e + a_w) + (a_n + a_s))
    coef[1] = a_e
    coef[2] = a_w
    coef[3] = a_n
    coef[4] = a_s

    def step(src, lo, hi, put):
        def body(r, _):
            c = [coef[i, pl.ds(r, 1), :] for i in range(5)]
            for g in range(DEEP // 8):
                here = slice(8 * g, 8 * g + 8)
                s = src[r, here, :]
                put(
                    r,
                    g,
                    c[0] * s
                    + (c[1] * pltpu.roll(s, cols - 1, axis=1) + c[2] * pltpu.roll(s, 1, axis=1))
                    + (c[3] * src[r + 1, here, :] + c[4] * src[r - 1, here, :]),
                )
            return 0

        lax.fori_loop(lo, hi, body, 0, unroll=UNROLL_DIFFUSE)

    def keep(dst):
        def put(r, g, v):
            dst[r, 8 * g : 8 * g + 8, :] = v

        return put

    def finish(r, g, v):
        n = min(8, levels - 8 * g)
        at = pl.ds(8 * g * 64 + r - 4, n, stride=64)
        out_ref[at, :] = es_ref[at, :] * v[0:n, 0:128]

    step(sa, 1, 71, keep(sb))
    step(sb, 2, 70, keep(sa))
    step(sa, 3, 69, keep(sb))
    step(sb, 4, 68, finish)


def vmem():
    return pl.BlockSpec(memory_space=pltpu.VMEM)


def smem():
    return pl.BlockSpec(memory_space=pltpu.SMEM)


def params():
    return pltpu.CompilerParams(vmem_limit_bytes=VMEM_LIMIT)


def perm_of(n_lat, n_lon, rule):
    pairs = []
    for a in range(n_lat):
        for b in range(n_lon):
            to = rule(a, b)
            if to is not None:
                pairs.append((a * n_lon + b, to[0] * n_lon + to[1] % n_lon))
    return pairs


def assemble_call(info, state, from_west, from_east):
    rows = jax.ShapeDtypeStruct((4, DEEP, 256), F32)
    return pl.pallas_call(
        assemble,
        grid=(1,),
        out_shape=(rows, rows),
        in_specs=[
            smem(),
            pl.BlockSpec((4, DEEP, 128), lambda i: (0, 0, 0)),
            pl.BlockSpec((4, DEEP, 128), lambda i: (15, 0, 0)),
            vmem(),
            vmem(),
        ],
        out_specs=(vmem(), vmem()),
        compiler_params=params(),
        name="assemble",
    )(info, state, state, from_west, from_east)


def exchange(state, to_east, to_west, info, turn):
    n_lat = lax.axis_size("lat")
    n_lon = lax.axis_size("lon")
    from_west = lax.ppermute(to_east, "lon", [(i, (i + 1) % n_lon) for i in range(n_lon)])
    from_east = lax.ppermute(to_west, "lon", [((i + 1) % n_lon, i) for i in range(n_lon)])
    one, two = assemble_call(info, state, from_west, from_east)
    got_one = lax.ppermute(one, ("lat", "lon"), perm_of(n_lat, n_lon, lambda a, b: (a ^ 1, b)))

    def branch(q):
        def rule(a, b):
            if a == n_lat - 1:
                return (a, q - b)
            if a == 0:
                return None
            return (((a + 1) ^ 1) - 1, b)

        return lambda v: lax.ppermute(v, ("lat", "lon"), perm_of(n_lat, n_lon, rule))

    got_two = lax.switch(turn, [branch(q) for q in range(n_lon)], two)
    return from_west, from_east, got_one, got_two


def diffuse_call(info, state, from_west, from_east, one, two, es):
    levels, ny, nx = es.shape
    out = pl.pallas_call(
        diffuse,
        out_shape=jax.ShapeDtypeStruct((levels * ny, nx), F32),
        in_specs=[smem()] + [vmem()] * 6,
        out_specs=vmem(),
        scratch_shapes=[
            pltpu.VMEM((ny + 8, DEEP, 2 * nx), F32),
            pltpu.VMEM((ny + 8, DEEP, 2 * nx), F32),
            pltpu.VMEM((5, ny + 8, 2 * nx), F32),
        ],
        compiler_params=params(),
        name="diffuse",
    )(info, state, from_west, from_east, one, two, es.reshape(levels * ny, nx))
    return out.reshape(levels, ny, nx)


def shards(
    background,
    error_scale,
    east_rate,
    north_rate,
    sea_mask,
    partner,
    obs_weight,
    obs_value,
    obs_error,
    obs_column,
    obs_count,
):
    levels = background.shape[0] * background.shape[1]
    ny = background.shape[2]
    nx = background.shape[3]
    capacity = obs_weight.shape[3]
    owners = obs_weight.shape[1]
    bg = background.reshape(levels, ny, nx)
    es = error_scale.reshape(levels, ny, nx)
    packed, bgm, info = pack_call(
        partner, obs_count, jnp.swapaxes(obs_weight[0], 0, 1), obs_value[0], obs_error[0], obs_column[0], bg
    )
    turn = info[3]
    packed, bgm, info, turn = lax.optimization_barrier((packed, bgm, info, turn))
    received = lax.all_to_all(packed, ("lat", "lon"), split_axis=0, concat_axis=0, tiled=True)
    state, to_east, to_west, cost = observe_call(received, bgm, east_rate, north_rate, sea_mask, es)
    state = state.reshape(ny, DEEP, nx)

    shares = lax.all_to_all(cost, ("lat", "lon"), split_axis=0, concat_axis=0, tiled=True)
    cost_share = jnp.sum(shares[:, 0, 0]) / (owners * owners * capacity)

    from_west, from_east, one, two = exchange(state, to_east, to_west, info, turn)
    increment = diffuse_call(info, state, from_west, from_east, one, two, es)
    return (increment.reshape(background.shape), cost_share)


def solution(mesh):
    in_specs = (
        P(None, None, "lat", "lon"),
        P(None, None, "lat", "lon"),
        P("lat", "lon"),
        P("lat", "lon"),
        P("lat", "lon"),
        P(),
        P(("lat", "lon"), None, None, None),
        P(("lat", "lon"), None, None),
        P(("lat", "lon"), None, None),
        P(("lat", "lon"), None, None),
        P(("lat", "lon"), None),
    )
    out_specs = (P(None, None, "lat", "lon"), P())
    return jax.shard_map(shards, mesh=mesh, in_specs=in_specs, out_specs=out_specs, check_vma=False)
```

```python
import jax
import jax.numpy as jnp
from jax import lax
from jax.experimental import pallas as pl
from jax.experimental.pallas import tpu as pltpu
from jax.sharding import PartitionSpec as P

STEPS = 4
HALO = 4
HUBER_EDGE = 1.5
F32 = jnp.float32
BF16 = jnp.bfloat16
WIDE = 2048
DEEP = 56
UNROLL_DIFFUSE = 7
VMEM_LIMIT = 56 * 1024 * 1024


def pack(
    partner_ref,
    count_ref,
    w_ref,
    value_ref,
    error_ref,
    cell_ref,
    bg_ref,
    out_ref,
    bgm_ref,
    info_ref,
    order_ref,
    counts_ref,
):
    levels, some, n = w_ref.shape
    owners = order_ref.shape[0]
    lane8 = lax.broadcasted_iota(jnp.int32, (8, n), 1)

    @pl.when(pl.program_id(0) == 0)
    def _():
        counts = jnp.transpose(jnp.broadcast_to(count_ref[...].astype(F32), (owners, n)))
        lane = lax.broadcasted_iota(jnp.int32, (owners, n), 1)
        cell = cell_ref[...]
        row = cell >> 7
        key = (((row >> 3) & 3) << 11) | ((row >> 5) << 10) | ((row & 7) << 7) | (cell & 127)
        counts_ref[...] = counts.astype(jnp.int32)
        filled = lane.astype(F32) < counts
        spread = (lane.astype(F32) - counts + 0.5) * (8192.0 / jnp.maximum(n - counts, 1.0))
        key = jnp.where(filled, key, jnp.clip(spread, 0.0, 8191.0).astype(jnp.int32))
        x = (key * n + lane).astype(F32)
        size = 2
        while size <= n:
            step = size // 2
            while step >= 1:
                first = (lane & step) == 0
                other = jnp.where(first, pltpu.roll(x, n - step, axis=1), pltpu.roll(x, step, axis=1))
                least = first == ((lane & size) == 0)
                x = jnp.where(least, jnp.minimum(x, other), jnp.maximum(x, other))
                step //= 2
            size *= 2
        order_ref[...] = x.astype(jnp.int32) & (n - 1)

    span = n * lax.axis_size("lon")
    moved = (partner_ref[0] + (span - 3)) % span
    lat_at = lax.axis_index("lat")
    info_ref[0] = moved % n
    info_ref[1] = 1 - lat_at % 2
    info_ref[2] = (lat_at == lax.axis_size("lat") - 1).astype(jnp.int32)
    info_ref[3] = moved // n

    for p in range(2):
        for k in range(0, levels, 2):
            x = jnp.concatenate([bg_ref[k, p, 0], bg_ref[k + 1, p, 0]], axis=0)
            hi = x.astype(BF16)
            at = p * 8 * levels + 8 * k
            bgm_ref[at : at + 16, 0:128] = hi
            bgm_ref[at : at + 16, 128:256] = (x - hi.astype(F32)).astype(BF16)

    for o in range(0, some, 8):
        at = pl.ds(pl.multiple_of(pl.program_id(0) * some + o, 8), 8)
        order = order_ref[at, :]
        valid = order < counts_ref[at, :]

        def put(k, v):
            out_ref[pl.ds(o * 56 + k, 8, stride=56), :] = v

        for k in range(levels):
            put(k, jnp.take_along_axis(w_ref[k, o : o + 8, :], order, axis=1))
        put(levels, jnp.take_along_axis(value_ref[at, :], order, axis=1))
        error = jnp.take_along_axis(error_ref[at, :], order, axis=1)
        put(levels + 1, jnp.where(valid, 1.0 / error, 0.0))
        put(levels + 2, jnp.take_along_axis(cell_ref[at, :], order, axis=1).astype(F32))
        for k in range(levels + 3, 56):
            put(k, jnp.zeros((8, n), F32))


def pack_call(partner, count, weight, value, error, column, bg):
    levels, owners, n = weight.shape
    ny, nx = bg.shape[1], bg.shape[2]
    steps = 4
    some = owners // steps
    whole = lambda i: (0, 0)
    return pl.pallas_call(
        pack,
        grid=(steps,),
        out_shape=(
            jax.ShapeDtypeStruct((owners * DEEP, n), F32),
            jax.ShapeDtypeStruct((levels * ny, 2 * nx), BF16),
            jax.ShapeDtypeStruct((4,), jnp.int32),
        ),
        in_specs=[
            smem(),
            pl.BlockSpec((1, owners), whole),
            pl.BlockSpec((levels, some, n), lambda i: (0, i, 0)),
            pl.BlockSpec((owners, n), whole),
            pl.BlockSpec((owners, n), whole),
            pl.BlockSpec((owners, n), whole),
            pl.BlockSpec((levels, 2, 1, 8, nx), lambda i: (0, 0, i, 0, 0)),
        ],
        out_specs=(
            pl.BlockSpec((some * DEEP, n), lambda i: (i, 0)),
            pl.BlockSpec((levels * ny // steps, 2 * nx), lambda i: (i, 0)),
            smem(),
        ),
        scratch_shapes=[pltpu.VMEM((owners, n), jnp.int32), pltpu.VMEM((owners, n), jnp.int32)],
        compiler_params=params(),
        name="pack",
    )(partner, count, weight, value, error, column, bg.reshape(levels, 2, 4, 8, nx))


def observe(rec_ref, bgm_ref, east_ref, north_ref, sea_ref, es_ref, state_ref, to_east_ref, to_west_ref, total_ref, tiles, force, whi, wlo, amat, cost_ref):
    levels = es_ref.shape[0]
    sources = rec_ref.shape[0] // 56
    rows_in = 8 * levels
    wide = whi.shape[1]
    total = tiles.shape[2]

    force[...] = jnp.zeros_like(force)
    cost_ref[...] = jnp.zeros_like(cost_ref)

    def regroup(eight, _):
        lane = lax.broadcasted_iota(jnp.int32, (8, 128), 1)
        for r in range(0, 56, 8):
            xs = [rec_ref[pl.ds(pl.multiple_of((eight * 8 + i) * 56 + r, 8), 8), :] for i in range(8)]
            for d in (1, 2, 4):
                keep = (lane // (16 * d)) % 2 == 0
                new = list(xs)
                for i in range(8):
                    if i & d == 0:
                        lo, hi = xs[i], xs[i + d]
                        new[i] = jnp.where(keep, lo, pltpu.roll(hi, 16 * d, axis=1))
                        new[i + d] = jnp.where(keep, pltpu.roll(lo, 128 - 16 * d, axis=1), hi)
                xs = new
            for i in range(8):
                tiles[i, r : r + 8, pl.ds(pl.multiple_of(eight * 128, 128), 128)] = xs[i]
        return 0

    lax.fori_loop(0, sources // 8, regroup, 0)

    iota8 = lax.broadcasted_iota(jnp.int32, (8, wide), 0)

    def tile(t, _):
        q = t // (total // wide)
        at_r = pl.ds(pl.multiple_of((t % (total // wide)) * wide, wide), wide)
        value = tiles[q, levels : levels + 1, at_r]
        inverse = tiles[q, levels + 1 : levels + 2, at_r]
        cell = tiles[q, levels + 2 : levels + 3, at_r].astype(jnp.int32)
        row = cell >> 7
        col = cell & 127
        part = row >> 5
        block = (row >> 3) & 3
        group = 2 * block + part
        valid = inverse > 0.0
        gmin = jnp.min(jnp.where(valid, group, 8))
        gmax = jnp.max(jnp.where(valid, group, -1))
        rmask = iota8 == (row & 7)
        iota128 = lax.broadcasted_iota(jnp.int32, (128, wide), 0)
        pick = jnp.where(iota128 == col, 1.0, 0.0)
        partf = part.astype(F32)
        pickb = pick.astype(BF16)
        pick2 = jnp.concatenate([pickb, pickb], axis=0)

        def sample(g, acc):
            s = jnp.dot(
                bgm_ref[pl.ds(pl.multiple_of(g * rows_in, 16), rows_in), :],
                pick2,
                preferred_element_type=F32,
            )
            parts = [None] * 4
            for k in range(levels):
                x = tiles[q, k : k + 1, at_r] * s[8 * k : 8 * k + 8, :]
                parts[k % 4] = x if parts[k % 4] is None else parts[k % 4] + x
            total_g = (parts[0] + parts[1]) + (parts[2] + parts[3])
            return acc + jnp.where(group == g, total_g, 0.0)

        acc = lax.fori_loop(gmin, gmax + 1, sample, jnp.zeros((8, wide), F32))
        equiv = jnp.sum(jnp.where(rmask, acc, 0.0), axis=0, keepdims=True)
        scaled = (value - equiv) * inverse
        magnitude = jnp.abs(scaled)
        cost_ref[...] += jnp.where(
            magnitude <= HUBER_EDGE,
            0.5 * scaled * scaled,
            HUBER_EDGE * magnitude - 0.5 * HUBER_EDGE * HUBER_EDGE,
        )
        response = HUBER_EDGE / jnp.maximum(magnitude, HUBER_EDGE) * scaled * inverse
        wr = tiles[q, 0:levels, at_r] * response
        hi = wr.astype(BF16).astype(F32)
        whi[0:levels, :] = hi
        wlo[0:levels, :] = wr - hi
        low = pick * partf
        place = jnp.concatenate([(pick - low).astype(BF16), low.astype(BF16)], axis=0)
        place2 = jnp.concatenate([place, place], axis=1)

        def spread(b, _):
            m = jnp.where(rmask & (block == b), 1.0, 0.0)
            for k in range(0, levels, 2):
                for half, src in ((0, whi), (wide, wlo)):
                    x = jnp.concatenate([m * src[k : k + 1, :], m * src[k + 1 : k + 2, :]], axis=0)
                    amat[8 * k : 8 * k + 16, half : half + wide] = x.astype(BF16)
            at = pl.ds(pl.multiple_of(b * rows_in, 8), rows_in)
            force[at, :] += lax.dot_general(
                amat[...], place2, (((1,), (1,)), ((), ())), preferred_element_type=F32
            )
            return 0

        lax.fori_loop(gmin >> 1, (gmax >> 1) + 1, spread, 0)
        return 0

    lax.fori_loop(0, 8 * (total // wide), tile, 0)

    total_ref[...] = jnp.broadcast_to(jnp.sum(cost_ref[...], axis=1, keepdims=True)[None], total_ref.shape)

    for r0 in range(0, 64, 8):
        b, part = (r0 // 8) % 4, r0 // 32
        sea = sea_ref[r0 : r0 + 8, :].astype(F32)

        def level_rows(k):
            return pl.ds(r0 * DEEP + k, 8, stride=DEEP)

        state_ref[level_rows(levels), :] = east_ref[r0 : r0 + 8, :]
        state_ref[level_rows(levels + 1), :] = north_ref[r0 : r0 + 8, :]
        state_ref[level_rows(levels + 2), :] = sea
        for k in range(levels + 3, DEEP):
            state_ref[level_rows(k), :] = jnp.zeros((8, 128), F32)
        for k in range(levels):
            f = force[b * rows_in + 8 * k : b * rows_in + 8 * k + 8, 128 * part : 128 * part + 128]
            state_ref[level_rows(k), :] = sea * es_ref[k, r0 : r0 + 8, :] * f

    lane = lax.broadcasted_iota(jnp.int32, (8, 128), 1)

    def messages(g, _):
        def row(r):
            return state_ref[pl.ds(pl.multiple_of(r * DEEP + 8 * g, 8), 8), :]

        here = pl.ds(pl.multiple_of(8 * g, 8), 8)
        for half in range(2):
            last = jnp.zeros((8, 128), F32)
            first = jnp.zeros((8, 128), F32)
            for i in range(32):
                x = row(32 * half + i)
                mine = (lane >> 2) == i
                last = jnp.where(mine, pltpu.roll(x, (4 * i + 4) % 128, axis=1), last)
                first = jnp.where(mine, pltpu.roll(x, 4 * i, axis=1), first)
            to_east_ref[here, 128 * half : 128 * half + 128] = last
            to_west_ref[here, 128 * half : 128 * half + 128] = first
        more = jnp.zeros((8, 128), F32)
        for d in range(4):
            x = row(60 + d)
            to_east_ref[here, 256 + 128 * d : 384 + 128 * d] = x
            more = jnp.where((lane >> 2) == d, pltpu.roll(x, (4 * d - 4) % 128, axis=1), more)
        to_west_ref[here, 256:384] = more
        return 0

    lax.fori_loop(0, DEEP // 8, messages, 0)


def observe_call(received, bgm, east_rate, north_rate, sea_mask, es, wide=WIDE):
    levels, ny, nx = es.shape
    owners = received.shape[0] // 56
    return pl.pallas_call(
        observe,
        out_shape=(
            jax.ShapeDtypeStruct((ny * DEEP, nx), F32),
            jax.ShapeDtypeStruct((DEEP, 768), F32),
            jax.ShapeDtypeStruct((DEEP, 384), F32),
            jax.ShapeDtypeStruct((owners, 1, 128), F32),
        ),
        in_specs=[vmem()] * 6,
        out_specs=(vmem(),) * 4,
        scratch_shapes=[
            pltpu.VMEM((8, 56, 16 * owners), F32),
            pltpu.VMEM((32 * levels, 256), F32),
            pltpu.VMEM((56, wide), F32),
            pltpu.VMEM((56, wide), F32),
            pltpu.VMEM((8 * levels, 2 * wide), BF16),
            pltpu.VMEM((1, wide), F32),
        ],
        compiler_params=params(),
        name="observe",
    )(received, bgm, east_rate, north_rate, sea_mask, es)


def side_tile(fe, fw, r, lane):
    half, i = r // 32, r % 32
    e = pltpu.roll(fe[128 * half], (128 - 4 * i) % 128, axis=1)
    w = pltpu.roll(fw[128 * half], (124 - 4 * i) % 128, axis=1)
    return jnp.where(lane < 64, e, w)


def assemble(info_ref, bot_ref, top_ref, fw_ref, fe_ref, one_ref, two_ref):
    shift = info_ref[0]
    even = info_ref[1] == 1
    fold = info_ref[2] == 1
    lane = lax.broadcasted_iota(jnp.int32, (8, 128), 1)
    rel_a = shift + 3 - lane
    rel_b = jnp.where(lane < 64, shift + 3 - 128 - lane, shift + 3 + 128 - lane)

    def mirror(west, own, east, rel):
        idx = rel & 127
        w = jnp.take_along_axis(west, idx, axis=1)
        o = jnp.take_along_axis(own, idx, axis=1)
        e = jnp.take_along_axis(east, idx, axis=1)
        return jnp.where(rel < 0, w, jnp.where(rel < 128, o, e))

    def body(g, _):
        here = pl.ds(pl.multiple_of(8 * g, 8), 8)
        fe = {c: fe_ref[here, c : c + 128] for c in (0, 128, 256)}
        fw = {c: fw_ref[here, c : c + 128] for c in range(0, 768, 128)}
        top = [top_ref[d, here, :] for d in range(4)]
        top_side = [side_tile(fe, fw, 60 + d, lane) for d in range(4)]
        sides = [jnp.zeros((8, 128), F32) for _ in range(3)]
        for d in range(4):
            u = 3 - d
            east = jnp.where(lane < 4, top_side[u], pltpu.roll(fe[256], (4 - 4 * u) % 128, axis=1))
            fold_a = mirror(fw[256 + 128 * u], top[u], east, rel_a)
            fold_b = mirror(fw[256 + 128 * u], top[u], east, rel_b)
            bot = bot_ref[d, here, :]
            one_ref[d, here, :] = jnp.where(even, top[d], bot)
            two_ref[d, here, :] = jnp.where(even, bot, jnp.where(fold, fold_a, top[d]))
            for n, x in enumerate((top_side[d], side_tile(fe, fw, d, lane), fold_b)):
                sides[n] = jnp.where((lane >> 3) == d, pltpu.roll(x, 8 * d + 4, axis=1), sides[n])
        one_ref[4, here, :] = jnp.where(even, sides[0], sides[1])
        two_ref[4, here, :] = jnp.where(even, sides[1], jnp.where(fold, sides[2], sides[0]))
        return 0

    lax.fori_loop(0, DEEP // 8, body, 0)


def diffuse(info_ref, x_ref, fw_ref, fe_ref, one_ref, two_ref, es_ref, out_ref, sa, sb, coef):
    levels = es_ref.shape[0] // 64
    even = info_ref[1] == 1
    lane = lax.broadcasted_iota(jnp.int32, (8, 128), 1)

    def fill(g, _):
        here = pl.ds(pl.multiple_of(8 * g, 8), 8)
        fe = {c: fe_ref[here, c : c + 128] for c in (0, 128)}
        fw = {c: fw_ref[here, c : c + 128] for c in (0, 128)}
        for r in range(64):
            sa[r + 4, here, 0:128] = x_ref[r, here, :]
            sa[r + 4, here, 128:256] = side_tile(fe, fw, r, lane)
        for d in range(4):
            one = one_ref[d, here, :]
            two = two_ref[d, here, :]
            sa[d, here, 0:128] = jnp.where(even, two, one)
            sa[68 + d, here, 0:128] = jnp.where(even, one, two)
            one = pltpu.roll(one_ref[4, here, :], 124 - 8 * d, axis=1)
            two = pltpu.roll(two_ref[4, here, :], 124 - 8 * d, axis=1)
            sa[d, here, 128:256] = jnp.where(even, two, one)
            sa[68 + d, here, 128:256] = jnp.where(even, one, two)
        return 0

    lax.fori_loop(0, DEEP // 8, fill, 0)

    rows, cols = sa.shape[0], sa.shape[2]
    col = lax.broadcasted_iota(jnp.int32, (rows, cols), 1)
    live = (col < 132) | (col >= 252)
    sea = jnp.where(live, sa[:, levels + 2, :], 0.0)
    east = jnp.where(live, sa[:, levels, :], 0.0) * sea
    north = jnp.where(live, sa[:, levels + 1, :], 0.0) * sea
    a_e = east * pltpu.roll(sea, cols - 1, axis=1)
    a_w = east * pltpu.roll(sea, 1, axis=1)
    a_n = north * pltpu.roll(sea, rows - 1, axis=0)
    a_s = north * pltpu.roll(sea, 1, axis=0)
    coef[0] = 1.0 - ((a_e + a_w) + (a_n + a_s))
    coef[1] = a_e
    coef[2] = a_w
    coef[3] = a_n
    coef[4] = a_s

    def step(src, lo, hi, put):
        def body(r, _):
            c = [coef[i, pl.ds(r, 1), :] for i in range(5)]
            for g in range(DEEP // 8):
                here = slice(8 * g, 8 * g + 8)
                s = src[r, here, :]
                put(
                    r,
                    g,
                    c[0] * s
                    + (c[1] * pltpu.roll(s, cols - 1, axis=1) + c[2] * pltpu.roll(s, 1, axis=1))
                    + (c[3] * src[r + 1, here, :] + c[4] * src[r - 1, here, :]),
                )
            return 0

        lax.fori_loop(lo, hi, body, 0, unroll=UNROLL_DIFFUSE)

    def keep(dst):
        def put(r, g, v):
            dst[r, 8 * g : 8 * g + 8, :] = v

        return put

    def finish(r, g, v):
        n = min(8, levels - 8 * g)
        at = pl.ds(8 * g * 64 + r - 4, n, stride=64)
        out_ref[at, :] = es_ref[at, :] * v[0:n, 0:128]

    step(sa, 1, 71, keep(sb))
    step(sb, 2, 70, keep(sa))
    step(sa, 3, 69, keep(sb))
    step(sb, 4, 68, finish)


def vmem():
    return pl.BlockSpec(memory_space=pltpu.VMEM)


def smem():
    return pl.BlockSpec(memory_space=pltpu.SMEM)


def params():
    return pltpu.CompilerParams(vmem_limit_bytes=VMEM_LIMIT)


def perm_of(n_lat, n_lon, rule):
    pairs = []
    for a in range(n_lat):
        for b in range(n_lon):
            to = rule(a, b)
            if to is not None:
                pairs.append((a * n_lon + b, to[0] * n_lon + to[1] % n_lon))
    return pairs


def assemble_call(info, state, from_west, from_east):
    rows = jax.ShapeDtypeStruct((5, DEEP, 128), F32)
    return pl.pallas_call(
        assemble,
        grid=(1,),
        out_shape=(rows, rows),
        in_specs=[
            smem(),
            pl.BlockSpec((4, DEEP, 128), lambda i: (0, 0, 0)),
            pl.BlockSpec((4, DEEP, 128), lambda i: (15, 0, 0)),
            vmem(),
            vmem(),
        ],
        out_specs=(vmem(), vmem()),
        compiler_params=params(),
        name="assemble",
    )(info, state, state, from_west, from_east)


def diffuse_call(info, state, from_west, from_east, one, two, es):
    levels, ny, nx = es.shape
    out = pl.pallas_call(
        diffuse,
        out_shape=jax.ShapeDtypeStruct((levels * ny, nx), F32),
        in_specs=[smem()] + [vmem()] * 6,
        out_specs=vmem(),
        scratch_shapes=[
            pltpu.VMEM((ny + 8, DEEP, 2 * nx), F32),
            pltpu.VMEM((ny + 8, DEEP, 2 * nx), F32),
            pltpu.VMEM((5, ny + 8, 2 * nx), F32),
        ],
        compiler_params=params(),
        cost_estimate=pl.CostEstimate(flops=20 * STEPS * levels * ny * nx, bytes_accessed=60000000, transcendentals=0),
        name="diffuse",
    )(info, state, from_west, from_east, one, two, es.reshape(levels * ny, nx))
    return out.reshape(levels, ny, nx)


def shards(
    background,
    error_scale,
    east_rate,
    north_rate,
    sea_mask,
    partner,
    obs_weight,
    obs_value,
    obs_error,
    obs_column,
    obs_count,
):
    levels = background.shape[0] * background.shape[1]
    ny = background.shape[2]
    nx = background.shape[3]
    capacity = obs_weight.shape[3]
    owners = obs_weight.shape[1]
    bg = background.reshape(levels, ny, nx)
    es = error_scale.reshape(levels, ny, nx)
    packed, bgm, info = pack_call(
        partner, obs_count, jnp.swapaxes(obs_weight[0], 0, 1), obs_value[0], obs_error[0], obs_column[0], bg
    )
    turn = info[3]
    packed, bgm, info, turn = lax.optimization_barrier((packed, bgm, info, turn))
    received = lax.all_to_all(packed, ("lat", "lon"), split_axis=0, concat_axis=0, tiled=True)
    state, to_east, to_west, cost = observe_call(received, bgm, east_rate, north_rate, sea_mask, es)
    state = state.reshape(ny, DEEP, nx)

    n_lat = lax.axis_size("lat")
    n_lon = lax.axis_size("lon")
    from_west = lax.ppermute(to_east, "lon", [(i, (i + 1) % n_lon) for i in range(n_lon)])
    from_east = lax.ppermute(to_west, "lon", [((i + 1) % n_lon, i) for i in range(n_lon)])
    one, two = assemble_call(info, state, from_west, from_east)

    def branch(q):
        def rule(a, b):
            if a == n_lat - 1:
                return (a, q - b)
            if a == 0:
                return None
            return (((a + 1) ^ 1) - 1, b)

        def run(one, two, cost, info, state, from_west, from_east, es):
            got_one = lax.ppermute(one, ("lat", "lon"), perm_of(n_lat, n_lon, lambda a, b: (a ^ 1, b)))
            got_two = lax.ppermute(two, ("lat", "lon"), perm_of(n_lat, n_lon, rule))
            shares = lax.all_to_all(cost, ("lat", "lon"), split_axis=0, concat_axis=0, tiled=True)
            grown = diffuse_call(info, state, from_west, from_east, got_one, got_two, es)
            grown, shares = lax.optimization_barrier((grown, shares))
            return grown, jnp.sum(shares[:, 0, 0]) / (owners * owners * capacity)

        return run

    increment, cost_share = lax.switch(
        turn, [branch(q) for q in range(n_lon)], one, two, cost, info, state, from_west, from_east, es
    )
    return (increment.reshape(background.shape), cost_share)


def solution(mesh):
    in_specs = (
        P(None, None, "lat", "lon"),
        P(None, None, "lat", "lon"),
        P("lat", "lon"),
        P("lat", "lon"),
        P("lat", "lon"),
        P(),
        P(("lat", "lon"), None, None, None),
        P(("lat", "lon"), None, None),
        P(("lat", "lon"), None, None),
        P(("lat", "lon"), None, None),
        P(("lat", "lon"), None),
    )
    out_specs = (P(None, None, "lat", "lon"), P())
    return jax.shard_map(shards, mesh=mesh, in_specs=in_specs, out_specs=out_specs, check_vma=False)
```

```python
import jax
import jax.numpy as jnp
from jax import lax
from jax.experimental import pallas as pl
from jax.experimental.pallas import tpu as pltpu
from jax.sharding import PartitionSpec as P

STEPS = 4
HALO = 4
HUBER_EDGE = 1.5
F32 = jnp.float32
BF16 = jnp.bfloat16
WIDE = 2048
DEEP = 56
UNROLL_DIFFUSE = 7
VMEM_LIMIT = 56 * 1024 * 1024


def pack(
    partner_ref,
    count_ref,
    w_ref,
    value_ref,
    error_ref,
    cell_ref,
    bg_ref,
    out_ref,
    bgm_ref,
    info_ref,
    order_ref,
    counts_ref,
):
    levels, some, n = w_ref.shape
    owners = order_ref.shape[0]
    lane8 = lax.broadcasted_iota(jnp.int32, (8, n), 1)

    @pl.when(pl.program_id(0) == 0)
    def _():
        counts = jnp.transpose(jnp.broadcast_to(count_ref[...].astype(F32), (owners, n)))
        lane = lax.broadcasted_iota(jnp.int32, (owners, n), 1)
        cell = cell_ref[...]
        row = cell >> 7
        key = (((row >> 3) & 3) << 11) | ((row >> 5) << 10) | ((row & 7) << 7) | (cell & 127)
        counts_ref[...] = counts.astype(jnp.int32)
        filled = lane.astype(F32) < counts
        spread = (lane.astype(F32) - counts + 0.5) * (8192.0 / jnp.maximum(n - counts, 1.0))
        key = jnp.where(filled, key, jnp.clip(spread, 0.0, 8191.0).astype(jnp.int32))
        x = (key * n + lane).astype(F32)
        size = 2
        while size <= n:
            step = size // 2
            while step >= 1:
                first = (lane & step) == 0
                other = jnp.where(first, pltpu.roll(x, n - step, axis=1), pltpu.roll(x, step, axis=1))
                least = first == ((lane & size) == 0)
                x = jnp.where(least, jnp.minimum(x, other), jnp.maximum(x, other))
                step //= 2
            size *= 2
        order_ref[...] = x.astype(jnp.int32) & (n - 1)

    span = n * lax.axis_size("lon")
    moved = (partner_ref[0] + (span - 3)) % span
    lat_at = lax.axis_index("lat")
    info_ref[0] = moved % n
    info_ref[1] = 1 - lat_at % 2
    info_ref[2] = (lat_at == lax.axis_size("lat") - 1).astype(jnp.int32)
    info_ref[3] = moved // n

    for p in range(2):
        for k in range(0, levels, 2):
            x = jnp.concatenate([bg_ref[k, p, 0], bg_ref[k + 1, p, 0]], axis=0)
            hi = x.astype(BF16)
            at = p * 8 * levels + 8 * k
            bgm_ref[at : at + 16, 0:128] = hi
            bgm_ref[at : at + 16, 128:256] = (x - hi.astype(F32)).astype(BF16)

    for o in range(0, some, 8):
        at = pl.ds(pl.multiple_of(pl.program_id(0) * some + o, 8), 8)
        order = order_ref[at, :]
        valid = order < counts_ref[at, :]

        def put(k, v):
            out_ref[pl.ds(o * 56 + k, 8, stride=56), :] = v

        for k in range(levels):
            put(k, jnp.take_along_axis(w_ref[k, o : o + 8, :], order, axis=1))
        put(levels, jnp.take_along_axis(value_ref[at, :], order, axis=1))
        error = jnp.take_along_axis(error_ref[at, :], order, axis=1)
        put(levels + 1, jnp.where(valid, 1.0 / error, 0.0))
        put(levels + 2, jnp.take_along_axis(cell_ref[at, :], order, axis=1).astype(F32))
        for k in range(levels + 3, 56):
            put(k, jnp.zeros((8, n), F32))


def pack_call(partner, count, weight, value, error, column, bg):
    levels, owners, n = weight.shape
    ny, nx = bg.shape[1], bg.shape[2]
    steps = 4
    some = owners // steps
    whole = lambda i: (0, 0)
    return pl.pallas_call(
        pack,
        grid=(steps,),
        out_shape=(
            jax.ShapeDtypeStruct((owners * DEEP, n), F32),
            jax.ShapeDtypeStruct((levels * ny, 2 * nx), BF16),
            jax.ShapeDtypeStruct((4,), jnp.int32),
        ),
        in_specs=[
            smem(),
            pl.BlockSpec((1, owners), whole),
            pl.BlockSpec((levels, some, n), lambda i: (0, i, 0)),
            pl.BlockSpec((owners, n), whole),
            pl.BlockSpec((owners, n), whole),
            pl.BlockSpec((owners, n), whole),
            pl.BlockSpec((levels, 2, 1, 8, nx), lambda i: (0, 0, i, 0, 0)),
        ],
        out_specs=(
            pl.BlockSpec((some * DEEP, n), lambda i: (i, 0)),
            pl.BlockSpec((levels * ny // steps, 2 * nx), lambda i: (i, 0)),
            smem(),
        ),
        scratch_shapes=[pltpu.VMEM((owners, n), jnp.int32), pltpu.VMEM((owners, n), jnp.int32)],
        compiler_params=params(),
        name="pack",
    )(partner, count, weight, value, error, column, bg.reshape(levels, 2, 4, 8, nx))


def observe(rec_ref, bgm_ref, east_ref, north_ref, sea_ref, es_ref, state_ref, to_east_ref, to_west_ref, total_ref, tiles, force, whi, wlo, amat, cost_ref):
    levels = es_ref.shape[0]
    sources = rec_ref.shape[0] // 56
    rows_in = 8 * levels
    wide = whi.shape[1]
    total = tiles.shape[2]

    force[...] = jnp.zeros_like(force)
    cost_ref[...] = jnp.zeros_like(cost_ref)

    def regroup(eight, _):
        lane = lax.broadcasted_iota(jnp.int32, (8, 128), 1)
        for r in range(0, 56, 8):
            xs = [rec_ref[pl.ds(pl.multiple_of((eight * 8 + i) * 56 + r, 8), 8), :] for i in range(8)]
            for d in (1, 2, 4):
                keep = (lane // (16 * d)) % 2 == 0
                new = list(xs)
                for i in range(8):
                    if i & d == 0:
                        lo, hi = xs[i], xs[i + d]
                        new[i] = jnp.where(keep, lo, pltpu.roll(hi, 16 * d, axis=1))
                        new[i + d] = jnp.where(keep, pltpu.roll(lo, 128 - 16 * d, axis=1), hi)
                xs = new
            for i in range(8):
                tiles[i, r : r + 8, pl.ds(pl.multiple_of(eight * 128, 128), 128)] = xs[i]
        return 0

    lax.fori_loop(0, sources // 8, regroup, 0)

    iota8 = lax.broadcasted_iota(jnp.int32, (8, wide), 0)

    def tile(t, _):
        q = t // (total // wide)
        at_r = pl.ds(pl.multiple_of((t % (total // wide)) * wide, wide), wide)
        value = tiles[q, levels : levels + 1, at_r]
        inverse = tiles[q, levels + 1 : levels + 2, at_r]
        cell = tiles[q, levels + 2 : levels + 3, at_r].astype(jnp.int32)
        row = cell >> 7
        col = cell & 127
        part = row >> 5
        block = (row >> 3) & 3
        group = 2 * block + part
        valid = inverse > 0.0
        gmin = jnp.min(jnp.where(valid, group, 8))
        gmax = jnp.max(jnp.where(valid, group, -1))
        rmask = iota8 == (row & 7)
        iota128 = lax.broadcasted_iota(jnp.int32, (128, wide), 0)
        pick = jnp.where(iota128 == col, 1.0, 0.0)
        partf = part.astype(F32)
        pickb = pick.astype(BF16)
        pick2 = jnp.concatenate([pickb, pickb], axis=0)

        def sample(g, acc):
            s = jnp.dot(
                bgm_ref[pl.ds(pl.multiple_of(g * rows_in, 16), rows_in), :],
                pick2,
                preferred_element_type=F32,
            )
            parts = [None] * 4
            for k in range(levels):
                x = tiles[q, k : k + 1, at_r] * s[8 * k : 8 * k + 8, :]
                parts[k % 4] = x if parts[k % 4] is None else parts[k % 4] + x
            total_g = (parts[0] + parts[1]) + (parts[2] + parts[3])
            return acc + jnp.where(group == g, total_g, 0.0)

        acc = lax.fori_loop(gmin, gmax + 1, sample, jnp.zeros((8, wide), F32))
        equiv = jnp.sum(jnp.where(rmask, acc, 0.0), axis=0, keepdims=True)
        scaled = (value - equiv) * inverse
        magnitude = jnp.abs(scaled)
        cost_ref[...] += jnp.where(
            magnitude <= HUBER_EDGE,
            0.5 * scaled * scaled,
            HUBER_EDGE * magnitude - 0.5 * HUBER_EDGE * HUBER_EDGE,
        )
        response = HUBER_EDGE / jnp.maximum(magnitude, HUBER_EDGE) * scaled * inverse
        wr = tiles[q, 0:levels, at_r] * response
        hi = wr.astype(BF16).astype(F32)
        whi[0:levels, :] = hi
        wlo[0:levels, :] = wr - hi
        low = pick * partf
        place = jnp.concatenate([(pick - low).astype(BF16), low.astype(BF16)], axis=0)
        place2 = jnp.concatenate([place, place], axis=1)

        def spread(b, _):
            m = jnp.where(rmask & (block == b), 1.0, 0.0)
            for k in range(0, levels, 2):
                for half, src in ((0, whi), (wide, wlo)):
                    x = jnp.concatenate([m * src[k : k + 1, :], m * src[k + 1 : k + 2, :]], axis=0)
                    amat[8 * k : 8 * k + 16, half : half + wide] = x.astype(BF16)
            at = pl.ds(pl.multiple_of(b * rows_in, 8), rows_in)
            force[at, :] += lax.dot_general(
                amat[...], place2, (((1,), (1,)), ((), ())), preferred_element_type=F32
            )
            return 0

        lax.fori_loop(gmin >> 1, (gmax >> 1) + 1, spread, 0)
        return 0

    lax.fori_loop(0, 8 * (total // wide), tile, 0)

    total_ref[...] = jnp.broadcast_to(jnp.sum(cost_ref[...], axis=1, keepdims=True)[None], total_ref.shape)

    for r0 in range(0, 64, 8):
        b, part = (r0 // 8) % 4, r0 // 32
        sea = sea_ref[r0 : r0 + 8, :].astype(F32)

        def level_rows(k):
            return pl.ds(r0 * DEEP + k, 8, stride=DEEP)

        state_ref[level_rows(levels), :] = east_ref[r0 : r0 + 8, :]
        state_ref[level_rows(levels + 1), :] = north_ref[r0 : r0 + 8, :]
        state_ref[level_rows(levels + 2), :] = sea
        for k in range(levels + 3, DEEP):
            state_ref[level_rows(k), :] = jnp.zeros((8, 128), F32)
        for k in range(levels):
            f = force[b * rows_in + 8 * k : b * rows_in + 8 * k + 8, 128 * part : 128 * part + 128]
            state_ref[level_rows(k), :] = sea * es_ref[k, r0 : r0 + 8, :] * f

    lane = lax.broadcasted_iota(jnp.int32, (8, 128), 1)

    def messages(g, _):
        def row(r):
            return state_ref[pl.ds(pl.multiple_of(r * DEEP + 8 * g, 8), 8), :]

        here = pl.ds(pl.multiple_of(8 * g, 8), 8)
        for half in range(2):
            last = jnp.zeros((8, 128), F32)
            first = jnp.zeros((8, 128), F32)
            for i in range(32):
                x = row(32 * half + i)
                mine = (lane >> 2) == i
                last = jnp.where(mine, pltpu.roll(x, (4 * i + 4) % 128, axis=1), last)
                first = jnp.where(mine, pltpu.roll(x, 4 * i, axis=1), first)
            to_east_ref[here, 128 * half : 128 * half + 128] = last
            to_west_ref[here, 128 * half : 128 * half + 128] = first
        more = jnp.zeros((8, 128), F32)
        for d in range(4):
            x = row(60 + d)
            to_east_ref[here, 256 + 128 * d : 384 + 128 * d] = x
            more = jnp.where((lane >> 2) == d, pltpu.roll(x, (4 * d - 4) % 128, axis=1), more)
        to_west_ref[here, 256:384] = more
        return 0

    lax.fori_loop(0, DEEP // 8, messages, 0)


def observe_call(received, bgm, east_rate, north_rate, sea_mask, es, wide=WIDE):
    levels, ny, nx = es.shape
    owners = received.shape[0] // 56
    return pl.pallas_call(
        observe,
        out_shape=(
            jax.ShapeDtypeStruct((ny * DEEP, nx), F32),
            jax.ShapeDtypeStruct((DEEP, 768), F32),
            jax.ShapeDtypeStruct((DEEP, 384), F32),
            jax.ShapeDtypeStruct((owners, 1, 128), F32),
        ),
        in_specs=[vmem()] * 6,
        out_specs=(vmem(),) * 4,
        scratch_shapes=[
            pltpu.VMEM((8, 56, 16 * owners), F32),
            pltpu.VMEM((32 * levels, 256), F32),
            pltpu.VMEM((56, wide), F32),
            pltpu.VMEM((56, wide), F32),
            pltpu.VMEM((8 * levels, 2 * wide), BF16),
            pltpu.VMEM((1, wide), F32),
        ],
        compiler_params=params(),
        name="observe",
    )(received, bgm, east_rate, north_rate, sea_mask, es)


def side_tile(fe, fw, r, lane):
    half, i = r // 32, r % 32
    e = pltpu.roll(fe[128 * half], (128 - 4 * i) % 128, axis=1)
    w = pltpu.roll(fw[128 * half], (124 - 4 * i) % 128, axis=1)
    return jnp.where(lane < 64, e, w)


def assemble(info_ref, bot_ref, top_ref, fw_ref, fe_ref, one_ref, two_ref):
    shift = info_ref[0]
    even = info_ref[1] == 1
    fold = info_ref[2] == 1
    lane = lax.broadcasted_iota(jnp.int32, (8, 128), 1)
    rel_a = shift + 3 - lane
    rel_b = jnp.where(lane < 64, shift + 3 - 128 - lane, shift + 3 + 128 - lane)

    def mirror(west, own, east, rel):
        idx = rel & 127
        w = jnp.take_along_axis(west, idx, axis=1)
        o = jnp.take_along_axis(own, idx, axis=1)
        e = jnp.take_along_axis(east, idx, axis=1)
        return jnp.where(rel < 0, w, jnp.where(rel < 128, o, e))

    def body(g, _):
        here = pl.ds(pl.multiple_of(8 * g, 8), 8)
        fe = {c: fe_ref[here, c : c + 128] for c in (0, 128, 256)}
        fw = {c: fw_ref[here, c : c + 128] for c in range(0, 768, 128)}
        top = [top_ref[d, here, :] for d in range(4)]
        top_side = [side_tile(fe, fw, 60 + d, lane) for d in range(4)]
        sides = [jnp.zeros((8, 128), F32) for _ in range(3)]
        for d in range(4):
            u = 3 - d
            east = jnp.where(lane < 4, top_side[u], pltpu.roll(fe[256], (4 - 4 * u) % 128, axis=1))
            fold_a = mirror(fw[256 + 128 * u], top[u], east, rel_a)
            fold_b = mirror(fw[256 + 128 * u], top[u], east, rel_b)
            bot = bot_ref[d, here, :]
            one_ref[d, here, :] = jnp.where(even, top[d], bot)
            two_ref[d, here, :] = jnp.where(even, bot, jnp.where(fold, fold_a, top[d]))
            for n, x in enumerate((top_side[d], side_tile(fe, fw, d, lane), fold_b)):
                sides[n] = jnp.where((lane >> 3) == d, pltpu.roll(x, 8 * d + 4, axis=1), sides[n])
        one_ref[4, here, :] = jnp.where(even, sides[0], sides[1])
        two_ref[4, here, :] = jnp.where(even, sides[1], jnp.where(fold, sides[2], sides[0]))
        return 0

    lax.fori_loop(0, DEEP // 8, body, 0)


def diffuse(info_ref, x_ref, fw_ref, fe_ref, one_ref, two_ref, es_ref, out_ref, sa, sb, coef):
    levels = es_ref.shape[0] // 64
    even = info_ref[1] == 1
    lane = lax.broadcasted_iota(jnp.int32, (8, 128), 1)

    def fill(g, _):
        here = pl.ds(pl.multiple_of(8 * g, 8), 8)
        fe = {c: fe_ref[here, c : c + 128] for c in (0, 128)}
        fw = {c: fw_ref[here, c : c + 128] for c in (0, 128)}
        for r in range(64):
            sa[r + 4, here, 0:128] = x_ref[r, here, :]
            sa[r + 4, here, 128:256] = side_tile(fe, fw, r, lane)
        for d in range(4):
            one = one_ref[d, here, :]
            two = two_ref[d, here, :]
            sa[d, here, 0:128] = jnp.where(even, two, one)
            sa[68 + d, here, 0:128] = jnp.where(even, one, two)
            one = pltpu.roll(one_ref[4, here, :], 124 - 8 * d, axis=1)
            two = pltpu.roll(two_ref[4, here, :], 124 - 8 * d, axis=1)
            sa[d, here, 128:256] = jnp.where(even, two, one)
            sa[68 + d, here, 128:256] = jnp.where(even, one, two)
        return 0

    lax.fori_loop(0, DEEP // 8, fill, 0)

    rows, cols = sa.shape[0], sa.shape[2]
    col = lax.broadcasted_iota(jnp.int32, (rows, cols), 1)
    live = (col < 132) | (col >= 252)
    sea = jnp.where(live, sa[:, levels + 2, :], 0.0)
    east = jnp.where(live, sa[:, levels, :], 0.0) * sea
    north = jnp.where(live, sa[:, levels + 1, :], 0.0) * sea
    a_e = east * pltpu.roll(sea, cols - 1, axis=1)
    a_w = east * pltpu.roll(sea, 1, axis=1)
    a_n = north * pltpu.roll(sea, rows - 1, axis=0)
    a_s = north * pltpu.roll(sea, 1, axis=0)
    coef[0] = 1.0 - ((a_e + a_w) + (a_n + a_s))
    coef[1] = a_e
    coef[2] = a_w
    coef[3] = a_n
    coef[4] = a_s

    def step(src, lo, hi, put):
        def body(r, _):
            c = [coef[i, pl.ds(r, 1), :] for i in range(5)]
            for g in range(DEEP // 8):
                here = slice(8 * g, 8 * g + 8)
                s = src[r, here, :]
                put(
                    r,
                    g,
                    c[0] * s
                    + (c[1] * pltpu.roll(s, cols - 1, axis=1) + c[2] * pltpu.roll(s, 1, axis=1))
                    + (c[3] * src[r + 1, here, :] + c[4] * src[r - 1, here, :]),
                )
            return 0

        lax.fori_loop(lo, hi, body, 0, unroll=UNROLL_DIFFUSE)

    def keep(dst):
        def put(r, g, v):
            dst[r, 8 * g : 8 * g + 8, :] = v

        return put

    def finish(r, g, v):
        n = min(8, levels - 8 * g)
        at = pl.ds(8 * g * 64 + r - 4, n, stride=64)
        out_ref[at, :] = es_ref[at, :] * v[0:n, 0:128]

    step(sa, 1, 71, keep(sb))
    step(sb, 2, 70, keep(sa))
    step(sa, 3, 69, keep(sb))
    step(sb, 4, 68, finish)


def vmem():
    return pl.BlockSpec(memory_space=pltpu.VMEM)


def smem():
    return pl.BlockSpec(memory_space=pltpu.SMEM)


def params():
    return pltpu.CompilerParams(vmem_limit_bytes=VMEM_LIMIT)


def perm_of(n_lat, n_lon, rule):
    pairs = []
    for a in range(n_lat):
        for b in range(n_lon):
            to = rule(a, b)
            if to is not None:
                pairs.append((a * n_lon + b, to[0] * n_lon + to[1] % n_lon))
    return pairs


def assemble_call(info, state, from_west, from_east):
    rows = jax.ShapeDtypeStruct((5, DEEP, 128), F32)
    return pl.pallas_call(
        assemble,
        grid=(1,),
        out_shape=(rows, rows),
        in_specs=[
            smem(),
            pl.BlockSpec((4, DEEP, 128), lambda i: (0, 0, 0)),
            pl.BlockSpec((4, DEEP, 128), lambda i: (15, 0, 0)),
            vmem(),
            vmem(),
        ],
        out_specs=(vmem(), vmem()),
        compiler_params=params(),
        name="assemble",
    )(info, state, state, from_west, from_east)


def diffuse_call(info, state, from_west, from_east, one, two, es):
    levels, ny, nx = es.shape
    out = pl.pallas_call(
        diffuse,
        out_shape=jax.ShapeDtypeStruct((levels * ny, nx), F32),
        in_specs=[smem()] + [vmem()] * 6,
        out_specs=vmem(),
        scratch_shapes=[
            pltpu.VMEM((ny + 8, DEEP, 2 * nx), F32),
            pltpu.VMEM((ny + 8, DEEP, 2 * nx), F32),
            pltpu.VMEM((5, ny + 8, 2 * nx), F32),
        ],
        compiler_params=params(),
        cost_estimate=pl.CostEstimate(flops=20 * STEPS * levels * ny * nx, bytes_accessed=60000000, transcendentals=0),
        name="diffuse",
    )(info, state, from_west, from_east, one, two, es.reshape(levels * ny, nx))
    return out.reshape(levels, ny, nx)


def shards(
    background,
    error_scale,
    east_rate,
    north_rate,
    sea_mask,
    partner,
    obs_weight,
    obs_value,
    obs_error,
    obs_column,
    obs_count,
):
    levels = background.shape[0] * background.shape[1]
    ny = background.shape[2]
    nx = background.shape[3]
    capacity = obs_weight.shape[3]
    owners = obs_weight.shape[1]
    bg = background.reshape(levels, ny, nx)
    es = error_scale.reshape(levels, ny, nx)
    packed, bgm, info = pack_call(
        partner, obs_count, jnp.swapaxes(obs_weight[0], 0, 1), obs_value[0], obs_error[0], obs_column[0], bg
    )
    turn = info[3]
    packed, bgm, info, turn = lax.optimization_barrier((packed, bgm, info, turn))
    received = lax.all_to_all(packed, ("lat", "lon"), split_axis=0, concat_axis=0, tiled=True)
    state, to_east, to_west, cost = observe_call(received, bgm, east_rate, north_rate, sea_mask, es)
    state = state.reshape(ny, DEEP, nx)

    n_lat = lax.axis_size("lat")
    n_lon = lax.axis_size("lon")
    from_west = lax.ppermute(to_east, "lon", [(i, (i + 1) % n_lon) for i in range(n_lon)])
    from_east = lax.ppermute(to_west, "lon", [((i + 1) % n_lon, i) for i in range(n_lon)])
    one, two = assemble_call(info, state, from_west, from_east)

    def branch(q):
        def rule(a, b):
            if a == n_lat - 1:
                return (a, q - b)
            if a == 0:
                return None
            return (((a + 1) ^ 1) - 1, b)

        def run(one, two, cost):
            got_one = lax.ppermute(one, ("lat", "lon"), perm_of(n_lat, n_lon, lambda a, b: (a ^ 1, b)))
            got_two = lax.ppermute(two, ("lat", "lon"), perm_of(n_lat, n_lon, rule))
            shares = lax.all_to_all(cost, ("lat", "lon"), split_axis=0, concat_axis=0, tiled=True)
            return got_one, got_two, shares

        return run

    got_one, got_two, shares = lax.switch(turn, [branch(q) for q in range(n_lon)], one, two, cost)
    cost_share = jnp.sum(shares[:, 0, 0]) / (owners * owners * capacity)
    increment = diffuse_call(info, state, from_west, from_east, got_one, got_two, es)
    return (increment.reshape(background.shape), cost_share)


def solution(mesh):
    in_specs = (
        P(None, None, "lat", "lon"),
        P(None, None, "lat", "lon"),
        P("lat", "lon"),
        P("lat", "lon"),
        P("lat", "lon"),
        P(),
        P(("lat", "lon"), None, None, None),
        P(("lat", "lon"), None, None),
        P(("lat", "lon"), None, None),
        P(("lat", "lon"), None, None),
        P(("lat", "lon"), None),
    )
    out_specs = (P(None, None, "lat", "lon"), P())
    return jax.shard_map(shards, mesh=mesh, in_specs=in_specs, out_specs=out_specs, check_vma=False)
```

```python
import jax
import jax.numpy as jnp
from jax import lax
from jax.experimental import pallas as pl
from jax.experimental.pallas import tpu as pltpu
from jax.sharding import PartitionSpec as P

STEPS = 4
HALO = 4
HUBER_EDGE = 1.5
F32 = jnp.float32
BF16 = jnp.bfloat16
WIDE = 2048
DEEP = 56
UNROLL_DIFFUSE = 7
VMEM_LIMIT = 56 * 1024 * 1024


def pack(
    partner_ref,
    count_ref,
    w_ref,
    value_ref,
    error_ref,
    cell_ref,
    bg_ref,
    out_ref,
    bgm_ref,
    info_ref,
    order_ref,
    counts_ref,
):
    levels, some, n = w_ref.shape
    owners = order_ref.shape[0]
    lane8 = lax.broadcasted_iota(jnp.int32, (8, n), 1)

    @pl.when(pl.program_id(0) == 0)
    def _():
        counts = jnp.transpose(jnp.broadcast_to(count_ref[...].astype(F32), (owners, n)))
        lane = lax.broadcasted_iota(jnp.int32, (owners, n), 1)
        cell = cell_ref[...]
        row = cell >> 7
        key = (((row >> 3) & 3) << 11) | ((row >> 5) << 10) | ((row & 7) << 7) | (cell & 127)
        counts_ref[...] = counts.astype(jnp.int32)
        filled = lane.astype(F32) < counts
        spread = (lane.astype(F32) - counts + 0.5) * (8192.0 / jnp.maximum(n - counts, 1.0))
        key = jnp.where(filled, key, jnp.clip(spread, 0.0, 8191.0).astype(jnp.int32))
        x = (key * n + lane).astype(F32)
        size = 2
        while size <= n:
            step = size // 2
            while step >= 1:
                first = (lane & step) == 0
                other = jnp.where(first, pltpu.roll(x, n - step, axis=1), pltpu.roll(x, step, axis=1))
                least = first == ((lane & size) == 0)
                x = jnp.where(least, jnp.minimum(x, other), jnp.maximum(x, other))
                step //= 2
            size *= 2
        order_ref[...] = x.astype(jnp.int32) & (n - 1)

    span = n * lax.axis_size("lon")
    moved = (partner_ref[0] + (span - 3)) % span
    lat_at = lax.axis_index("lat")
    info_ref[0] = moved % n
    info_ref[1] = 1 - lat_at % 2
    info_ref[2] = (lat_at == lax.axis_size("lat") - 1).astype(jnp.int32)
    info_ref[3] = moved // n

    for p in range(2):
        for k in range(0, levels, 2):
            x = jnp.concatenate([bg_ref[k, p, 0], bg_ref[k + 1, p, 0]], axis=0)
            hi = x.astype(BF16)
            at = p * 8 * levels + 8 * k
            bgm_ref[at : at + 16, 0:128] = hi
            bgm_ref[at : at + 16, 128:256] = (x - hi.astype(F32)).astype(BF16)

    for o in range(0, some, 8):
        at = pl.ds(pl.multiple_of(pl.program_id(0) * some + o, 8), 8)
        order = order_ref[at, :]
        valid = order < counts_ref[at, :]

        def put(k, v):
            out_ref[pl.ds(o * 56 + k, 8, stride=56), :] = v

        for k in range(levels):
            put(k, jnp.take_along_axis(w_ref[k, o : o + 8, :], order, axis=1))
        put(levels, jnp.take_along_axis(value_ref[at, :], order, axis=1))
        error = jnp.take_along_axis(error_ref[at, :], order, axis=1)
        put(levels + 1, jnp.where(valid, 1.0 / error, 0.0))
        put(levels + 2, jnp.take_along_axis(cell_ref[at, :], order, axis=1).astype(F32))
        for k in range(levels + 3, 56):
            put(k, jnp.zeros((8, n), F32))


def pack_call(partner, count, weight, value, error, column, bg):
    levels, owners, n = weight.shape
    ny, nx = bg.shape[1], bg.shape[2]
    steps = 4
    some = owners // steps
    whole = lambda i: (0, 0)
    return pl.pallas_call(
        pack,
        grid=(steps,),
        out_shape=(
            jax.ShapeDtypeStruct((owners * DEEP, n), F32),
            jax.ShapeDtypeStruct((levels * ny, 2 * nx), BF16),
            jax.ShapeDtypeStruct((4,), jnp.int32),
        ),
        in_specs=[
            smem(),
            pl.BlockSpec((1, owners), whole),
            pl.BlockSpec((levels, some, n), lambda i: (0, i, 0)),
            pl.BlockSpec((owners, n), whole),
            pl.BlockSpec((owners, n), whole),
            pl.BlockSpec((owners, n), whole),
            pl.BlockSpec((levels, 2, 1, 8, nx), lambda i: (0, 0, i, 0, 0)),
        ],
        out_specs=(
            pl.BlockSpec((some * DEEP, n), lambda i: (i, 0)),
            pl.BlockSpec((levels * ny // steps, 2 * nx), lambda i: (i, 0)),
            smem(),
        ),
        scratch_shapes=[pltpu.VMEM((owners, n), jnp.int32), pltpu.VMEM((owners, n), jnp.int32)],
        compiler_params=params(),
        name="pack",
    )(partner, count, weight, value, error, column, bg.reshape(levels, 2, 4, 8, nx))


def observe(rec_ref, bgm_ref, east_ref, north_ref, sea_ref, es_ref, state_ref, to_east_ref, to_west_ref, total_ref, tiles, force, whi, wlo, amat, cost_ref):
    levels = es_ref.shape[0]
    sources = rec_ref.shape[0] // 56
    rows_in = 8 * levels
    wide = whi.shape[1]
    total = tiles.shape[2]

    force[...] = jnp.zeros_like(force)
    cost_ref[...] = jnp.zeros_like(cost_ref)

    def regroup(eight, _):
        lane = lax.broadcasted_iota(jnp.int32, (8, 128), 1)
        for r in range(0, 56, 8):
            xs = [rec_ref[pl.ds(pl.multiple_of((eight * 8 + i) * 56 + r, 8), 8), :] for i in range(8)]
            for d in (1, 2, 4):
                keep = (lane // (16 * d)) % 2 == 0
                new = list(xs)
                for i in range(8):
                    if i & d == 0:
                        lo, hi = xs[i], xs[i + d]
                        new[i] = jnp.where(keep, lo, pltpu.roll(hi, 16 * d, axis=1))
                        new[i + d] = jnp.where(keep, pltpu.roll(lo, 128 - 16 * d, axis=1), hi)
                xs = new
            for i in range(8):
                tiles[i, r : r + 8, pl.ds(pl.multiple_of(eight * 128, 128), 128)] = xs[i]
        return 0

    lax.fori_loop(0, sources // 8, regroup, 0)

    iota8 = lax.broadcasted_iota(jnp.int32, (8, wide), 0)

    def tile(t, _):
        q = t // (total // wide)
        at_r = pl.ds(pl.multiple_of((t % (total // wide)) * wide, wide), wide)
        value = tiles[q, levels : levels + 1, at_r]
        inverse = tiles[q, levels + 1 : levels + 2, at_r]
        cell = tiles[q, levels + 2 : levels + 3, at_r].astype(jnp.int32)
        row = cell >> 7
        col = cell & 127
        part = row >> 5
        block = (row >> 3) & 3
        group = 2 * block + part
        valid = inverse > 0.0
        gmin = jnp.min(jnp.where(valid, group, 8))
        gmax = jnp.max(jnp.where(valid, group, -1))
        rmask = iota8 == (row & 7)
        iota128 = lax.broadcasted_iota(jnp.int32, (128, wide), 0)
        pick = jnp.where(iota128 == col, 1.0, 0.0)
        partf = part.astype(F32)
        pickb = pick.astype(BF16)
        pick2 = jnp.concatenate([pickb, pickb], axis=0)

        def sample(g, acc):
            s = jnp.dot(
                bgm_ref[pl.ds(pl.multiple_of(g * rows_in, 16), rows_in), :],
                pick2,
                preferred_element_type=F32,
            )
            parts = [None] * 4
            for k in range(levels):
                x = tiles[q, k : k + 1, at_r] * s[8 * k : 8 * k + 8, :]
                parts[k % 4] = x if parts[k % 4] is None else parts[k % 4] + x
            total_g = (parts[0] + parts[1]) + (parts[2] + parts[3])
            return acc + jnp.where(group == g, total_g, 0.0)

        acc = lax.fori_loop(gmin, gmax + 1, sample, jnp.zeros((8, wide), F32))
        equiv = jnp.sum(jnp.where(rmask, acc, 0.0), axis=0, keepdims=True)
        scaled = (value - equiv) * inverse
        magnitude = jnp.abs(scaled)
        cost_ref[...] += jnp.where(
            magnitude <= HUBER_EDGE,
            0.5 * scaled * scaled,
            HUBER_EDGE * magnitude - 0.5 * HUBER_EDGE * HUBER_EDGE,
        )
        response = HUBER_EDGE / jnp.maximum(magnitude, HUBER_EDGE) * scaled * inverse
        wr = tiles[q, 0:levels, at_r] * response
        hi = wr.astype(BF16).astype(F32)
        whi[0:levels, :] = hi
        wlo[0:levels, :] = wr - hi
        low = pick * partf
        place = jnp.concatenate([(pick - low).astype(BF16), low.astype(BF16)], axis=0)
        place2 = jnp.concatenate([place, place], axis=1)

        def spread(b, _):
            m = jnp.where(rmask & (block == b), 1.0, 0.0)
            for k in range(0, levels, 2):
                for half, src in ((0, whi), (wide, wlo)):
                    x = jnp.concatenate([m * src[k : k + 1, :], m * src[k + 1 : k + 2, :]], axis=0)
                    amat[8 * k : 8 * k + 16, half : half + wide] = x.astype(BF16)
            at = pl.ds(pl.multiple_of(b * rows_in, 8), rows_in)
            force[at, :] += lax.dot_general(
                amat[...], place2, (((1,), (1,)), ((), ())), preferred_element_type=F32
            )
            return 0

        lax.fori_loop(gmin >> 1, (gmax >> 1) + 1, spread, 0)
        return 0

    lax.fori_loop(0, 8 * (total // wide), tile, 0)

    total_ref[...] = jnp.broadcast_to(jnp.sum(cost_ref[...], axis=1, keepdims=True)[None], total_ref.shape)

    for r0 in range(0, 64, 8):
        b, part = (r0 // 8) % 4, r0 // 32
        sea = sea_ref[r0 : r0 + 8, :].astype(F32)

        def level_rows(k):
            return pl.ds(r0 * DEEP + k, 8, stride=DEEP)

        state_ref[level_rows(levels), :] = east_ref[r0 : r0 + 8, :]
        state_ref[level_rows(levels + 1), :] = north_ref[r0 : r0 + 8, :]
        state_ref[level_rows(levels + 2), :] = sea
        for k in range(levels + 3, DEEP):
            state_ref[level_rows(k), :] = jnp.zeros((8, 128), F32)
        for k in range(levels):
            f = force[b * rows_in + 8 * k : b * rows_in + 8 * k + 8, 128 * part : 128 * part + 128]
            state_ref[level_rows(k), :] = sea * es_ref[k, r0 : r0 + 8, :] * f

    lane = lax.broadcasted_iota(jnp.int32, (8, 128), 1)

    def messages(g, _):
        def row(r):
            return state_ref[pl.ds(pl.multiple_of(r * DEEP + 8 * g, 8), 8), :]

        here = pl.ds(pl.multiple_of(8 * g, 8), 8)
        for half in range(2):
            last = jnp.zeros((8, 128), F32)
            first = jnp.zeros((8, 128), F32)
            for i in range(32):
                x = row(32 * half + i)
                mine = (lane >> 2) == i
                last = jnp.where(mine, pltpu.roll(x, (4 * i + 4) % 128, axis=1), last)
                first = jnp.where(mine, pltpu.roll(x, 4 * i, axis=1), first)
            to_east_ref[here, 128 * half : 128 * half + 128] = last
            to_west_ref[here, 128 * half : 128 * half + 128] = first
        more = jnp.zeros((8, 128), F32)
        for d in range(4):
            x = row(60 + d)
            to_east_ref[here, 256 + 128 * d : 384 + 128 * d] = x
            more = jnp.where((lane >> 2) == d, pltpu.roll(x, (4 * d - 4) % 128, axis=1), more)
        to_west_ref[here, 256:384] = more
        return 0

    lax.fori_loop(0, DEEP // 8, messages, 0)


def observe_call(received, bgm, east_rate, north_rate, sea_mask, es, wide=WIDE):
    levels, ny, nx = es.shape
    owners = received.shape[0] // 56
    return pl.pallas_call(
        observe,
        out_shape=(
            jax.ShapeDtypeStruct((ny * DEEP, nx), F32),
            jax.ShapeDtypeStruct((DEEP, 768), F32),
            jax.ShapeDtypeStruct((DEEP, 384), F32),
            jax.ShapeDtypeStruct((owners, 1, 128), F32),
        ),
        in_specs=[vmem()] * 6,
        out_specs=(vmem(),) * 4,
        scratch_shapes=[
            pltpu.VMEM((8, 56, 16 * owners), F32),
            pltpu.VMEM((32 * levels, 256), F32),
            pltpu.VMEM((56, wide), F32),
            pltpu.VMEM((56, wide), F32),
            pltpu.VMEM((8 * levels, 2 * wide), BF16),
            pltpu.VMEM((1, wide), F32),
        ],
        compiler_params=params(),
        name="observe",
    )(received, bgm, east_rate, north_rate, sea_mask, es)


def side_tile(fe, fw, r, lane):
    half, i = r // 32, r % 32
    e = pltpu.roll(fe[128 * half], (128 - 4 * i) % 128, axis=1)
    w = pltpu.roll(fw[128 * half], (124 - 4 * i) % 128, axis=1)
    return jnp.where(lane < 64, e, w)


def assemble(info_ref, bot_ref, top_ref, fw_ref, fe_ref, one_ref, two_ref):
    shift = info_ref[0]
    even = info_ref[1] == 1
    fold = info_ref[2] == 1
    lane = lax.broadcasted_iota(jnp.int32, (8, 128), 1)
    rel_a = shift + 3 - lane
    rel_b = jnp.where(lane < 64, shift + 3 - 128 - lane, shift + 3 + 128 - lane)

    def mirror(west, own, east, rel):
        idx = rel & 127
        w = jnp.take_along_axis(west, idx, axis=1)
        o = jnp.take_along_axis(own, idx, axis=1)
        e = jnp.take_along_axis(east, idx, axis=1)
        return jnp.where(rel < 0, w, jnp.where(rel < 128, o, e))

    def body(g, _):
        here = pl.ds(pl.multiple_of(8 * g, 8), 8)
        fe = {c: fe_ref[here, c : c + 128] for c in (0, 128, 256)}
        fw = {c: fw_ref[here, c : c + 128] for c in range(0, 768, 128)}
        top = [top_ref[d, here, :] for d in range(4)]
        top_side = [side_tile(fe, fw, 60 + d, lane) for d in range(4)]
        sides = [jnp.zeros((8, 128), F32) for _ in range(3)]
        for d in range(4):
            u = 3 - d
            east = jnp.where(lane < 4, top_side[u], pltpu.roll(fe[256], (4 - 4 * u) % 128, axis=1))
            fold_a = mirror(fw[256 + 128 * u], top[u], east, rel_a)
            fold_b = mirror(fw[256 + 128 * u], top[u], east, rel_b)
            bot = bot_ref[d, here, :]
            one_ref[d, here, :] = jnp.where(even, top[d], bot)
            two_ref[d, here, :] = jnp.where(even, bot, jnp.where(fold, fold_a, top[d]))
            for n, x in enumerate((top_side[d], side_tile(fe, fw, d, lane), fold_b)):
                sides[n] = jnp.where((lane >> 3) == d, pltpu.roll(x, 8 * d + 4, axis=1), sides[n])
        one_ref[4, here, :] = jnp.where(even, sides[0], sides[1])
        two_ref[4, here, :] = jnp.where(even, sides[1], jnp.where(fold, sides[2], sides[0]))
        return 0

    lax.fori_loop(0, DEEP // 8, body, 0)


def diffuse(info_ref, x_ref, fw_ref, fe_ref, one_ref, two_ref, es_ref, out_ref, sa, sb, coef):
    levels = es_ref.shape[0] // 64
    even = info_ref[1] == 1
    lane = lax.broadcasted_iota(jnp.int32, (8, 128), 1)

    def fill(g, _):
        here = pl.ds(pl.multiple_of(8 * g, 8), 8)
        fe = {c: fe_ref[here, c : c + 128] for c in (0, 128)}
        fw = {c: fw_ref[here, c : c + 128] for c in (0, 128)}
        for r in range(64):
            sa[r + 4, here, 0:128] = x_ref[r, here, :]
            sa[r + 4, here, 128:256] = side_tile(fe, fw, r, lane)
        for d in range(4):
            one = one_ref[d, here, :]
            two = two_ref[d, here, :]
            sa[d, here, 0:128] = jnp.where(even, two, one)
            sa[68 + d, here, 0:128] = jnp.where(even, one, two)
            one = pltpu.roll(one_ref[4, here, :], 124 - 8 * d, axis=1)
            two = pltpu.roll(two_ref[4, here, :], 124 - 8 * d, axis=1)
            sa[d, here, 128:256] = jnp.where(even, two, one)
            sa[68 + d, here, 128:256] = jnp.where(even, one, two)
        return 0

    lax.fori_loop(0, DEEP // 8, fill, 0)

    rows, cols = sa.shape[0], sa.shape[2]
    col = lax.broadcasted_iota(jnp.int32, (rows, cols), 1)
    live = (col < 132) | (col >= 252)
    sea = jnp.where(live, sa[:, levels + 2, :], 0.0)
    east = jnp.where(live, sa[:, levels, :], 0.0) * sea
    north = jnp.where(live, sa[:, levels + 1, :], 0.0) * sea
    a_e = east * pltpu.roll(sea, cols - 1, axis=1)
    a_w = east * pltpu.roll(sea, 1, axis=1)
    a_n = north * pltpu.roll(sea, rows - 1, axis=0)
    a_s = north * pltpu.roll(sea, 1, axis=0)
    coef[0] = 1.0 - ((a_e + a_w) + (a_n + a_s))
    coef[1] = a_e
    coef[2] = a_w
    coef[3] = a_n
    coef[4] = a_s

    def step(src, lo, hi, put):
        def body(r, _):
            c = [coef[i, pl.ds(r, 1), :] for i in range(5)]
            for g in range(DEEP // 8):
                here = slice(8 * g, 8 * g + 8)
                s = src[r, here, :]
                put(
                    r,
                    g,
                    c[0] * s
                    + (c[1] * pltpu.roll(s, cols - 1, axis=1) + c[2] * pltpu.roll(s, 1, axis=1))
                    + (c[3] * src[r + 1, here, :] + c[4] * src[r - 1, here, :]),
                )
            return 0

        lax.fori_loop(lo, hi, body, 0, unroll=UNROLL_DIFFUSE)

    def keep(dst):
        def put(r, g, v):
            dst[r, 8 * g : 8 * g + 8, :] = v

        return put

    def finish(r, g, v):
        n = min(8, levels - 8 * g)
        at = pl.ds(8 * g * 64 + r - 4, n, stride=64)
        out_ref[at, :] = es_ref[at, :] * v[0:n, 0:128]

    step(sa, 1, 71, keep(sb))
    step(sb, 2, 70, keep(sa))
    step(sa, 3, 69, keep(sb))
    step(sb, 4, 68, finish)


def vmem():
    return pl.BlockSpec(memory_space=pltpu.VMEM)


def smem():
    return pl.BlockSpec(memory_space=pltpu.SMEM)


def params():
    return pltpu.CompilerParams(vmem_limit_bytes=VMEM_LIMIT)


def perm_of(n_lat, n_lon, rule):
    pairs = []
    for a in range(n_lat):
        for b in range(n_lon):
            to = rule(a, b)
            if to is not None:
                pairs.append((a * n_lon + b, to[0] * n_lon + to[1] % n_lon))
    return pairs


def assemble_call(info, state, from_west, from_east):
    rows = jax.ShapeDtypeStruct((5, DEEP, 128), F32)
    return pl.pallas_call(
        assemble,
        grid=(1,),
        out_shape=(rows, rows),
        in_specs=[
            smem(),
            pl.BlockSpec((4, DEEP, 128), lambda i: (0, 0, 0)),
            pl.BlockSpec((4, DEEP, 128), lambda i: (15, 0, 0)),
            vmem(),
            vmem(),
        ],
        out_specs=(vmem(), vmem()),
        compiler_params=params(),
        name="assemble",
    )(info, state, state, from_west, from_east)


def diffuse_call(info, state, from_west, from_east, one, two, es):
    levels, ny, nx = es.shape
    out = pl.pallas_call(
        diffuse,
        out_shape=jax.ShapeDtypeStruct((levels * ny, nx), F32),
        in_specs=[smem()] + [vmem()] * 6,
        out_specs=vmem(),
        scratch_shapes=[
            pltpu.VMEM((ny + 8, DEEP, 2 * nx), F32),
            pltpu.VMEM((ny + 8, DEEP, 2 * nx), F32),
            pltpu.VMEM((5, ny + 8, 2 * nx), F32),
        ],
        compiler_params=params(),
        cost_estimate=pl.CostEstimate(flops=20 * STEPS * levels * ny * nx, bytes_accessed=60000000, transcendentals=0),
        name="diffuse",
    )(info, state, from_west, from_east, one, two, es.reshape(levels * ny, nx))
    return out.reshape(levels, ny, nx)


def shards(
    background,
    error_scale,
    east_rate,
    north_rate,
    sea_mask,
    partner,
    obs_weight,
    obs_value,
    obs_error,
    obs_column,
    obs_count,
):
    levels = background.shape[0] * background.shape[1]
    ny = background.shape[2]
    nx = background.shape[3]
    capacity = obs_weight.shape[3]
    owners = obs_weight.shape[1]
    bg = background.reshape(levels, ny, nx)
    es = error_scale.reshape(levels, ny, nx)
    packed, bgm, info = pack_call(
        partner, obs_count, jnp.swapaxes(obs_weight[0], 0, 1), obs_value[0], obs_error[0], obs_column[0], bg
    )
    turn = info[3]
    packed, bgm, info, turn = lax.optimization_barrier((packed, bgm, info, turn))
    received = lax.all_to_all(packed, ("lat", "lon"), split_axis=0, concat_axis=0, tiled=True)
    state, to_east, to_west, cost = observe_call(received, bgm, east_rate, north_rate, sea_mask, es)
    state = state.reshape(ny, DEEP, nx)

    n_lat = lax.axis_size("lat")
    n_lon = lax.axis_size("lon")
    from_west = lax.ppermute(to_east, "lon", [(i, (i + 1) % n_lon) for i in range(n_lon)])
    from_east = lax.ppermute(to_west, "lon", [((i + 1) % n_lon, i) for i in range(n_lon)])
    one, two = assemble_call(info, state, from_west, from_east)

    shares = lax.all_to_all(cost, ("lat", "lon"), split_axis=0, concat_axis=0, tiled=True)

    def branch(q):
        def rule(a, b):
            if a == n_lat - 1:
                return (a, q - b)
            if a == 0:
                return None
            return (((a + 1) ^ 1) - 1, b)

        def run(one, two):
            got_one = lax.ppermute(one, ("lat", "lon"), perm_of(n_lat, n_lon, lambda a, b: (a ^ 1, b)))
            got_two = lax.ppermute(two, ("lat", "lon"), perm_of(n_lat, n_lon, rule))
            return got_one, got_two

        return run

    one, two, shares = lax.optimization_barrier((one, two, shares))
    got_one, got_two = lax.switch(turn, [branch(q) for q in range(n_lon)], one, two)
    cost_share = jnp.sum(shares[:, 0, 0]) / (owners * owners * capacity)
    increment = diffuse_call(info, state, from_west, from_east, got_one, got_two, es)
    return (increment.reshape(background.shape), cost_share)


def solution(mesh):
    in_specs = (
        P(None, None, "lat", "lon"),
        P(None, None, "lat", "lon"),
        P("lat", "lon"),
        P("lat", "lon"),
        P("lat", "lon"),
        P(),
        P(("lat", "lon"), None, None, None),
        P(("lat", "lon"), None, None),
        P(("lat", "lon"), None, None),
        P(("lat", "lon"), None, None),
        P(("lat", "lon"), None),
    )
    out_specs = (P(None, None, "lat", "lon"), P())
    return jax.shard_map(shards, mesh=mesh, in_specs=in_specs, out_specs=out_specs, check_vma=False)
```

```python
import jax
import jax.numpy as jnp
from jax import lax
from jax.experimental import pallas as pl
from jax.experimental.pallas import tpu as pltpu
from jax.sharding import PartitionSpec as P

STEPS = 4
HALO = 4
HUBER_EDGE = 1.5
F32 = jnp.float32
BF16 = jnp.bfloat16
WIDE = 2048
DEEP = 56
UNROLL_DIFFUSE = 7
VMEM_LIMIT = 56 * 1024 * 1024


def pack(
    partner_ref,
    count_ref,
    w_ref,
    value_ref,
    error_ref,
    cell_ref,
    bg_ref,
    out_ref,
    bgm_ref,
    info_ref,
    turn_ref,
    order_ref,
    counts_ref,
):
    levels, some, n = w_ref.shape
    owners = order_ref.shape[0]
    lane8 = lax.broadcasted_iota(jnp.int32, (8, n), 1)

    @pl.when(pl.program_id(0) == 0)
    def _():
        counts = jnp.transpose(jnp.broadcast_to(count_ref[...].astype(F32), (owners, n)))
        lane = lax.broadcasted_iota(jnp.int32, (owners, n), 1)
        cell = cell_ref[...]
        row = cell >> 7
        key = (((row >> 3) & 3) << 11) | ((row >> 5) << 10) | ((row & 7) << 7) | (cell & 127)
        counts_ref[...] = counts.astype(jnp.int32)
        filled = lane.astype(F32) < counts
        spread = (lane.astype(F32) - counts + 0.5) * (8192.0 / jnp.maximum(n - counts, 1.0))
        key = jnp.where(filled, key, jnp.clip(spread, 0.0, 8191.0).astype(jnp.int32))
        x = (key * n + lane).astype(F32)
        size = 2
        while size <= n:
            step = size // 2
            while step >= 1:
                first = (lane & step) == 0
                other = jnp.where(first, pltpu.roll(x, n - step, axis=1), pltpu.roll(x, step, axis=1))
                least = first == ((lane & size) == 0)
                x = jnp.where(least, jnp.minimum(x, other), jnp.maximum(x, other))
                step //= 2
            size *= 2
        order = x.astype(jnp.int32) & (n - 1)
        here = lax.axis_index("lat") * lax.axis_size("lon") + lax.axis_index("lon")
        order_ref[...] = jnp.take_along_axis(order, lane ^ (16 * (here % 8)), axis=1)

    span = n * lax.axis_size("lon")
    moved = (partner_ref[0] + (span - 3)) % span
    lat_at = lax.axis_index("lat")
    info_ref[0] = moved % n
    info_ref[1] = 1 - lat_at % 2
    info_ref[2] = (lat_at == lax.axis_size("lat") - 1).astype(jnp.int32)
    info_ref[3] = 0
    turn_ref[0] = moved // n

    for p in range(2):
        for k in range(0, levels, 2):
            x = jnp.concatenate([bg_ref[k, p, 0], bg_ref[k + 1, p, 0]], axis=0)
            hi = x.astype(BF16)
            at = p * 8 * levels + 8 * k
            bgm_ref[at : at + 16, 0:128] = hi
            bgm_ref[at : at + 16, 128:256] = (x - hi.astype(F32)).astype(BF16)

    for o in range(0, some, 8):
        at = pl.ds(pl.multiple_of(pl.program_id(0) * some + o, 8), 8)
        order = order_ref[at, :]
        valid = order < counts_ref[at, :]

        def put(k, v):
            out_ref[pl.ds(o * 56 + k, 8, stride=56), :] = v

        for k in range(levels):
            put(k, jnp.take_along_axis(w_ref[k, o : o + 8, :], order, axis=1))
        put(levels, jnp.take_along_axis(value_ref[at, :], order, axis=1))
        error = jnp.take_along_axis(error_ref[at, :], order, axis=1)
        put(levels + 1, jnp.where(valid, 1.0 / error, 0.0))
        put(levels + 2, jnp.take_along_axis(cell_ref[at, :], order, axis=1).astype(F32))
        for k in range(levels + 3, 56):
            put(k, jnp.zeros((8, n), F32))


def pack_call(partner, count, weight, value, error, column, bg):
    levels, owners, n = weight.shape
    ny, nx = bg.shape[1], bg.shape[2]
    steps = 4
    some = owners // steps
    whole = lambda i: (0, 0)
    return pl.pallas_call(
        pack,
        grid=(steps,),
        out_shape=(
            jax.ShapeDtypeStruct((owners * DEEP, n), F32),
            jax.ShapeDtypeStruct((levels * ny, 2 * nx), BF16),
            jax.ShapeDtypeStruct((4,), jnp.int32),
            jax.ShapeDtypeStruct((1,), jnp.int32),
        ),
        in_specs=[
            smem(),
            pl.BlockSpec((1, owners), whole),
            pl.BlockSpec((levels, some, n), lambda i: (0, i, 0)),
            pl.BlockSpec((owners, n), whole),
            pl.BlockSpec((owners, n), whole),
            pl.BlockSpec((owners, n), whole),
            pl.BlockSpec((levels, 2, 1, 8, nx), lambda i: (0, 0, i, 0, 0)),
        ],
        out_specs=(
            pl.BlockSpec((some * DEEP, n), lambda i: (i, 0)),
            pl.BlockSpec((levels * ny // steps, 2 * nx), lambda i: (i, 0)),
            smem(),
            smem(),
        ),
        scratch_shapes=[pltpu.VMEM((owners, n), jnp.int32), pltpu.VMEM((owners, n), jnp.int32)],
        compiler_params=params(),
        name="pack",
    )(partner, count, weight, value, error, column, bg.reshape(levels, 2, 4, 8, nx))


def observe(rec_ref, bgm_ref, east_ref, north_ref, sea_ref, es_ref, state_ref, to_east_ref, to_west_ref, total_ref, tiles, force, whi, wlo, amat, cost_ref):
    levels = es_ref.shape[0]
    sources = rec_ref.shape[0] // 56
    rows_in = 8 * levels
    wide = whi.shape[1]
    total = tiles.shape[2]

    force[...] = jnp.zeros_like(force)
    cost_ref[...] = jnp.zeros_like(cost_ref)

    def regroup(eight, _):
        lane = lax.broadcasted_iota(jnp.int32, (8, 128), 1)
        for r in range(0, 56, 8):
            xs = [rec_ref[pl.ds(pl.multiple_of((eight * 8 + i) * 56 + r, 8), 8), :] for i in range(8)]
            for d in (1, 2, 4):
                keep = (lane & (16 * d)) == 0
                xs = [jnp.where(keep, xs[i], xs[i ^ d]) for i in range(8)]
            for i in range(8):
                tiles[i, r : r + 8, pl.ds(pl.multiple_of(eight * 128, 128), 128)] = xs[i]
        return 0

    lax.fori_loop(0, sources // 8, regroup, 0)

    iota8 = lax.broadcasted_iota(jnp.int32, (8, wide), 0)

    def tile(t, _):
        q = t // (total // wide)
        at_r = pl.ds(pl.multiple_of((t % (total // wide)) * wide, wide), wide)
        value = tiles[q, levels : levels + 1, at_r]
        inverse = tiles[q, levels + 1 : levels + 2, at_r]
        cell = tiles[q, levels + 2 : levels + 3, at_r].astype(jnp.int32)
        row = cell >> 7
        col = cell & 127
        part = row >> 5
        block = (row >> 3) & 3
        group = 2 * block + part
        valid = inverse > 0.0
        gmin = jnp.min(jnp.where(valid, group, 8))
        gmax = jnp.max(jnp.where(valid, group, -1))
        rmask = iota8 == (row & 7)
        iota128 = lax.broadcasted_iota(jnp.int32, (128, wide), 0)
        pick = jnp.where(iota128 == col, 1.0, 0.0)
        partf = part.astype(F32)
        pickb = pick.astype(BF16)
        pick2 = jnp.concatenate([pickb, pickb], axis=0)

        def sample(g, acc):
            s = jnp.dot(
                bgm_ref[pl.ds(pl.multiple_of(g * rows_in, 16), rows_in), :],
                pick2,
                preferred_element_type=F32,
            )
            parts = [None] * 4
            for k in range(levels):
                x = tiles[q, k : k + 1, at_r] * s[8 * k : 8 * k + 8, :]
                parts[k % 4] = x if parts[k % 4] is None else parts[k % 4] + x
            total_g = (parts[0] + parts[1]) + (parts[2] + parts[3])
            return acc + jnp.where(group == g, total_g, 0.0)

        acc = lax.fori_loop(gmin, gmax + 1, sample, jnp.zeros((8, wide), F32))
        equiv = jnp.sum(jnp.where(rmask, acc, 0.0), axis=0, keepdims=True)
        scaled = (value - equiv) * inverse
        magnitude = jnp.abs(scaled)
        cost_ref[...] += jnp.where(
            magnitude <= HUBER_EDGE,
            0.5 * scaled * scaled,
            HUBER_EDGE * magnitude - 0.5 * HUBER_EDGE * HUBER_EDGE,
        )
        response = HUBER_EDGE / jnp.maximum(magnitude, HUBER_EDGE) * scaled * inverse
        wr = tiles[q, 0:levels, at_r] * response
        hi = wr.astype(BF16).astype(F32)
        whi[0:levels, :] = hi
        wlo[0:levels, :] = wr - hi
        low = pick * partf
        place = jnp.concatenate([(pick - low).astype(BF16), low.astype(BF16)], axis=0)
        place2 = jnp.concatenate([place, place], axis=1)

        def spread(b, _):
            m = jnp.where(rmask & (block == b), 1.0, 0.0)
            for k in range(0, levels, 2):
                for half, src in ((0, whi), (wide, wlo)):
                    x = jnp.concatenate([m * src[k : k + 1, :], m * src[k + 1 : k + 2, :]], axis=0)
                    amat[8 * k : 8 * k + 16, half : half + wide] = x.astype(BF16)
            at = pl.ds(pl.multiple_of(b * rows_in, 8), rows_in)
            force[at, :] += lax.dot_general(
                amat[...], place2, (((1,), (1,)), ((), ())), preferred_element_type=F32
            )
            return 0

        lax.fori_loop(gmin >> 1, (gmax >> 1) + 1, spread, 0)
        return 0

    lax.fori_loop(0, 8 * (total // wide), tile, 0)

    total_ref[...] = jnp.broadcast_to(jnp.sum(cost_ref[...], axis=1, keepdims=True)[None], total_ref.shape)

    for r0 in range(0, 64, 8):
        b, part = (r0 // 8) % 4, r0 // 32
        sea = sea_ref[r0 : r0 + 8, :].astype(F32)

        def level_rows(k):
            return pl.ds(r0 * DEEP + k, 8, stride=DEEP)

        state_ref[level_rows(levels), :] = east_ref[r0 : r0 + 8, :]
        state_ref[level_rows(levels + 1), :] = north_ref[r0 : r0 + 8, :]
        state_ref[level_rows(levels + 2), :] = sea
        for k in range(levels + 3, DEEP):
            state_ref[level_rows(k), :] = jnp.zeros((8, 128), F32)
        for k in range(levels):
            f = force[b * rows_in + 8 * k : b * rows_in + 8 * k + 8, 128 * part : 128 * part + 128]
            state_ref[level_rows(k), :] = sea * es_ref[k, r0 : r0 + 8, :] * f

    lane = lax.broadcasted_iota(jnp.int32, (8, 128), 1)

    def messages(g, _):
        def row(r):
            return state_ref[pl.ds(pl.multiple_of(r * DEEP + 8 * g, 8), 8), :]

        here = pl.ds(pl.multiple_of(8 * g, 8), 8)
        for half in range(2):
            last = jnp.zeros((8, 128), F32)
            first = jnp.zeros((8, 128), F32)
            for i in range(32):
                x = row(32 * half + i)
                mine = (lane >> 2) == i
                last = jnp.where(mine, pltpu.roll(x, (4 * i + 4) % 128, axis=1), last)
                first = jnp.where(mine, pltpu.roll(x, 4 * i, axis=1), first)
            to_east_ref[here, 128 * half : 128 * half + 128] = last
            to_west_ref[here, 128 * half : 128 * half + 128] = first
        more = jnp.zeros((8, 128), F32)
        for d in range(4):
            x = row(60 + d)
            to_east_ref[here, 256 + 128 * d : 384 + 128 * d] = x
            more = jnp.where((lane >> 2) == d, pltpu.roll(x, (4 * d - 4) % 128, axis=1), more)
        to_west_ref[here, 256:384] = more
        return 0

    lax.fori_loop(0, DEEP // 8, messages, 0)


def observe_call(received, bgm, east_rate, north_rate, sea_mask, es, wide=WIDE):
    levels, ny, nx = es.shape
    owners = received.shape[0] // 56
    return pl.pallas_call(
        observe,
        out_shape=(
            jax.ShapeDtypeStruct((ny * DEEP, nx), F32),
            jax.ShapeDtypeStruct((DEEP, 768), F32),
            jax.ShapeDtypeStruct((DEEP, 384), F32),
            jax.ShapeDtypeStruct((owners, 1, 128), F32),
        ),
        in_specs=[vmem()] * 6,
        out_specs=(vmem(),) * 4,
        scratch_shapes=[
            pltpu.VMEM((8, 56, 16 * owners), F32),
            pltpu.VMEM((32 * levels, 256), F32),
            pltpu.VMEM((56, wide), F32),
            pltpu.VMEM((56, wide), F32),
            pltpu.VMEM((8 * levels, 2 * wide), BF16),
            pltpu.VMEM((1, wide), F32),
        ],
        compiler_params=params(),
        name="observe",
    )(received, bgm, east_rate, north_rate, sea_mask, es)


def side_tile(fe, fw, r, lane):
    half, i = r // 32, r % 32
    e = pltpu.roll(fe[128 * half], (128 - 4 * i) % 128, axis=1)
    w = pltpu.roll(fw[128 * half], (124 - 4 * i) % 128, axis=1)
    return jnp.where(lane < 64, e, w)


def assemble(info_ref, bot_ref, top_ref, fw_ref, fe_ref, one_ref, two_ref):
    shift = info_ref[0]
    even = info_ref[1] == 1
    fold = info_ref[2] == 1
    lane = lax.broadcasted_iota(jnp.int32, (8, 128), 1)
    rel_a = shift + 3 - lane
    rel_b = jnp.where(lane < 64, shift + 3 - 128 - lane, shift + 3 + 128 - lane)

    def mirror(west, own, east, rel):
        idx = rel & 127
        w = jnp.take_along_axis(west, idx, axis=1)
        o = jnp.take_along_axis(own, idx, axis=1)
        e = jnp.take_along_axis(east, idx, axis=1)
        return jnp.where(rel < 0, w, jnp.where(rel < 128, o, e))

    def body(g, _):
        here = pl.ds(pl.multiple_of(8 * g, 8), 8)
        fe = {c: fe_ref[here, c : c + 128] for c in (0, 128, 256)}
        fw = {c: fw_ref[here, c : c + 128] for c in range(0, 768, 128)}
        top = [top_ref[d, here, :] for d in range(4)]
        top_side = [side_tile(fe, fw, 60 + d, lane) for d in range(4)]
        sides = [jnp.zeros((8, 128), F32) for _ in range(3)]
        for d in range(4):
            u = 3 - d
            east = jnp.where(lane < 4, top_side[u], pltpu.roll(fe[256], (4 - 4 * u) % 128, axis=1))
            fold_a = mirror(fw[256 + 128 * u], top[u], east, rel_a)
            fold_b = mirror(fw[256 + 128 * u], top[u], east, rel_b)
            bot = bot_ref[d, here, :]
            one_ref[d, here, :] = jnp.where(even, top[d], bot)
            two_ref[d, here, :] = jnp.where(even, bot, jnp.where(fold, fold_a, top[d]))
            for n, x in enumerate((top_side[d], side_tile(fe, fw, d, lane), fold_b)):
                sides[n] = jnp.where((lane >> 3) == d, pltpu.roll(x, 8 * d + 4, axis=1), sides[n])
        one_ref[4, here, :] = jnp.where(even, sides[0], sides[1])
        two_ref[4, here, :] = jnp.where(even, sides[1], jnp.where(fold, sides[2], sides[0]))
        return 0

    lax.fori_loop(0, DEEP // 8, body, 0)


def diffuse(info_ref, x_ref, fw_ref, fe_ref, one_ref, two_ref, es_ref, out_ref, sa, sb, coef):
    levels = es_ref.shape[0] // 64
    even = info_ref[1] == 1
    lane = lax.broadcasted_iota(jnp.int32, (8, 128), 1)

    def fill(g, _):
        here = pl.ds(pl.multiple_of(8 * g, 8), 8)
        fe = {c: fe_ref[here, c : c + 128] for c in (0, 128)}
        fw = {c: fw_ref[here, c : c + 128] for c in (0, 128)}
        for r in range(64):
            sa[r + 4, here, 0:128] = x_ref[r, here, :]
            sa[r + 4, here, 128:256] = side_tile(fe, fw, r, lane)
        for d in range(4):
            one = one_ref[d, here, :]
            two = two_ref[d, here, :]
            sa[d, here, 0:128] = jnp.where(even, two, one)
            sa[68 + d, here, 0:128] = jnp.where(even, one, two)
            one = pltpu.roll(one_ref[4, here, :], 124 - 8 * d, axis=1)
            two = pltpu.roll(two_ref[4, here, :], 124 - 8 * d, axis=1)
            sa[d, here, 128:256] = jnp.where(even, two, one)
            sa[68 + d, here, 128:256] = jnp.where(even, one, two)
        return 0

    lax.fori_loop(0, DEEP // 8, fill, 0)

    rows, cols = sa.shape[0], sa.shape[2]
    col = lax.broadcasted_iota(jnp.int32, (rows, cols), 1)
    live = (col < 132) | (col >= 252)
    sea = jnp.where(live, sa[:, levels + 2, :], 0.0)
    east = jnp.where(live, sa[:, levels, :], 0.0) * sea
    north = jnp.where(live, sa[:, levels + 1, :], 0.0) * sea
    a_e = east * pltpu.roll(sea, cols - 1, axis=1)
    a_w = east * pltpu.roll(sea, 1, axis=1)
    a_n = north * pltpu.roll(sea, rows - 1, axis=0)
    a_s = north * pltpu.roll(sea, 1, axis=0)
    coef[0] = 1.0 - ((a_e + a_w) + (a_n + a_s))
    coef[1] = a_e
    coef[2] = a_w
    coef[3] = a_n
    coef[4] = a_s

    def step(src, lo, hi, put):
        def body(r, _):
            c = [coef[i, pl.ds(r, 1), :] for i in range(5)]
            for g in range(DEEP // 8):
                here = slice(8 * g, 8 * g + 8)
                s = src[r, here, :]
                put(
                    r,
                    g,
                    c[0] * s
                    + (c[1] * pltpu.roll(s, cols - 1, axis=1) + c[2] * pltpu.roll(s, 1, axis=1))
                    + (c[3] * src[r + 1, here, :] + c[4] * src[r - 1, here, :]),
                )
            return 0

        lax.fori_loop(lo, hi, body, 0, unroll=UNROLL_DIFFUSE)

    def keep(dst):
        def put(r, g, v):
            dst[r, 8 * g : 8 * g + 8, :] = v

        return put

    def finish(r, g, v):
        n = min(8, levels - 8 * g)
        at = pl.ds(8 * g * 64 + r - 4, n, stride=64)
        out_ref[at, :] = es_ref[at, :] * v[0:n, 0:128]

    step(sa, 1, 71, keep(sb))
    step(sb, 2, 70, keep(sa))
    step(sa, 3, 69, keep(sb))
    step(sb, 4, 68, finish)


def vmem():
    return pl.BlockSpec(memory_space=pltpu.VMEM)


def smem():
    return pl.BlockSpec(memory_space=pltpu.SMEM)


def params():
    return pltpu.CompilerParams(vmem_limit_bytes=VMEM_LIMIT)


def perm_of(n_lat, n_lon, rule):
    pairs = []
    for a in range(n_lat):
        for b in range(n_lon):
            to = rule(a, b)
            if to is not None:
                pairs.append((a * n_lon + b, to[0] * n_lon + to[1] % n_lon))
    return pairs


def assemble_call(info, state, from_west, from_east):
    rows = jax.ShapeDtypeStruct((5, DEEP, 128), F32)
    return pl.pallas_call(
        assemble,
        grid=(1,),
        out_shape=(rows, rows),
        in_specs=[
            smem(),
            pl.BlockSpec((4, DEEP, 128), lambda i: (0, 0, 0)),
            pl.BlockSpec((4, DEEP, 128), lambda i: (15, 0, 0)),
            vmem(),
            vmem(),
        ],
        out_specs=(vmem(), vmem()),
        compiler_params=params(),
        name="assemble",
    )(info, state, state, from_west, from_east)


def diffuse_call(info, state, from_west, from_east, one, two, es):
    levels, ny, nx = es.shape
    out = pl.pallas_call(
        diffuse,
        out_shape=jax.ShapeDtypeStruct((levels * ny, nx), F32),
        in_specs=[smem()] + [vmem()] * 6,
        out_specs=vmem(),
        scratch_shapes=[
            pltpu.VMEM((ny + 8, DEEP, 2 * nx), F32),
            pltpu.VMEM((ny + 8, DEEP, 2 * nx), F32),
            pltpu.VMEM((5, ny + 8, 2 * nx), F32),
        ],
        compiler_params=params(),
        cost_estimate=pl.CostEstimate(flops=20 * STEPS * levels * ny * nx, bytes_accessed=60000000, transcendentals=0),
        name="diffuse",
    )(info, state, from_west, from_east, one, two, es.reshape(levels * ny, nx))
    return out.reshape(levels, ny, nx)


def shards(
    background,
    error_scale,
    east_rate,
    north_rate,
    sea_mask,
    partner,
    obs_weight,
    obs_value,
    obs_error,
    obs_column,
    obs_count,
):
    levels = background.shape[0] * background.shape[1]
    ny = background.shape[2]
    nx = background.shape[3]
    capacity = obs_weight.shape[3]
    owners = obs_weight.shape[1]
    bg = background.reshape(levels, ny, nx)
    es = error_scale.reshape(levels, ny, nx)
    packed, bgm, info, turn = pack_call(
        partner, obs_count, jnp.swapaxes(obs_weight[0], 0, 1), obs_value[0], obs_error[0], obs_column[0], bg
    )
    turn = turn.reshape(())
    packed, bgm, info, turn = lax.optimization_barrier((packed, bgm, info, turn))
    received = lax.all_to_all(packed, ("lat", "lon"), split_axis=0, concat_axis=0, tiled=True)
    state, to_east, to_west, cost = observe_call(received, bgm, east_rate, north_rate, sea_mask, es)
    state = state.reshape(ny, DEEP, nx)

    n_lat = lax.axis_size("lat")
    n_lon = lax.axis_size("lon")
    from_west = lax.ppermute(to_east, "lon", [(i, (i + 1) % n_lon) for i in range(n_lon)])
    from_east = lax.ppermute(to_west, "lon", [((i + 1) % n_lon, i) for i in range(n_lon)])
    one, two = assemble_call(info, state, from_west, from_east)

    def branch(q):
        def rule(a, b):
            if a == n_lat - 1:
                return (a, q - b)
            if a == 0:
                return None
            return (((a + 1) ^ 1) - 1, b)

        def run(one, two, cost):
            got_one = lax.ppermute(one, ("lat", "lon"), perm_of(n_lat, n_lon, lambda a, b: (a ^ 1, b)))
            got_two = lax.ppermute(two, ("lat", "lon"), perm_of(n_lat, n_lon, rule))
            shares = lax.all_to_all(cost, ("lat", "lon"), split_axis=0, concat_axis=0, tiled=True)
            return got_one, got_two, shares

        return run

    got_one, got_two, shares = lax.switch(turn, [branch(q) for q in range(n_lon)], one, two, cost)
    cost_share = jnp.sum(shares[:, 0, 0]) / (owners * owners * capacity)
    increment = diffuse_call(info, state, from_west, from_east, got_one, got_two, es)
    return (increment.reshape(background.shape), cost_share)


def solution(mesh):
    in_specs = (
        P(None, None, "lat", "lon"),
        P(None, None, "lat", "lon"),
        P("lat", "lon"),
        P("lat", "lon"),
        P("lat", "lon"),
        P(),
        P(("lat", "lon"), None, None, None),
        P(("lat", "lon"), None, None),
        P(("lat", "lon"), None, None),
        P(("lat", "lon"), None, None),
        P(("lat", "lon"), None),
    )
    out_specs = (P(None, None, "lat", "lon"), P())
    return jax.shard_map(shards, mesh=mesh, in_specs=in_specs, out_specs=out_specs, check_vma=False)
```

```python
import jax
import jax.numpy as jnp
from jax import lax
from jax.experimental import pallas as pl
from jax.experimental.pallas import tpu as pltpu
from jax.sharding import PartitionSpec as P

STEPS = 4
HALO = 4
HUBER_EDGE = 1.5
F32 = jnp.float32
BF16 = jnp.bfloat16
WIDE = 2048
DEEP = 56
UNROLL_DIFFUSE = 7
VMEM_LIMIT = 56 * 1024 * 1024


def pack(
    partner_ref,
    count_ref,
    w_ref,
    value_ref,
    error_ref,
    cell_ref,
    bg_ref,
    out_ref,
    bgm_ref,
    info_ref,
    turn_ref,
    order_ref,
    counts_ref,
):
    levels, some, n = w_ref.shape
    owners = order_ref.shape[0]
    lane8 = lax.broadcasted_iota(jnp.int32, (8, n), 1)

    @pl.when(pl.program_id(0) == 0)
    def _():
        counts = jnp.transpose(jnp.broadcast_to(count_ref[...].astype(F32), (owners, n)))
        lane = lax.broadcasted_iota(jnp.int32, (owners, n), 1)
        cell = cell_ref[...]
        row = cell >> 7
        key = (((row >> 3) & 3) << 11) | ((row >> 5) << 10) | ((row & 7) << 7) | (cell & 127)
        counts_ref[...] = counts.astype(jnp.int32)
        filled = lane.astype(F32) < counts
        spread = (lane.astype(F32) - counts + 0.5) * (8192.0 / jnp.maximum(n - counts, 1.0))
        key = jnp.where(filled, key, jnp.clip(spread, 0.0, 8191.0).astype(jnp.int32))
        x = (key * n + lane).astype(F32)
        size = 2
        while size <= n:
            step = size // 2
            while step >= 1:
                first = (lane & step) == 0
                other = jnp.where(first, pltpu.roll(x, n - step, axis=1), pltpu.roll(x, step, axis=1))
                least = first == ((lane & size) == 0)
                x = jnp.where(least, jnp.minimum(x, other), jnp.maximum(x, other))
                step //= 2
            size *= 2
        order = x.astype(jnp.int32) & (n - 1)
        here = lax.axis_index("lat") * lax.axis_size("lon") + lax.axis_index("lon")
        order_ref[...] = jnp.take_along_axis(order, lane ^ (16 * (here % 8)), axis=1)

    span = n * lax.axis_size("lon")
    moved = (partner_ref[0] + (span - 3)) % span
    lat_at = lax.axis_index("lat")
    info_ref[0] = moved % n
    info_ref[1] = 1 - lat_at % 2
    info_ref[2] = (lat_at == lax.axis_size("lat") - 1).astype(jnp.int32)
    info_ref[3] = 0
    turn_ref[0] = moved // n

    for p in range(2):
        for k in range(0, levels, 2):
            x = jnp.concatenate([bg_ref[k, p, 0], bg_ref[k + 1, p, 0]], axis=0)
            hi = x.astype(BF16)
            at = p * 8 * levels + 8 * k
            bgm_ref[at : at + 16, 0:128] = hi
            bgm_ref[at : at + 16, 128:256] = (x - hi.astype(F32)).astype(BF16)

    for o in range(0, some, 8):
        at = pl.ds(pl.multiple_of(pl.program_id(0) * some + o, 8), 8)
        order = order_ref[at, :]
        valid = order < counts_ref[at, :]

        def put(k, v):
            out_ref[pl.ds(o * 56 + k, 8, stride=56), :] = v

        for k in range(levels):
            put(k, jnp.take_along_axis(w_ref[k, o : o + 8, :], order, axis=1))
        put(levels, jnp.take_along_axis(value_ref[at, :], order, axis=1))
        error = jnp.take_along_axis(error_ref[at, :], order, axis=1)
        put(levels + 1, jnp.where(valid, 1.0 / error, 0.0))
        put(levels + 2, jnp.take_along_axis(cell_ref[at, :], order, axis=1).astype(F32))
        for k in range(levels + 3, 56):
            put(k, jnp.zeros((8, n), F32))


def pack_call(partner, count, weight, value, error, column, bg):
    levels, owners, n = weight.shape
    ny, nx = bg.shape[1], bg.shape[2]
    steps = 4
    some = owners // steps
    whole = lambda i: (0, 0)
    return pl.pallas_call(
        pack,
        grid=(steps,),
        out_shape=(
            jax.ShapeDtypeStruct((owners * DEEP, n), F32),
            jax.ShapeDtypeStruct((levels * ny, 2 * nx), BF16),
            jax.ShapeDtypeStruct((4,), jnp.int32),
            jax.ShapeDtypeStruct((1,), jnp.int32),
        ),
        in_specs=[
            smem(),
            pl.BlockSpec((1, owners), whole),
            pl.BlockSpec((levels, some, n), lambda i: (0, i, 0)),
            pl.BlockSpec((owners, n), whole),
            pl.BlockSpec((owners, n), whole),
            pl.BlockSpec((owners, n), whole),
            pl.BlockSpec((levels, 2, 1, 8, nx), lambda i: (0, 0, i, 0, 0)),
        ],
        out_specs=(
            pl.BlockSpec((some * DEEP, n), lambda i: (i, 0)),
            pl.BlockSpec((levels * ny // steps, 2 * nx), lambda i: (i, 0)),
            smem(),
            smem(),
        ),
        scratch_shapes=[pltpu.VMEM((owners, n), jnp.int32), pltpu.VMEM((owners, n), jnp.int32)],
        compiler_params=params(),
        name="pack",
    )(partner, count, weight, value, error, column, bg.reshape(levels, 2, 4, 8, nx))


def observe(rec_ref, bgm_ref, east_ref, north_ref, sea_ref, es_ref, state_ref, to_east_ref, to_west_ref, total_ref, tiles, force, whi, wlo, amat, cost_ref):
    levels = es_ref.shape[0]
    sources = rec_ref.shape[0] // 56
    rows_in = 8 * levels
    wide = whi.shape[1]
    total = tiles.shape[2]

    force[...] = jnp.zeros_like(force)
    cost_ref[...] = jnp.zeros_like(cost_ref)

    def regroup(eight, _):
        lane = lax.broadcasted_iota(jnp.int32, (8, 128), 1)
        for r in range(0, 56, 8):
            xs = [rec_ref[pl.ds(pl.multiple_of((eight * 8 + i) * 56 + r, 8), 8), :] for i in range(8)]
            for d in (1, 2, 4):
                keep = (lane & (16 * d)) == 0
                xs = [jnp.where(keep, xs[i], xs[i ^ d]) for i in range(8)]
            for i in range(8):
                tiles[i, r : r + 8, pl.ds(pl.multiple_of(eight * 128, 128), 128)] = xs[i]
        return 0

    lax.fori_loop(0, sources // 8, regroup, 0)

    iota8 = lax.broadcasted_iota(jnp.int32, (8, wide), 0)

    def tile(t, _):
        q = t // (total // wide)
        at_r = pl.ds(pl.multiple_of((t % (total // wide)) * wide, wide), wide)
        value = tiles[q, levels : levels + 1, at_r]
        inverse = tiles[q, levels + 1 : levels + 2, at_r]
        cell = tiles[q, levels + 2 : levels + 3, at_r].astype(jnp.int32)
        row = cell >> 7
        col = cell & 127
        part = row >> 5
        block = (row >> 3) & 3
        group = 2 * block + part
        valid = inverse > 0.0
        gmin = jnp.min(jnp.where(valid, group, 8))
        gmax = jnp.max(jnp.where(valid, group, -1))
        rmask = iota8 == (row & 7)
        iota128 = lax.broadcasted_iota(jnp.int32, (128, wide), 0)
        pick = jnp.where(iota128 == col, 1.0, 0.0)
        partf = part.astype(F32)
        pickb = pick.astype(BF16)
        pick2 = jnp.concatenate([pickb, pickb], axis=0)

        def sample(g, acc):
            s = jnp.dot(
                bgm_ref[pl.ds(pl.multiple_of(g * rows_in, 16), rows_in), :],
                pick2,
                preferred_element_type=F32,
            )
            parts = [None] * 4
            for k in range(levels):
                x = tiles[q, k : k + 1, at_r] * s[8 * k : 8 * k + 8, :]
                parts[k % 4] = x if parts[k % 4] is None else parts[k % 4] + x
            total_g = (parts[0] + parts[1]) + (parts[2] + parts[3])
            return acc + jnp.where(group == g, total_g, 0.0)

        acc = lax.fori_loop(gmin, gmax + 1, sample, jnp.zeros((8, wide), F32))
        equiv = jnp.sum(jnp.where(rmask, acc, 0.0), axis=0, keepdims=True)
        scaled = (value - equiv) * inverse
        magnitude = jnp.abs(scaled)
        cost_ref[...] += jnp.where(
            magnitude <= HUBER_EDGE,
            0.5 * scaled * scaled,
            HUBER_EDGE * magnitude - 0.5 * HUBER_EDGE * HUBER_EDGE,
        )
        response = HUBER_EDGE / jnp.maximum(magnitude, HUBER_EDGE) * scaled * inverse
        wr = tiles[q, 0:levels, at_r] * response
        hi = wr.astype(BF16).astype(F32)
        whi[0:levels, :] = hi
        wlo[0:levels, :] = wr - hi
        low = pick * partf
        place = jnp.concatenate([(pick - low).astype(BF16), low.astype(BF16)], axis=0)
        place2 = jnp.concatenate([place, place], axis=1)

        def spread(b, _):
            m = jnp.where(rmask & (block == b), 1.0, 0.0)
            for k in range(0, levels, 2):
                for half, src in ((0, whi), (wide, wlo)):
                    x = jnp.concatenate([m * src[k : k + 1, :], m * src[k + 1 : k + 2, :]], axis=0)
                    amat[8 * k : 8 * k + 16, half : half + wide] = x.astype(BF16)
            at = pl.ds(pl.multiple_of(b * rows_in, 8), rows_in)
            force[at, :] += lax.dot_general(
                amat[...], place2, (((1,), (1,)), ((), ())), preferred_element_type=F32
            )
            return 0

        lax.fori_loop(gmin >> 1, (gmax >> 1) + 1, spread, 0)
        return 0

    lax.fori_loop(0, 8 * (total // wide), tile, 0)

    total_ref[...] = jnp.broadcast_to(jnp.sum(cost_ref[...], axis=1, keepdims=True)[None], total_ref.shape)

    for r0 in range(0, 64, 8):
        b, part = (r0 // 8) % 4, r0 // 32
        sea = sea_ref[r0 : r0 + 8, :].astype(F32)

        def level_rows(k):
            return pl.ds(r0 * DEEP + k, 8, stride=DEEP)

        state_ref[level_rows(levels), :] = east_ref[r0 : r0 + 8, :]
        state_ref[level_rows(levels + 1), :] = north_ref[r0 : r0 + 8, :]
        state_ref[level_rows(levels + 2), :] = sea
        for k in range(levels + 3, DEEP):
            state_ref[level_rows(k), :] = jnp.zeros((8, 128), F32)
        for k in range(levels):
            f = force[b * rows_in + 8 * k : b * rows_in + 8 * k + 8, 128 * part : 128 * part + 128]
            state_ref[level_rows(k), :] = sea * es_ref[k, r0 : r0 + 8, :] * f

    lane = lax.broadcasted_iota(jnp.int32, (8, 128), 1)

    def messages(g, _):
        def row(r):
            return state_ref[pl.ds(pl.multiple_of(r * DEEP + 8 * g, 8), 8), :]

        here = pl.ds(pl.multiple_of(8 * g, 8), 8)
        for half in range(2):
            last = jnp.zeros((8, 128), F32)
            first = jnp.zeros((8, 128), F32)
            for i in range(32):
                x = row(32 * half + i)
                mine = (lane >> 2) == i
                last = jnp.where(mine, pltpu.roll(x, (4 * i + 4) % 128, axis=1), last)
                first = jnp.where(mine, pltpu.roll(x, 4 * i, axis=1), first)
            to_east_ref[here, 128 * half : 128 * half + 128] = last
            to_west_ref[here, 128 * half : 128 * half + 128] = first
        more = jnp.zeros((8, 128), F32)
        for d in range(4):
            x = row(60 + d)
            to_east_ref[here, 256 + 128 * d : 384 + 128 * d] = x
            more = jnp.where((lane >> 2) == d, pltpu.roll(x, (4 * d - 4) % 128, axis=1), more)
        to_west_ref[here, 256:384] = more
        return 0

    lax.fori_loop(0, DEEP // 8, messages, 0)


def observe_call(received, bgm, east_rate, north_rate, sea_mask, es, wide=WIDE):
    levels, ny, nx = es.shape
    owners = received.shape[0] // 56
    return pl.pallas_call(
        observe,
        out_shape=(
            jax.ShapeDtypeStruct((ny * DEEP, nx), F32),
            jax.ShapeDtypeStruct((DEEP, 768), F32),
            jax.ShapeDtypeStruct((DEEP, 384), F32),
            jax.ShapeDtypeStruct((owners, 1, 128), F32),
        ),
        in_specs=[vmem()] * 6,
        out_specs=(vmem(),) * 4,
        scratch_shapes=[
            pltpu.VMEM((8, 56, 16 * owners), F32),
            pltpu.VMEM((32 * levels, 256), F32),
            pltpu.VMEM((56, wide), F32),
            pltpu.VMEM((56, wide), F32),
            pltpu.VMEM((8 * levels, 2 * wide), BF16),
            pltpu.VMEM((1, wide), F32),
        ],
        compiler_params=params(),
        name="observe",
    )(received, bgm, east_rate, north_rate, sea_mask, es)


def side_tile(fe, fw, r, lane):
    half, i = r // 32, r % 32
    e = pltpu.roll(fe[128 * half], (128 - 4 * i) % 128, axis=1)
    w = pltpu.roll(fw[128 * half], (124 - 4 * i) % 128, axis=1)
    return jnp.where(lane < 64, e, w)


def assemble(info_ref, bot_ref, top_ref, fw_ref, fe_ref, one_ref, two_ref):
    shift = info_ref[0]
    even = info_ref[1] == 1
    fold = info_ref[2] == 1
    lane = lax.broadcasted_iota(jnp.int32, (8, 128), 1)
    rel_a = shift + 3 - lane
    rel_b = jnp.where(lane < 64, shift + 3 - 128 - lane, shift + 3 + 128 - lane)

    def mirror(west, own, east, rel):
        idx = rel & 127
        w = jnp.take_along_axis(west, idx, axis=1)
        o = jnp.take_along_axis(own, idx, axis=1)
        e = jnp.take_along_axis(east, idx, axis=1)
        return jnp.where(rel < 0, w, jnp.where(rel < 128, o, e))

    def body(g, _):
        here = pl.ds(pl.multiple_of(8 * g, 8), 8)
        fe = {c: fe_ref[here, c : c + 128] for c in (0, 128, 256)}
        fw = {c: fw_ref[here, c : c + 128] for c in range(0, 768, 128)}
        top = [top_ref[d, here, :] for d in range(4)]
        top_side = [side_tile(fe, fw, 60 + d, lane) for d in range(4)]
        sides = [jnp.zeros((8, 128), F32) for _ in range(3)]
        for d in range(4):
            u = 3 - d
            east = jnp.where(lane < 4, top_side[u], pltpu.roll(fe[256], (4 - 4 * u) % 128, axis=1))
            fold_a = mirror(fw[256 + 128 * u], top[u], east, rel_a)
            fold_b = mirror(fw[256 + 128 * u], top[u], east, rel_b)
            bot = bot_ref[d, here, :]
            one_ref[d, here, :] = jnp.where(even, top[d], bot)
            two_ref[d, here, :] = jnp.where(even, bot, jnp.where(fold, fold_a, top[d]))
            for n, x in enumerate((top_side[d], side_tile(fe, fw, d, lane), fold_b)):
                sides[n] = jnp.where((lane >> 3) == d, pltpu.roll(x, 8 * d + 4, axis=1), sides[n])
        one_ref[4, here, :] = jnp.where(even, sides[0], sides[1])
        two_ref[4, here, :] = jnp.where(even, sides[1], jnp.where(fold, sides[2], sides[0]))
        return 0

    lax.fori_loop(0, DEEP // 8, body, 0)


def diffuse(info_ref, x_ref, fw_ref, fe_ref, one_ref, two_ref, es_ref, out_ref, sa, sb, coef):
    levels = es_ref.shape[0] // 64
    even = info_ref[1] == 1
    lane = lax.broadcasted_iota(jnp.int32, (8, 128), 1)

    def fill(g, _):
        here = pl.ds(pl.multiple_of(8 * g, 8), 8)
        fe = {c: fe_ref[here, c : c + 128] for c in (0, 128)}
        fw = {c: fw_ref[here, c : c + 128] for c in (0, 128)}
        for r in range(64):
            sa[r + 4, here, 0:128] = x_ref[r, here, :]
            sa[r + 4, here, 128:256] = side_tile(fe, fw, r, lane)
        for d in range(4):
            one = one_ref[d, here, :]
            two = two_ref[d, here, :]
            sa[d, here, 0:128] = jnp.where(even, two, one)
            sa[68 + d, here, 0:128] = jnp.where(even, one, two)
            one = pltpu.roll(one_ref[4, here, :], 124 - 8 * d, axis=1)
            two = pltpu.roll(two_ref[4, here, :], 124 - 8 * d, axis=1)
            sa[d, here, 128:256] = jnp.where(even, two, one)
            sa[68 + d, here, 128:256] = jnp.where(even, one, two)
        return 0

    lax.fori_loop(0, DEEP // 8, fill, 0)

    rows, cols = sa.shape[0], sa.shape[2]
    col = lax.broadcasted_iota(jnp.int32, (rows, cols), 1)
    live = (col < 132) | (col >= 252)
    sea = jnp.where(live, sa[:, levels + 2, :], 0.0)
    east = jnp.where(live, sa[:, levels, :], 0.0) * sea
    north = jnp.where(live, sa[:, levels + 1, :], 0.0) * sea
    a_e = east * pltpu.roll(sea, cols - 1, axis=1)
    a_w = east * pltpu.roll(sea, 1, axis=1)
    a_n = north * pltpu.roll(sea, rows - 1, axis=0)
    a_s = north * pltpu.roll(sea, 1, axis=0)
    coef[0] = 1.0 - ((a_e + a_w) + (a_n + a_s))
    coef[1] = a_e
    coef[2] = a_w
    coef[3] = a_n
    coef[4] = a_s

    def step(src, lo, hi, put):
        def body(r, _):
            c = [coef[i, pl.ds(r, 1), :] for i in range(5)]
            for g in range(DEEP // 8):
                here = slice(8 * g, 8 * g + 8)
                s = src[r, here, :]
                put(
                    r,
                    g,
                    c[0] * s
                    + (c[1] * pltpu.roll(s, cols - 1, axis=1) + c[2] * pltpu.roll(s, 1, axis=1))
                    + (c[3] * src[r + 1, here, :] + c[4] * src[r - 1, here, :]),
                )
            return 0

        lax.fori_loop(lo, hi, body, 0, unroll=UNROLL_DIFFUSE)

    def keep(dst):
        def put(r, g, v):
            dst[r, 8 * g : 8 * g + 8, :] = v

        return put

    def finish(r, g, v):
        n = min(8, levels - 8 * g)
        at = pl.ds(8 * g * 64 + r - 4, n, stride=64)
        out_ref[at, :] = es_ref[at, :] * v[0:n, 0:128]

    step(sa, 1, 71, keep(sb))
    step(sb, 2, 70, keep(sa))
    step(sa, 3, 69, keep(sb))
    step(sb, 4, 68, finish)


def vmem():
    return pl.BlockSpec(memory_space=pltpu.VMEM)


def smem():
    return pl.BlockSpec(memory_space=pltpu.SMEM)


def params():
    return pltpu.CompilerParams(vmem_limit_bytes=VMEM_LIMIT)


def perm_of(n_lat, n_lon, rule):
    pairs = []
    for a in range(n_lat):
        for b in range(n_lon):
            to = rule(a, b)
            if to is not None:
                pairs.append((a * n_lon + b, to[0] * n_lon + to[1] % n_lon))
    return pairs


def assemble_call(info, state, from_west, from_east):
    rows = jax.ShapeDtypeStruct((5, DEEP, 128), F32)
    return pl.pallas_call(
        assemble,
        grid=(1,),
        out_shape=(rows, rows),
        in_specs=[
            smem(),
            pl.BlockSpec((4, DEEP, 128), lambda i: (0, 0, 0)),
            pl.BlockSpec((4, DEEP, 128), lambda i: (15, 0, 0)),
            vmem(),
            vmem(),
        ],
        out_specs=(vmem(), vmem()),
        compiler_params=params(),
        name="assemble",
    )(info, state, state, from_west, from_east)


def diffuse_call(info, state, from_west, from_east, one, two, es):
    levels, ny, nx = es.shape
    out = pl.pallas_call(
        diffuse,
        out_shape=jax.ShapeDtypeStruct((levels * ny, nx), F32),
        in_specs=[smem()] + [vmem()] * 6,
        out_specs=vmem(),
        scratch_shapes=[
            pltpu.VMEM((ny + 8, DEEP, 2 * nx), F32),
            pltpu.VMEM((ny + 8, DEEP, 2 * nx), F32),
            pltpu.VMEM((5, ny + 8, 2 * nx), F32),
        ],
        compiler_params=params(),
        cost_estimate=pl.CostEstimate(flops=20 * STEPS * levels * ny * nx, bytes_accessed=60000000, transcendentals=0),
        name="diffuse",
    )(info, state, from_west, from_east, one, two, es.reshape(levels * ny, nx))
    return out.reshape(levels, ny, nx)


def shards(
    background,
    error_scale,
    east_rate,
    north_rate,
    sea_mask,
    partner,
    obs_weight,
    obs_value,
    obs_error,
    obs_column,
    obs_count,
):
    levels = background.shape[0] * background.shape[1]
    ny = background.shape[2]
    nx = background.shape[3]
    capacity = obs_weight.shape[3]
    owners = obs_weight.shape[1]
    bg = background.reshape(levels, ny, nx)
    es = error_scale.reshape(levels, ny, nx)
    packed, bgm, info, turn = pack_call(
        partner, obs_count, jnp.swapaxes(obs_weight[0], 0, 1), obs_value[0], obs_error[0], obs_column[0], bg
    )
    turn = turn.reshape(())
    packed, bgm, info, turn = lax.optimization_barrier((packed, bgm, info, turn))
    received = lax.all_to_all(packed, ("lat", "lon"), split_axis=0, concat_axis=0, tiled=True)
    state, to_east, to_west, cost = observe_call(received, bgm, east_rate, north_rate, sea_mask, es)
    state = state.reshape(ny, DEEP, nx)

    n_lat = lax.axis_size("lat")
    n_lon = lax.axis_size("lon")
    from_west = lax.ppermute(to_east, "lon", [(i, (i + 1) % n_lon) for i in range(n_lon)])
    from_east = lax.ppermute(to_west, "lon", [((i + 1) % n_lon, i) for i in range(n_lon)])
    one, two = assemble_call(info, state, from_west, from_east)

    shares = lax.all_to_all(cost, ("lat", "lon"), split_axis=0, concat_axis=0, tiled=True)

    def branch(q):
        def rule(a, b):
            if a == n_lat - 1:
                return (a, q - b)
            if a == 0:
                return None
            return (((a + 1) ^ 1) - 1, b)

        def run(one, two):
            got_one = lax.ppermute(one, ("lat", "lon"), perm_of(n_lat, n_lon, lambda a, b: (a ^ 1, b)))
            got_two = lax.ppermute(two, ("lat", "lon"), perm_of(n_lat, n_lon, rule))
            return got_one, got_two

        return run

    one, two, shares = lax.optimization_barrier((one, two, shares))
    got_one, got_two = lax.switch(turn, [branch(q) for q in range(n_lon)], one, two)
    increment = diffuse_call(info, state, from_west, from_east, got_one, got_two, es)
    increment, shares = lax.optimization_barrier((increment, shares))
    cost_share = jnp.sum(shares[:, 0, 0]) / (owners * owners * capacity)
    return (increment.reshape(background.shape), cost_share)


def solution(mesh):
    in_specs = (
        P(None, None, "lat", "lon"),
        P(None, None, "lat", "lon"),
        P("lat", "lon"),
        P("lat", "lon"),
        P("lat", "lon"),
        P(),
        P(("lat", "lon"), None, None, None),
        P(("lat", "lon"), None, None),
        P(("lat", "lon"), None, None),
        P(("lat", "lon"), None, None),
        P(("lat", "lon"), None),
    )
    out_specs = (P(None, None, "lat", "lon"), P())
    return jax.shard_map(shards, mesh=mesh, in_specs=in_specs, out_specs=out_specs, check_vma=False)
```
